32 devices in a mesh: groups: 2 (over y), row: 4 (over z), col: 4 (over x, core).
Axes of the slice: x: 2, y: 2, z: 4, core: 2. Of those that a mesh axis runs over, the one named last changes fastest.
Arguments:
- tokens: bfloat16 [1280, 8192], P(('groups', 'col'), 'row'), parts along dimension 0, may hold values from -6 to 6
- lengths: int32 [8], P('groups'), parts along dimension 0, may hold values from 1 to 160, 320 in all
- gate_weight: bfloat16 [8192, 14336], P('col', 'row'), may hold values from -0.0625 to 0.0625
- up_weight: bfloat16 [8192, 14336], P('col', 'row'), may hold values from -0.0625 to 0.0625
- down_weight: bfloat16 [14336, 8192], P('col', 'row'), may hold values from -0.046875 to 0.046875
Outputs:
- mixed: bfloat16 [1280, 8192], P(('groups', 'col'), 'row'), parts along dimension 0
The draws below stay inside these ranges and needn't reach their ends.
There are 2 independent parts, one for each index of `groups`. The reference program is written for one: setup_inputs(seed, part) draws one part's arguments, and reference() takes and returns one part's arrays. A program takes and returns all parts, laid end to end along the dimension named above; an argument that names none is the same for every part. Nothing has to cross between parts.
Inputs may be any that keep to these rules, and one draw needn't show every extreme that they name: `lengths`: each packed row uses 1 to 160 slots, all rows together half of the 640 slots, and some row uses all 160.
All inputs are finite; a program needn't handle non-finite values.
Results may differ from the reference program's by a relative error of at most 0.0042.
Values may be sent and summed in bfloat16 or wider, within the bound.
No kernel may reach another device: no remote copies, remote signals or barrier semaphores. Data moves between devices by JAX's collectives and lax.ppermute only.
A program may use at most 448 MiB of HBM per device.

```python
import math
import jax
import jax.numpy as jnp
import numpy as np

D = 8192
FW = 14336
TOK_DEV = 160
TOKENS = 640
N_COL = 4


def block_levels(rng, extent, split, smallest, high):
    level, own = 1.0, jax.random.fold_in(rng, 6)
    for axis_at, parts in split:
        draws = jnp.exp(jax.random.uniform(jax.random.fold_in(own, axis_at), (parts,), jnp.float32, smallest / len(split), high / len(split)))
        level = level * jnp.repeat(draws, extent[axis_at] // parts).reshape([-1 if axis == axis_at else 1 for axis in range(len(extent))])
    return level


def profile(number_of, total, reach, slope):
    loads = [(1 << 20) // math.isqrt(grade ** slope) + 1 for grade in range(2, number_of + 1)]
    rest, given = total - reach - (number_of - 1), [1] * (number_of - 1)
    while rest > 0:
        free = [i for i in range(number_of - 1) if given[i] < reach]
        whole, remaining = sum([loads[i] for i in free]), rest
        for i in free:
            extra = min(reach - given[i], max(1, remaining * loads[i] // whole), rest)
            given[i] = given[i] + extra
            rest = rest - extra
    return np.array([reach] + given)


def uneven_parts(key, number_of, total, limit, slope):
    if number_of == 2:
        one = jax.random.randint(key, (), max(1, total - limit), min(limit, total - 1) + 1)
        return jnp.stack([one, total - one])
    tallies = jnp.asarray(profile(number_of, total, limit, slope), jnp.int32)
    pairs = (number_of - 1) // 2
    giver, sink = tallies[1:1 + 2 * pairs:2], tallies[2:2 + 2 * pairs:2]
    slack = jnp.minimum(giver - 1, limit - sink)
    passed = jax.random.randint(jax.random.fold_in(key, 1), (pairs,), 0, 1 << 20) % (slack + 1)
    tallies = tallies.at[1:1 + 2 * pairs:2].set(giver - passed).at[2:2 + 2 * pairs:2].set(sink + passed)
    return tallies[jax.random.permutation(jax.random.fold_in(key, 2), number_of)]


def normal_values(key, extent, deviation, limit, split=(), kind=jnp.bfloat16):
    result = deviation * jax.random.normal(key, extent, jnp.float32)
    if split:
        result = result * block_levels(key, extent, split, -0.22, 0.18)
    return jnp.clip(result, -limit, limit).astype(kind)


def setup_inputs(seed: int = 0, part: int = 0) -> dict:
    key_list = jax.random.split(jax.random.key(seed), 6)
    part_splits = jax.random.split(jax.random.fold_in(key_list[5], part), 6)
    return {
        "tokens": normal_values(part_splits[0], (TOKENS, D), 1.0, 6.0, ((0, 4), (1, 4))),
        "lengths": uneven_parts(part_splits[1], N_COL, N_COL * TOK_DEV // 2, TOK_DEV, 2).astype(jnp.int32),
        "gate_weight": normal_values(key_list[2], (D, FW), D ** -0.5, 0.0625, ((0, 4), (1, 4))),
        "up_weight": normal_values(key_list[3], (D, FW), D ** -0.5, 0.0625, ((0, 4), (1, 4))),
        "down_weight": normal_values(key_list[4], (FW, D), FW ** -0.5, 0.046875, ((0, 4), (1, 4))),
    }


def reference(tokens, lengths, gate_weight, up_weight, down_weight):
    gate = jnp.dot(tokens, gate_weight, preferred_element_type=jnp.float32)
    up = jnp.dot(tokens, up_weight, preferred_element_type=jnp.float32)
    hidden = (jax.nn.silu(gate) * up).astype(jnp.bfloat16)
    branch = jnp.dot(hidden, down_weight, preferred_element_type=jnp.float32)
    slots = jnp.arange(TOKENS, dtype=jnp.int32)
    packed = slots // TOK_DEV
    inside = slots % TOK_DEV
    valid = inside < lengths[packed]
    total = tokens.astype(jnp.float32) + branch
    return jnp.where(valid[:, None], total, jnp.float32(0.0)).astype(jnp.bfloat16)
```

```python
import jax
import jax.numpy as jnp
from jax import lax
from jax.sharding import PartitionSpec as P

UNIT_CHUNKS = 2


def dot(a, b):
    return jnp.dot(a, b, preferred_element_type=jnp.float32)


def flip(value, axis, bit):
    count = lax.axis_size(axis)
    return lax.ppermute(value, axis, [(i, i ^ bit) for i in range(count)])


def spread(piece, zh, zl, x, k):
    other = flip(piece, "row", 2)
    stay = zh == x
    keep = jnp.where(stay, piece, other)
    send = jnp.where(stay, other, piece)
    pair = jnp.concatenate([keep, flip(send, "col", 2)], axis=0)
    other = flip(pair, "row", 1)
    stay = zl == k
    keep = jnp.where(stay, pair, other)
    send = jnp.where(stay, other, pair)
    return jnp.concatenate([keep, flip(send, "col", 1)], axis=0)


def stationary(tokens, lengths, gate_weight, up_weight, down_weight):
    slots, width = tokens.shape
    units = gate_weight.shape[1]
    c = lax.axis_index("col")
    r = lax.axis_index("row")
    x, k, zh, zl = c // 2, c % 2, r // 2, r % 2
    quarter = slots // 2
    starts = jnp.cumsum(lengths) - lengths
    first = jnp.take(starts, jnp.stack([c, c ^ 1]))
    count = jnp.take(lengths, jnp.stack([c, c ^ 1]))

    slot = jnp.arange(slots, dtype=jnp.int32)
    place = jnp.where(slot[None] < count[:, None], slot[None] + first[:, None], -1)
    inside = jnp.arange(quarter, dtype=jnp.int32)
    mine = jnp.concatenate([inside + quarter * c, inside + quarter * (c ^ 2)])

    sibling = flip(tokens, "col", 1)
    both = jnp.concatenate([tokens, sibling], axis=0)
    pick = (mine[:, None] == place.reshape(-1)[None]).astype(jnp.bfloat16)
    picked = dot(pick, both).astype(jnp.bfloat16)
    own = picked[:quarter] + flip(picked[quarter:], "col", 2)
    full = spread(own, zh, zl, x, k)

    half = 2 * quarter
    step = units // UNIT_CHUNKS
    branch = jnp.zeros((2 * half, down_weight.shape[1]), jnp.float32)
    for i in range(UNIT_CHUNKS):
        part = slice(i * step, (i + 1) * step)
        sums = jnp.stack([dot(full, gate_weight[:, part]), dot(full, up_weight[:, part])])
        sums = sums[:, :half] + flip(sums[:, half:].astype(jnp.bfloat16), "col", 1)
        sums = sums[:, :quarter] + flip(sums[:, quarter:].astype(jnp.bfloat16), "col", 2)
        hidden = (jax.nn.silu(sums[0]) * sums[1]).astype(jnp.bfloat16)
        branch = branch + dot(spread(hidden, zh, zl, x, k), down_weight[part])

    total = branch[:half] + flip(branch[half:].astype(jnp.bfloat16), "col", 1)
    theirs = flip(total.astype(jnp.bfloat16), "col", 2)
    total = total + jnp.concatenate([theirs[quarter:], theirs[:quarter]], axis=0)
    put = place.reshape(-1)[:, None] == mine[None]
    moved = jnp.dot(put.astype(jnp.float32), total, precision=lax.Precision.HIGHEST)
    handled = jnp.any(put, axis=1)
    mixed = jnp.where(handled[:, None], both.astype(jnp.float32) + moved, 0.0).astype(jnp.bfloat16)
    return mixed[:slots] + flip(mixed[slots:], "col", 1)


def general(tokens, lengths, gate_weight, up_weight, down_weight):
    c = lax.axis_index("col")
    slots = tokens.shape[0]
    whole = lax.all_gather(tokens, "row", axis=1, tiled=True)
    whole = lax.all_gather(whole, "col", axis=0, tiled=True)
    depth = gate_weight.shape[0]
    block = lax.dynamic_slice_in_dim(whole, c * depth, depth, axis=1)

    def summed(a, b):
        return lax.psum_scatter(dot(a, b), "col", scatter_dimension=0, tiled=True)

    hidden = (jax.nn.silu(summed(block, gate_weight)) * summed(block, up_weight)).astype(jnp.bfloat16)
    hidden = lax.all_gather(hidden, "row", axis=1, tiled=True)
    hidden = lax.all_gather(hidden, "col", axis=0, tiled=True)
    depth = down_weight.shape[0]
    branch = summed(lax.dynamic_slice_in_dim(hidden, c * depth, depth, axis=1), down_weight)
    valid = jnp.arange(slots, dtype=jnp.int32) < jnp.take(lengths, c)
    total = tokens.astype(jnp.float32) + branch
    return jnp.where(valid[:, None], total, jnp.float32(0.0)).astype(jnp.bfloat16)


def solution(mesh):
    square = mesh.shape["row"] == 4 and mesh.shape["col"] == 4
    in_specs = (
        P(("groups", "col"), "row"),
        P("groups"),
        P("col", "row"),
        P("col", "row"),
        P("col", "row"),
    )
    out_specs = P(("groups", "col"), "row")
    return jax.shard_map(
        stationary if square else general,
        mesh=mesh, in_specs=in_specs, out_specs=out_specs, check_vma=False,
    )
```

```python
import jax
import jax.numpy as jnp
from jax import lax
from jax.experimental import pallas as pl
from jax.experimental.pallas import tpu as pltpu
from jax.sharding import PartitionSpec as P

UNIT_CHUNKS = 2
HALVES = 2
TILE = 256


def dot(a, b):
    return jnp.dot(a, b, preferred_element_type=jnp.float32)


def flip(value, axis, bit):
    count = lax.axis_size(axis)
    return lax.ppermute(value, axis, [(i, i ^ bit) for i in range(count)])


def spread(piece, zh, zl, x, k):
    other = flip(piece, "row", 2)
    stay = zh == x
    keep = jnp.where(stay, piece, other)
    send = jnp.where(stay, other, piece)
    pair = jnp.concatenate([keep, flip(send, "col", 2)], axis=0)
    other = flip(pair, "row", 1)
    stay = zl == k
    keep = jnp.where(stay, pair, other)
    send = jnp.where(stay, other, pair)
    return jnp.concatenate([keep, flip(send, "col", 1)], axis=0)


def partial_sums_kernel(full_ref, gate_ref, up_ref, keep_ref, send_ref):
    half = full_ref.shape[0] // 2
    for i, weight_ref in enumerate((gate_ref, up_ref)):
        sums = dot(full_ref[...], weight_ref[...])
        keep_ref[i] = sums[:half]
        send_ref[i] = sums[half:].astype(jnp.bfloat16)


def partial_sums(full, gate_weight, up_weight, first, units):
    rows, depth = full.shape
    half = rows // 2
    weight = pl.BlockSpec((depth, TILE), lambda j: (0, first // TILE + j))
    out = pl.BlockSpec((2, half, TILE), lambda j: (0, 0, j))
    return pl.pallas_call(
        partial_sums_kernel,
        grid=(units // TILE,),
        in_specs=[pl.BlockSpec((rows, depth), lambda j: (0, 0)), weight, weight],
        out_specs=[out, out],
        out_shape=[
            jax.ShapeDtypeStruct((2, half, units), jnp.float32),
            jax.ShapeDtypeStruct((2, half, units), jnp.bfloat16),
        ],
        compiler_params=pltpu.CompilerParams(vmem_limit_bytes=24 * 2**20),
        cost_estimate=pl.CostEstimate(
            flops=4 * rows * depth * units,
            bytes_accessed=4 * depth * units + 6 * rows * units,
            transcendentals=0,
        ),
    )(full, gate_weight, up_weight)


def stationary(tokens, lengths, gate_weight, up_weight, down_weight):
    slots, width = tokens.shape
    units = gate_weight.shape[1]
    c = lax.axis_index("col")
    r = lax.axis_index("row")
    x, k, zh, zl = c // 2, c % 2, r // 2, r % 2
    quarter = slots // 2
    piece = quarter // HALVES

    rows = jnp.arange(lengths.shape[0], dtype=jnp.int32)
    slot = jnp.arange(slots, dtype=jnp.int32)
    places = []
    for row in (c, c ^ 1):
        first = jnp.sum(jnp.where(rows < row, lengths, 0))
        count = jnp.sum(jnp.where(rows == row, lengths, 0))
        places.append(jnp.where(slot < count, slot + first, -1))
    place = jnp.concatenate(places)
    inside = jnp.arange(piece, dtype=jnp.int32)
    mine = [
        jnp.concatenate([inside + quarter * c, inside + quarter * (c ^ 2)]) + h * piece
        for h in range(HALVES)
    ]

    both = jnp.concatenate([tokens, flip(tokens, "col", 1)], axis=0)
    half = 2 * piece
    step = units // UNIT_CHUNKS
    totals = []
    fulls = []
    for h in range(HALVES):
        pick = (mine[h][:, None] == place[None]).astype(jnp.bfloat16)
        picked = dot(pick, both).astype(jnp.bfloat16)
        own = picked[:piece] + flip(picked[piece:], "col", 2)
        fulls.append(spread(own, zh, zl, x, k))
    for h in range(HALVES):
        full = fulls[h]
        branch = 0.0
        for i in range(UNIT_CHUNKS):
            keep, send = partial_sums(full, gate_weight, up_weight, i * step, step)
            sums = keep + flip(send, "col", 1)
            sums = sums[:, :piece] + flip(sums[:, piece:].astype(jnp.bfloat16), "col", 2)
            hidden = (jax.nn.silu(sums[0]) * sums[1]).astype(jnp.bfloat16)
            part = slice(i * step, (i + 1) * step)
            branch = branch + dot(spread(hidden, zh, zl, x, k), down_weight[part])
        total = branch[:half] + flip(branch[half:].astype(jnp.bfloat16), "col", 1)
        theirs = flip(total.astype(jnp.bfloat16), "col", 2)
        totals.append(total + jnp.concatenate([theirs[piece:], theirs[:piece]], axis=0))

    put = place[:, None] == jnp.concatenate(mine)[None]
    moved = jnp.dot(
        put.astype(jnp.float32), jnp.concatenate(totals), precision=lax.Precision.HIGHEST
    )
    handled = jnp.any(put, axis=1)
    mixed = jnp.where(handled[:, None], both.astype(jnp.float32) + moved, 0.0).astype(jnp.bfloat16)
    return mixed[:slots] + flip(mixed[slots:], "col", 1)


def general(tokens, lengths, gate_weight, up_weight, down_weight):
    c = lax.axis_index("col")
    slots = tokens.shape[0]
    whole = lax.all_gather(tokens, "row", axis=1, tiled=True)
    whole = lax.all_gather(whole, "col", axis=0, tiled=True)
    depth = gate_weight.shape[0]
    block = lax.dynamic_slice_in_dim(whole, c * depth, depth, axis=1)

    def summed(a, b):
        return lax.psum_scatter(dot(a, b), "col", scatter_dimension=0, tiled=True)

    hidden = (jax.nn.silu(summed(block, gate_weight)) * summed(block, up_weight)).astype(jnp.bfloat16)
    hidden = lax.all_gather(hidden, "row", axis=1, tiled=True)
    hidden = lax.all_gather(hidden, "col", axis=0, tiled=True)
    depth = down_weight.shape[0]
    branch = summed(lax.dynamic_slice_in_dim(hidden, c * depth, depth, axis=1), down_weight)
    valid = jnp.arange(slots, dtype=jnp.int32) < jnp.take(lengths, c)
    total = tokens.astype(jnp.float32) + branch
    return jnp.where(valid[:, None], total, jnp.float32(0.0)).astype(jnp.bfloat16)


def solution(mesh):
    square = mesh.shape["row"] == 4 and mesh.shape["col"] == 4
    in_specs = (
        P(("groups", "col"), "row"),
        P("groups"),
        P("col", "row"),
        P("col", "row"),
        P("col", "row"),
    )
    out_specs = P(("groups", "col"), "row")
    return jax.shard_map(
        stationary if square else general,
        mesh=mesh, in_specs=in_specs, out_specs=out_specs, check_vma=False,
    )
```

```python
import jax
import jax.numpy as jnp
from jax import lax
from jax.sharding import PartitionSpec as P

UNIT_CHUNKS = 2
HALVES = 2


def dot(a, b):
    return jnp.dot(a, b, preferred_element_type=jnp.float32)


def flip(value, axis, bit):
    count = lax.axis_size(axis)
    return lax.ppermute(value, axis, [(i, i ^ bit) for i in range(count)])


def after(value, *others):
    return lax.optimization_barrier((value, *others))[0]


def stationary(tokens, lengths, gate_weight, up_weight, down_weight):
    slots, width = tokens.shape
    units = gate_weight.shape[1]
    c = lax.axis_index("col")
    r = lax.axis_index("row")
    x, k, zh, zl = c // 2, c % 2, r // 2, r % 2
    quarter = slots // 2
    piece = quarter // HALVES

    rows = jnp.arange(lengths.shape[0], dtype=jnp.int32)
    slot = jnp.arange(slots, dtype=jnp.int32)
    places = []
    for row in (c, c ^ 1):
        first = jnp.sum(jnp.where(rows < row, lengths, 0))
        count = jnp.sum(jnp.where(rows == row, lengths, 0))
        places.append(jnp.where(slot < count, slot + first, -1))
    inside = jnp.arange(piece, dtype=jnp.int32)
    mine = [
        jnp.concatenate([inside + quarter * c, inside + quarter * (c ^ 2)]) + h * piece
        for h in range(HALVES)
    ]

    busy = {}

    def swap(value, axis, bit, depth=1):
        link = (axis, bit) if bit == 1 and axis == "col" else axis
        line = busy.setdefault(link, [])
        if depth and len(line) >= depth:
            value = after(value, line[-depth])
        got = flip(value, axis, bit)
        line.append(got)
        return got

    def steps_of_spread(piece):
        other = swap(piece, "row", 2)
        yield
        stay = zh == x
        keep = jnp.where(stay, piece, other)
        send = jnp.where(stay, other, piece)
        pair = jnp.concatenate([keep, swap(send, "col", 2)], axis=0)
        yield
        other = swap(pair, "row", 1)
        yield
        stay = zl == k
        keep = jnp.where(stay, pair, other)
        send = jnp.where(stay, other, pair)
        yield jnp.concatenate([keep, swap(send, "col", 1, 0)], axis=0)

    sibling = flip(tokens, "col", 1)
    half = 2 * piece
    step = units // UNIT_CHUNKS

    def half_steps(h):
        own_pick = (mine[h][:, None] == places[0][None]).astype(jnp.bfloat16)
        sib_pick = (mine[h][:, None] == places[1][None]).astype(jnp.bfloat16)
        picked = (dot(own_pick, tokens) + dot(sib_pick, sibling)).astype(jnp.bfloat16)
        own = picked[:piece] + swap(picked[piece:], "col", 2)
        yield
        for full in steps_of_spread(own):
            yield full

    def chunk_steps(full, i):
        part = slice(i * step, (i + 1) * step)
        if "sums" in busy:
            full = after(full, busy["sums"])
        gate, up = dot(full, gate_weight[:, part]), dot(full, up_weight[:, part])
        send = jnp.stack([gate[half:], up[half:]]).astype(jnp.bfloat16)
        got = busy["sums"] = swap(send, "col", 1, 0)
        gate, up = gate[:half] + got[0], up[:half] + got[1]
        send = jnp.stack([gate[piece:], up[piece:]]).astype(jnp.bfloat16)
        got = swap(send, "col", 2)
        gate, up = gate[:piece] + got[0], up[:piece] + got[1]
        yield
        hidden = (jax.nn.silu(gate) * up).astype(jnp.bfloat16)
        for whole in steps_of_spread(hidden):
            yield whole

    def run(generators):
        results = [None] * len(generators)
        live = []
        waiting = list(range(len(generators)))
        while live or waiting:
            if waiting:
                live.append(waiting.pop(0))
            for index in list(live):
                try:
                    value = next(generators[index])
                    if value is not None:
                        results[index] = value
                except StopIteration:
                    live.remove(index)
        return results

    fulls = run([half_steps(h) for h in range(HALVES)])
    wholes = run([chunk_steps(fulls[h], i) for h in range(HALVES) for i in range(UNIT_CHUNKS)])
    totals = []
    for h in range(HALVES):
        branch = 0.0
        for i in range(UNIT_CHUNKS):
            branch = branch + dot(wholes[h * UNIT_CHUNKS + i], down_weight[i * step : (i + 1) * step])
        total = branch[:half] + swap(branch[half:].astype(jnp.bfloat16), "col", 1, 0)
        theirs = swap(total.astype(jnp.bfloat16), "col", 2)
        totals.append(total + jnp.concatenate([theirs[piece:], theirs[:piece]], axis=0))

    total = jnp.concatenate(totals)
    mixed = []
    for place, known in zip(places, (tokens, sibling)):
        put = place[:, None] == jnp.concatenate(mine)[None]
        moved = jnp.dot(put.astype(jnp.float32), total, precision=lax.Precision.HIGHEST)
        handled = jnp.any(put, axis=1)[:, None]
        mixed.append(jnp.where(handled, known.astype(jnp.float32) + moved, 0.0).astype(jnp.bfloat16))
    return mixed[0] + flip(mixed[1], "col", 1)


def general(tokens, lengths, gate_weight, up_weight, down_weight):
    c = lax.axis_index("col")
    slots = tokens.shape[0]
    whole = lax.all_gather(tokens, "row", axis=1, tiled=True)
    whole = lax.all_gather(whole, "col", axis=0, tiled=True)
    depth = gate_weight.shape[0]
    block = lax.dynamic_slice_in_dim(whole, c * depth, depth, axis=1)

    def summed(a, b):
        return lax.psum_scatter(dot(a, b), "col", scatter_dimension=0, tiled=True)

    hidden = (jax.nn.silu(summed(block, gate_weight)) * summed(block, up_weight)).astype(jnp.bfloat16)
    hidden = lax.all_gather(hidden, "row", axis=1, tiled=True)
    hidden = lax.all_gather(hidden, "col", axis=0, tiled=True)
    depth = down_weight.shape[0]
    branch = summed(lax.dynamic_slice_in_dim(hidden, c * depth, depth, axis=1), down_weight)
    valid = jnp.arange(slots, dtype=jnp.int32) < jnp.take(lengths, c)
    total = tokens.astype(jnp.float32) + branch
    return jnp.where(valid[:, None], total, jnp.float32(0.0)).astype(jnp.bfloat16)


def solution(mesh):
    square = mesh.shape["row"] == 4 and mesh.shape["col"] == 4
    in_specs = (
        P(("groups", "col"), "row"),
        P("groups"),
        P("col", "row"),
        P("col", "row"),
        P("col", "row"),
    )
    out_specs = P(("groups", "col"), "row")
    return jax.shard_map(
        stationary if square else general,
        mesh=mesh, in_specs=in_specs, out_specs=out_specs, check_vma=False,
    )
```

```python
import jax
import jax.numpy as jnp
from jax import lax
from jax.sharding import PartitionSpec as P

UNIT_CHUNKS = 2
HALVES = 2
ORDER = (
    "t0 t0 t1 t0 t1 t0 c00 c01 c00 c01 "
    "t1 t1 c10 c11 c00 c10 c01 c11 c00 "
    "c10 c01 c11 c00 c10 c01 b0 c11 "
    "b0 c10 c11 b1 b0 b1 b1"
)


def dot(a, b):
    return jnp.dot(a, b, preferred_element_type=jnp.float32)


def flip(value, axis, bit):
    count = lax.axis_size(axis)
    return lax.ppermute(value, axis, [(i, i ^ bit) for i in range(count)])


def stationary(tokens, lengths, gate_weight, up_weight, down_weight):
    slots, width = tokens.shape
    units = gate_weight.shape[1]
    col_count = lax.axis_size("col")
    c = lax.axis_index("col")
    r = lax.axis_index("row")
    x, k, zh, zl = c // 2, c % 2, r // 2, r % 2
    quarter = slots // 2
    piece = quarter // HALVES
    half = 2 * piece
    step = units // UNIT_CHUNKS

    rows = jnp.arange(lengths.shape[0], dtype=jnp.int32)
    slot = jnp.arange(slots, dtype=jnp.int32)
    places = []
    for row in (c, c ^ 1):
        first = jnp.sum(jnp.where(rows < row, lengths, 0))
        count = jnp.sum(jnp.where(rows == row, lengths, 0))
        places.append(jnp.where(slot < count, slot + first, -1))
    inside = jnp.arange(piece, dtype=jnp.int32)
    mine = [
        jnp.concatenate([inside + quarter * c, inside + quarter * (c ^ 2)]) + h * piece
        for h in range(HALVES)
    ]

    devices = [(i // col_count, i % col_count) for i in range(lax.axis_size("row") * col_count)]

    def move(value, where_to):
        pairs = []
        for i, (row, col) in enumerate(devices):
            to = where_to(row // 2, row % 2, col // 2, col % 2)
            if to is not None:
                to_zh, to_zl, to_x, to_k = to
                pairs.append((i, (to_zh * 2 + to_zl) * col_count + to_x * 2 + to_k))
        return lax.ppermute(value, ("row", "col"), pairs)

    def one_step(value, stay, first_to, second_to):
        first, second = move(value, first_to), move(value, second_to)

        def finish(value):
            return jnp.concatenate(
                [jnp.where(stay, value, first), jnp.where(stay, first, second)], axis=0
            )

        return finish

    def to_columns(value):
        return one_step(
            value,
            zh == x,
            lambda zh, zl, x, k: (1 - zh, zl, x, k) if x == zh else (zh, zl, 1 - x, k),
            lambda zh, zl, x, k: None if x == zh else (1 - zh, zl, 1 - x, k),
        )

    def to_cores(value):
        return one_step(
            value,
            zl == k,
            lambda zh, zl, x, k: (zh, 1 - zl, x, k) if k == zl else (zh, zl, x, 1 - k),
            lambda zh, zl, x, k: None if k == zl else (zh, 1 - zl, x, 1 - k),
        )

    sibling = flip(tokens, "col", 1)
    last = []

    def ordered(value):
        if last:
            value = lax.optimization_barrier((value, last[-1]))[0]
        return value

    def issued(value):
        last.append(value)
        return value

    def spread_steps(value):
        finish = to_columns(value)
        yield
        pair = issued(finish(ordered(value)))
        finish = to_cores(pair)
        yield
        whole = issued(finish(ordered(pair)))
        return whole

    def half_steps(h):
        own_pick = (mine[h][:, None] == places[0][None]).astype(jnp.bfloat16)
        sib_pick = (mine[h][:, None] == places[1][None]).astype(jnp.bfloat16)
        picked = dot(own_pick, tokens) + dot(ordered(sib_pick), sibling)
        picked = issued(picked.astype(jnp.bfloat16))
        got = flip(picked[piece:], "col", 2)
        yield
        own = issued(ordered(picked[:piece]) + got)
        return (yield from spread_steps(own))

    def chunk_steps(full, i):
        part = slice(i * step, (i + 1) * step)
        full = ordered(full)
        gate, up = dot(full, gate_weight[:, part]), dot(full, up_weight[:, part])
        send = issued(jnp.stack([gate[half:], up[half:]]).astype(jnp.bfloat16))
        got = flip(send, "col", 1)
        yield
        got = ordered(got)
        gate, up = gate[:half] + got[0], up[:half] + got[1]
        send = issued(jnp.stack([gate[piece:], up[piece:]]).astype(jnp.bfloat16))
        got = flip(send, "col", 2)
        yield
        got = ordered(got)
        gate, up = gate[:piece] + got[0], up[:piece] + got[1]
        hidden = issued((jax.nn.silu(gate) * up).astype(jnp.bfloat16))
        whole = yield from spread_steps(hidden)
        return issued(dot(ordered(whole), down_weight[part]))

    def branch_steps(parts):
        branch = issued(sum(parts[1:], parts[0]))
        got = flip(branch[half:].astype(jnp.bfloat16), "col", 1)
        yield
        total = issued(branch[:half] + ordered(got))
        got = flip(total.astype(jnp.bfloat16), "col", 2)
        yield
        got = ordered(got)
        return issued(total + jnp.concatenate([got[piece:], got[:piece]], axis=0))

    chains, results = {}, {}

    def advance(name):
        if name not in chains:
            kind, rest = name[0], name[1:]
            if kind == "t":
                chains[name] = half_steps(int(rest))
            elif kind == "c":
                chains[name] = chunk_steps(results["t" + rest[0]], int(rest[1]))
            else:
                parts = [results["c" + rest + str(i)] for i in range(UNIT_CHUNKS)]
                chains[name] = branch_steps(parts)
        try:
            next(chains[name])
        except StopIteration as stop:
            results[name] = stop.value

    for name in ORDER.split():
        advance(name)

    total = jnp.concatenate([results["b" + str(h)] for h in range(HALVES)])
    mixed = []
    for place, known in zip(places, (tokens, sibling)):
        put = place[:, None] == jnp.concatenate(mine)[None]
        moved = jnp.dot(put.astype(jnp.float32), total, precision=lax.Precision.HIGHEST)
        handled = jnp.any(put, axis=1)[:, None]
        mixed.append(jnp.where(handled, known.astype(jnp.float32) + moved, 0.0).astype(jnp.bfloat16))
    return mixed[0] + flip(mixed[1], "col", 1)


def general(tokens, lengths, gate_weight, up_weight, down_weight):
    c = lax.axis_index("col")
    slots = tokens.shape[0]
    whole = lax.all_gather(tokens, "row", axis=1, tiled=True)
    whole = lax.all_gather(whole, "col", axis=0, tiled=True)
    depth = gate_weight.shape[0]
    block = lax.dynamic_slice_in_dim(whole, c * depth, depth, axis=1)

    def summed(a, b):
        return lax.psum_scatter(dot(a, b), "col", scatter_dimension=0, tiled=True)

    hidden = (jax.nn.silu(summed(block, gate_weight)) * summed(block, up_weight)).astype(jnp.bfloat16)
    hidden = lax.all_gather(hidden, "row", axis=1, tiled=True)
    hidden = lax.all_gather(hidden, "col", axis=0, tiled=True)
    depth = down_weight.shape[0]
    branch = summed(lax.dynamic_slice_in_dim(hidden, c * depth, depth, axis=1), down_weight)
    valid = jnp.arange(slots, dtype=jnp.int32) < jnp.take(lengths, c)
    total = tokens.astype(jnp.float32) + branch
    return jnp.where(valid[:, None], total, jnp.float32(0.0)).astype(jnp.bfloat16)


def solution(mesh):
    square = mesh.shape["row"] == 4 and mesh.shape["col"] == 4
    in_specs = (
        P(("groups", "col"), "row"),
        P("groups"),
        P("col", "row"),
        P("col", "row"),
        P("col", "row"),
    )
    out_specs = P(("groups", "col"), "row")
    return jax.shard_map(
        stationary if square else general,
        mesh=mesh, in_specs=in_specs, out_specs=out_specs, check_vma=False,
    )
```

```python
import functools

import jax
import jax.numpy as jnp
from jax import lax
from jax.experimental import pallas as pl
from jax.experimental.pallas import tpu as pltpu
from jax.sharding import PartitionSpec as P

UNIT_CHUNKS = 2
HALVES = 2
ORDER = (
    "p t0 w0a t0",
    "t1 t0 c00 c00",
    "w1a c01 c01 t1",
    "t1 c00 c11 c01",
    "w0b c10 c11 c00",
    "c10 c01 c11 c00",
    "c10 c11 c01 b0",
    "c10 c11 b0 c10",
    "b1 b1 b0 b1",
)


def dot(a, b):
    return jnp.dot(a, b, preferred_element_type=jnp.float32)


def flip(value, axis, bit):
    count = lax.axis_size(axis)
    return lax.ppermute(value, axis, [(i, i ^ bit) for i in range(count)])


def pull_kernel(first, units, tick_ref, gate_ref, up_ref, gate_here, up_here, done_ref, sems):
    del tick_ref
    columns = pl.ds(first, units)
    copies = [
        pltpu.make_async_copy(source.at[:, columns], here, sems.at[i])
        for i, (source, here) in enumerate(((gate_ref, gate_here), (up_ref, up_here)))
    ]
    for copy in copies:
        copy.start()
    for copy in copies:
        copy.wait()
    done_ref[...] = jnp.zeros_like(done_ref)


def pull(gate_weight, up_weight, first, units, tick):
    far = pl.BlockSpec(memory_space=pltpu.HBM)
    near = pl.BlockSpec(memory_space=pltpu.VMEM)
    here = pltpu.VMEM((gate_weight.shape[0], units), gate_weight.dtype)
    return pl.pallas_call(
        functools.partial(pull_kernel, first, units),
        in_specs=[pl.BlockSpec(memory_space=pltpu.SMEM), far, far],
        out_specs=[near, near, near],
        out_shape=[here, here, jax.ShapeDtypeStruct((8, 128), jnp.float32)],
        scratch_shapes=[pltpu.SemaphoreType.DMA((2,))],
        compiler_params=pltpu.CompilerParams(
            vmem_limit_bytes=4 * gate_weight.shape[0] * units + 2**20
        ),
        cost_estimate=pl.CostEstimate(flops=0, bytes_accessed=0, transcendentals=0),
    )(
        tick,
        pltpu.with_memory_space_constraint(gate_weight, pltpu.HBM),
        pltpu.with_memory_space_constraint(up_weight, pltpu.HBM),
    )


def stationary(tokens, lengths, gate_weight, up_weight, down_weight):
    slots, width = tokens.shape
    units = gate_weight.shape[1]
    col_count = lax.axis_size("col")
    c = lax.axis_index("col")
    r = lax.axis_index("row")
    x, k, zh, zl = c // 2, c % 2, r // 2, r % 2
    quarter = slots // 2
    piece = quarter // HALVES
    half = 2 * piece
    step = units // UNIT_CHUNKS

    rows = jnp.arange(lengths.shape[0], dtype=jnp.int32)
    slot = jnp.arange(slots, dtype=jnp.int32)
    places = []
    for row in (c, c ^ 1):
        first = jnp.sum(jnp.where(rows < row, lengths, 0))
        count = jnp.sum(jnp.where(rows == row, lengths, 0))
        places.append(jnp.where(slot < count, slot + first, -1))
    inside = jnp.arange(piece, dtype=jnp.int32)
    mine = [
        jnp.concatenate([inside + quarter * c, inside + quarter * (c ^ 2)]) + h * piece
        for h in range(HALVES)
    ]

    devices = [(i // col_count, i % col_count) for i in range(lax.axis_size("row") * col_count)]

    def move(value, where_to):
        pairs = []
        for i, (row, col) in enumerate(devices):
            to = where_to(row // 2, row % 2, col // 2, col % 2)
            if to is not None:
                to_zh, to_zl, to_x, to_k = to
                pairs.append((i, (to_zh * 2 + to_zl) * col_count + to_x * 2 + to_k))
        return lax.ppermute(value, ("row", "col"), pairs)

    def one_step(value, stay, first_to, second_to):
        first, second = move(value, first_to), move(value, second_to)

        def finish(value):
            return jnp.concatenate(
                [jnp.where(stay, value, first), jnp.where(stay, first, second)], axis=0
            )

        return finish

    def to_columns(value):
        return one_step(
            value,
            zh == x,
            lambda zh, zl, x, k: (1 - zh, zl, x, k) if x == zh else (zh, zl, 1 - x, k),
            lambda zh, zl, x, k: None if x == zh else (1 - zh, zl, 1 - x, k),
        )

    def to_cores(value):
        return one_step(
            value,
            zl == k,
            lambda zh, zl, x, k: (zh, 1 - zl, x, k) if k == zl else (zh, zl, x, 1 - k),
            lambda zh, zl, x, k: None if k == zl else (zh, 1 - zl, x, 1 - k),
        )

    sibling = flip(tokens, "col", 1)
    last = []

    def ordered(value):
        if last:
            value = lax.optimization_barrier((value, last[-1]))[0]
        return value

    def issued(value):
        last.append(value)
        return value

    def spread_steps(value):
        finish = to_columns(value)
        yield
        pair = issued(finish(ordered(value)))
        finish = to_cores(pair)
        yield
        whole = issued(finish(ordered(pair)))
        return whole

    picked = {}

    def pick_steps():
        own = jnp.concatenate(mine)[:, None] == places[0][None]
        sib = jnp.concatenate(mine)[:, None] == places[1][None]
        rows = dot(own.astype(jnp.bfloat16), tokens) + dot(sib.astype(jnp.bfloat16), sibling)
        rows = issued(rows.astype(jnp.bfloat16)).reshape(HALVES, 2, piece, width)
        picked["got"] = flip(rows[:, 1], "col", 2)
        picked["rows"] = rows[:, 0]
        return None
        yield

    def half_steps(h):
        own = issued(ordered(picked["rows"][h]) + picked["got"][h])
        return (yield from spread_steps(own))

    weights = {}

    def pull_steps(i):
        gate, up, done = pull(gate_weight, up_weight, i * step, step, ordered(lengths))
        weights[i] = gate, up
        issued(done)
        return None
        yield

    def chunk_steps(full, i):
        part = slice(i * step, (i + 1) * step)
        full = ordered(full)
        gate, up = (dot(full, weight) for weight in weights[i])
        send = issued(jnp.stack([gate[half:], up[half:]]).astype(jnp.bfloat16))
        got = flip(send, "col", 1)
        yield
        got = ordered(got)
        gate, up = gate[:half] + got[0], up[:half] + got[1]
        send = issued(jnp.stack([gate[piece:], up[piece:]]).astype(jnp.bfloat16))
        got = flip(send, "col", 2)
        yield
        got = ordered(got)
        gate, up = gate[:piece] + got[0], up[:piece] + got[1]
        hidden = issued((jax.nn.silu(gate) * up).astype(jnp.bfloat16))
        whole = yield from spread_steps(hidden)
        return issued(dot(ordered(whole), down_weight[part]))

    def branch_steps(parts):
        branch = issued(sum(parts[1:], parts[0]))
        got = flip(branch[half:].astype(jnp.bfloat16), "col", 1)
        yield
        total = issued(branch[:half] + ordered(got))
        got = flip(total.astype(jnp.bfloat16), "col", 2)
        yield
        got = ordered(got)
        return issued(total + jnp.concatenate([got[piece:], got[:piece]], axis=0))

    chains, results = {}, {}

    def advance(name):
        if name not in chains:
            kind, rest = name[0], name[1:]
            if kind == "p":
                chains[name] = pick_steps()
            elif kind == "w":
                chains[name] = pull_steps(int(rest[0]))
            elif kind == "t":
                chains[name] = half_steps(int(rest))
            elif kind == "c":
                chains[name] = chunk_steps(results["t" + rest[0]], int(rest[1]))
            else:
                parts = [results["c" + rest + str(i)] for i in range(UNIT_CHUNKS)]
                chains[name] = branch_steps(parts)
        try:
            next(chains[name])
        except StopIteration as stop:
            results[name] = stop.value

    for line in ORDER:
        for name in line.split():
            advance(name)

    total = jnp.concatenate([results["b" + str(h)] for h in range(HALVES)])
    mixed = []
    for place, known in zip(places, (tokens, sibling)):
        put = place[:, None] == jnp.concatenate(mine)[None]
        moved = jnp.dot(put.astype(jnp.float32), total, precision=lax.Precision.HIGHEST)
        handled = jnp.any(put, axis=1)[:, None]
        mixed.append(jnp.where(handled, known.astype(jnp.float32) + moved, 0.0).astype(jnp.bfloat16))
    return mixed[0] + flip(mixed[1], "col", 1)


def general(tokens, lengths, gate_weight, up_weight, down_weight):
    c = lax.axis_index("col")
    slots = tokens.shape[0]
    whole = lax.all_gather(tokens, "row", axis=1, tiled=True)
    whole = lax.all_gather(whole, "col", axis=0, tiled=True)
    depth = gate_weight.shape[0]
    block = lax.dynamic_slice_in_dim(whole, c * depth, depth, axis=1)

    def summed(a, b):
        return lax.psum_scatter(dot(a, b), "col", scatter_dimension=0, tiled=True)

    hidden = (jax.nn.silu(summed(block, gate_weight)) * summed(block, up_weight)).astype(jnp.bfloat16)
    hidden = lax.all_gather(hidden, "row", axis=1, tiled=True)
    hidden = lax.all_gather(hidden, "col", axis=0, tiled=True)
    depth = down_weight.shape[0]
    branch = summed(lax.dynamic_slice_in_dim(hidden, c * depth, depth, axis=1), down_weight)
    valid = jnp.arange(slots, dtype=jnp.int32) < jnp.take(lengths, c)
    total = tokens.astype(jnp.float32) + branch
    return jnp.where(valid[:, None], total, jnp.float32(0.0)).astype(jnp.bfloat16)


def solution(mesh):
    square = mesh.shape["row"] == 4 and mesh.shape["col"] == 4
    in_specs = (
        P(("groups", "col"), "row"),
        P("groups"),
        P("col", "row"),
        P("col", "row"),
        P("col", "row"),
    )
    out_specs = P(("groups", "col"), "row")
    return jax.shard_map(
        stationary if square else general,
        mesh=mesh, in_specs=in_specs, out_specs=out_specs, check_vma=False,
    )
```

```python
import jax
import jax.numpy as jnp
from jax import lax
from jax.sharding import PartitionSpec as P

UNIT_CHUNKS = 2
HALVES = 2
EDGES = {
    "t1.add": ["t0.columns"],
    "c00.dots": ["t1.columns"],
    "t1.cores": ["c01.dots"],
    "c01.dots": ["c00.sum"],
    "c10.dots": ["c01.cores_swapped"],
    "c11.dots": ["c10.cores_swapped"],
    "c00.hidden": ["c01.sum"],
    "c01.hidden": ["c10.sum"],
    "c10.hidden": ["c11.sum"],
    "c00.columns": ["c01.hidden"],
    "c01.columns": ["c10.hidden"],
    "c10.columns": ["c11.hidden"],
    "c00.cores": ["c01.columns"],
    "c01.cores": ["c10.columns"],
    "c10.cores": ["c11.columns"],
}


def dot(a, b):
    return jnp.dot(a, b, preferred_element_type=jnp.float32)


def flip(value, axis, bit):
    count = lax.axis_size(axis)
    return lax.ppermute(value, axis, [(i, i ^ bit) for i in range(count)])


def stationary(tokens, lengths, gate_weight, up_weight, down_weight):
    slots, width = tokens.shape
    units = gate_weight.shape[1]
    col_count = lax.axis_size("col")
    c = lax.axis_index("col")
    r = lax.axis_index("row")
    x, k, zh, zl = c // 2, c % 2, r // 2, r % 2
    quarter = slots // 2
    piece = quarter // HALVES
    half = 2 * piece
    step = units // UNIT_CHUNKS

    rows = jnp.arange(lengths.shape[0], dtype=jnp.int32)
    slot = jnp.arange(slots, dtype=jnp.int32)
    places = []
    for row in (c, c ^ 1):
        first = jnp.sum(jnp.where(rows < row, lengths, 0))
        count = jnp.sum(jnp.where(rows == row, lengths, 0))
        places.append(jnp.where(slot < count, slot + first, -1))
    inside = jnp.arange(piece, dtype=jnp.int32)
    mine = [
        jnp.concatenate([inside + quarter * c, inside + quarter * (c ^ 2)]) + h * piece
        for h in range(HALVES)
    ]

    devices = [(i // col_count, i % col_count) for i in range(lax.axis_size("row") * col_count)]

    def move(value, where_to):
        pairs = []
        for i, (row, col) in enumerate(devices):
            to = where_to(row // 2, row % 2, col // 2, col % 2)
            if to is not None:
                to_zh, to_zl, to_x, to_k = to
                pairs.append((i, (to_zh * 2 + to_zl) * col_count + to_x * 2 + to_k))
        return lax.ppermute(value, ("row", "col"), pairs)

    def one_step(value, stay, first_to, second_to):
        first, second = move(value, first_to), move(value, second_to)

        def finish(value):
            return jnp.concatenate(
                [jnp.where(stay, value, first), jnp.where(stay, first, second)], axis=0
            )

        return finish

    def to_columns(value):
        return one_step(
            value,
            zh == x,
            lambda zh, zl, x, k: (1 - zh, zl, x, k) if x == zh else (zh, zl, 1 - x, k),
            lambda zh, zl, x, k: None if x == zh else (1 - zh, zl, 1 - x, k),
        )

    def to_cores(value):
        return one_step(
            value,
            zl == k,
            lambda zh, zl, x, k: (zh, 1 - zl, x, k) if k == zl else (zh, zl, x, 1 - k),
            lambda zh, zl, x, k: None if k == zl else (zh, 1 - zl, x, 1 - k),
        )

    sibling = flip(tokens, "col", 1)
    seen = {}

    def ordered(step, value):
        for name in EDGES.get(step, ()):
            while name not in seen:
                advance(name.split(".")[0])
        others = [seen[name] for name in EDGES.get(step, ())]
        return lax.optimization_barrier((value, *others))[0] if others else value

    def issued(step, value):
        seen[step] = value
        return value

    def spread_steps(name, value):
        finish = to_columns(value)
        yield
        pair = issued(name + ".columns", finish(ordered(name + ".columns", value)))
        finish = to_cores(pair)
        yield
        return issued(name + ".cores", finish(ordered(name + ".cores", pair)))

    picked = {}

    def pick_steps():
        own = jnp.concatenate(mine)[:, None] == places[0][None]
        sib = jnp.concatenate(mine)[:, None] == places[1][None]
        rows = dot(own.astype(jnp.bfloat16), tokens) + dot(sib.astype(jnp.bfloat16), sibling)
        rows = rows.astype(jnp.bfloat16).reshape(HALVES, 2, piece, width)
        picked["got"] = flip(rows[:, 1], "col", 2)
        picked["rows"] = rows[:, 0]
        return None
        yield

    def half_steps(name, h):
        own = ordered(name + ".add", picked["rows"][h]) + picked["got"][h]
        own = issued(name + ".add", own)
        return (yield from spread_steps(name, own))

    def chunk_steps(name, h, i):
        full = result("t" + str(h))
        part = slice(i * step, (i + 1) * step)
        full = ordered(name + ".dots", full)
        gate, up = dot(full, gate_weight[:, part]), dot(full, up_weight[:, part])
        send = issued(name + ".dots", jnp.stack([gate[half:], up[half:]]).astype(jnp.bfloat16))
        got = issued(name + ".cores_swapped", flip(send, "col", 1))
        yield
        got = ordered(name + ".sum", got)
        gate, up = gate[:half] + got[0], up[:half] + got[1]
        send = issued(name + ".sum", jnp.stack([gate[piece:], up[piece:]]).astype(jnp.bfloat16))
        got = flip(send, "col", 2)
        yield
        got = ordered(name + ".hidden", got)
        gate, up = gate[:piece] + got[0], up[:piece] + got[1]
        hidden = issued(name + ".hidden", (jax.nn.silu(gate) * up).astype(jnp.bfloat16))
        whole = yield from spread_steps(name, hidden)
        whole = ordered(name + ".down", whole)
        return issued(name + ".down", dot(whole, down_weight[part]))

    def branch_steps(name, h):
        parts = [result("c" + str(h) + str(i)) for i in range(UNIT_CHUNKS)]
        branch = issued(name + ".branch", sum(parts[1:], parts[0]))
        got = flip(branch[half:].astype(jnp.bfloat16), "col", 1)
        yield
        total = issued(name + ".total", branch[:half] + ordered(name + ".total", got))
        got = flip(total.astype(jnp.bfloat16), "col", 2)
        yield
        got = ordered(name + ".all", got)
        return issued(name + ".all", total + jnp.concatenate([got[piece:], got[:piece]], axis=0))

    chains, results = {"p": pick_steps()}, {}
    for h in range(HALVES):
        chains["t" + str(h)] = half_steps("t" + str(h), h)
        for i in range(UNIT_CHUNKS):
            chains["c" + str(h) + str(i)] = chunk_steps("c" + str(h) + str(i), h, i)
        chains["b" + str(h)] = branch_steps("b" + str(h), h)

    def advance(name):
        try:
            next(chains[name])
        except StopIteration as stop:
            results[name] = stop.value

    def result(name):
        while name not in results:
            advance(name)
        return results[name]

    result("p")
    for h in range(HALVES):
        result("b" + str(h))

    total = jnp.concatenate([results["b" + str(h)] for h in range(HALVES)])
    mixed = []
    for place, known in zip(places, (tokens, sibling)):
        put = place[:, None] == jnp.concatenate(mine)[None]
        moved = jnp.dot(put.astype(jnp.float32), total, precision=lax.Precision.HIGHEST)
        handled = jnp.any(put, axis=1)[:, None]
        mixed.append(jnp.where(handled, known.astype(jnp.float32) + moved, 0.0).astype(jnp.bfloat16))
    return mixed[0] + flip(mixed[1], "col", 1)


def general(tokens, lengths, gate_weight, up_weight, down_weight):
    c = lax.axis_index("col")
    slots = tokens.shape[0]
    whole = lax.all_gather(tokens, "row", axis=1, tiled=True)
    whole = lax.all_gather(whole, "col", axis=0, tiled=True)
    depth = gate_weight.shape[0]
    block = lax.dynamic_slice_in_dim(whole, c * depth, depth, axis=1)

    def summed(a, b):
        return lax.psum_scatter(dot(a, b), "col", scatter_dimension=0, tiled=True)

    hidden = (jax.nn.silu(summed(block, gate_weight)) * summed(block, up_weight)).astype(jnp.bfloat16)
    hidden = lax.all_gather(hidden, "row", axis=1, tiled=True)
    hidden = lax.all_gather(hidden, "col", axis=0, tiled=True)
    depth = down_weight.shape[0]
    branch = summed(lax.dynamic_slice_in_dim(hidden, c * depth, depth, axis=1), down_weight)
    valid = jnp.arange(slots, dtype=jnp.int32) < jnp.take(lengths, c)
    total = tokens.astype(jnp.float32) + branch
    return jnp.where(valid[:, None], total, jnp.float32(0.0)).astype(jnp.bfloat16)


def solution(mesh):
    square = mesh.shape["row"] == 4 and mesh.shape["col"] == 4
    in_specs = (
        P(("groups", "col"), "row"),
        P("groups"),
        P("col", "row"),
        P("col", "row"),
        P("col", "row"),
    )
    out_specs = P(("groups", "col"), "row")
    return jax.shard_map(
        stationary if square else general,
        mesh=mesh, in_specs=in_specs, out_specs=out_specs, check_vma=False,
    )
```

```python
import jax
import jax.numpy as jnp
from jax import lax
from jax.sharding import PartitionSpec as P

UNIT_CHUNKS = 2
HALVES = 2
EDGES = {
    "t1.add": ["t0.halves"],
    "c01.dots": ["c00.sum"],
    "c10.dots": ["c01.sum"],
    "c11.dots": ["c10.sum"],
}


def dot(a, b):
    return jnp.dot(a, b, preferred_element_type=jnp.float32)


def flip(value, axis, bit):
    count = lax.axis_size(axis)
    return lax.ppermute(value, axis, [(i, i ^ bit) for i in range(count)])


def stationary(tokens, lengths, gate_weight, up_weight, down_weight):
    slots, width = tokens.shape
    units = gate_weight.shape[1]
    col_count = lax.axis_size("col")
    c = lax.axis_index("col")
    r = lax.axis_index("row")
    x, k, zh, zl = c // 2, c % 2, r // 2, r % 2
    quarter = slots // 2
    piece = quarter // HALVES
    half = 2 * piece
    step = units // UNIT_CHUNKS

    rows = jnp.arange(lengths.shape[0], dtype=jnp.int32)
    slot = jnp.arange(slots, dtype=jnp.int32)
    places = []
    for row in (c, c ^ 1):
        first = jnp.sum(jnp.where(rows < row, lengths, 0))
        count = jnp.sum(jnp.where(rows == row, lengths, 0))
        places.append(jnp.where(slot < count, slot + first, -1))
    inside = jnp.arange(piece, dtype=jnp.int32)
    mine = [
        jnp.concatenate([inside + quarter * c, inside + quarter * (c ^ 2)]) + h * piece
        for h in range(HALVES)
    ]

    devices = [(i // col_count, i % col_count) for i in range(lax.axis_size("row") * col_count)]

    def move(value, where_to):
        pairs = []
        for i, (row, col) in enumerate(devices):
            to = where_to(row // 2, row % 2, col // 2, col % 2)
            if to is not None:
                to_zh, to_zl, to_x, to_k = to
                pairs.append((i, (to_zh * 2 + to_zl) * col_count + to_x * 2 + to_k))
        return lax.ppermute(value, ("row", "col"), pairs)

    def one_step(value, stay, first_to, second_to):
        first, second = move(value, first_to), move(value, second_to)

        def finish(value):
            return jnp.concatenate(
                [jnp.where(stay, value, first), jnp.where(stay, first, second)], axis=0
            )

        return finish

    def to_cores(value):
        return one_step(
            value,
            zl == k,
            lambda zh, zl, x, k: (zh, 1 - zl, x, k) if k == zl else (zh, zl, x, 1 - k),
            lambda zh, zl, x, k: None if k == zl else (zh, 1 - zl, x, 1 - k),
        )

    sibling = flip(tokens, "col", 1)
    seen = {}

    def ordered(step, value):
        for name in EDGES.get(step, ()):
            while name not in seen:
                advance(name.split(".")[0])
        others = [seen[name] for name in EDGES.get(step, ())]
        return lax.optimization_barrier((value, *others))[0] if others else value

    def issued(step, value):
        seen[step] = value
        return value

    def swap_x(value):
        pairs = [[i, i ^ 2] for i in range(col_count) if not i & 2]
        both = lax.all_gather(value, "col", axis_index_groups=pairs)
        return lax.dynamic_index_in_dim(both, 1 - x, keepdims=False)

    def spread_steps(name, value):
        other = flip(value, "row", 2)
        yield
        other = ordered(name + ".halves", other)
        keep = jnp.where(zh == x, value, other)
        send = issued(name + ".halves", jnp.where(zh == x, other, value))
        got = swap_x(send)
        yield
        got = ordered(name + ".columns", got)
        pair = issued(name + ".columns", jnp.concatenate([keep, got], axis=0))
        finish = to_cores(pair)
        yield
        return issued(name + ".cores", finish(ordered(name + ".cores", pair)))

    picked = {}

    def pick_steps():
        own = jnp.concatenate(mine)[:, None] == places[0][None]
        sib = jnp.concatenate(mine)[:, None] == places[1][None]
        rows = dot(own.astype(jnp.bfloat16), tokens) + dot(sib.astype(jnp.bfloat16), sibling)
        rows = rows.astype(jnp.bfloat16).reshape(HALVES, 2, piece, width)
        picked["got"] = swap_x(rows[:, 1])
        picked["rows"] = rows[:, 0]
        return None
        yield

    def half_steps(name, h):
        own = ordered(name + ".add", picked["rows"][h]) + picked["got"][h]
        own = issued(name + ".add", own)
        return (yield from spread_steps(name, own))

    def chunk_steps(name, h, i):
        full = result("t" + str(h))
        part = slice(i * step, (i + 1) * step)
        full = ordered(name + ".dots", full)
        gate, up = dot(full, gate_weight[:, part]), dot(full, up_weight[:, part])
        send = issued(name + ".dots", jnp.stack([gate[half:], up[half:]]).astype(jnp.bfloat16))
        got = issued(name + ".cores_swapped", flip(send, "col", 1))
        yield
        got = ordered(name + ".sum", got)
        gate, up = gate[:half] + got[0], up[:half] + got[1]
        send = issued(name + ".sum", jnp.stack([gate[piece:], up[piece:]]).astype(jnp.bfloat16))
        got = swap_x(send)
        yield
        got = ordered(name + ".hidden", got)
        gate, up = gate[:piece] + got[0], up[:piece] + got[1]
        hidden = issued(name + ".hidden", (jax.nn.silu(gate) * up).astype(jnp.bfloat16))
        whole = yield from spread_steps(name, hidden)
        whole = ordered(name + ".down", whole)
        return issued(name + ".down", dot(whole, down_weight[part]))

    def branch_steps(name, h):
        parts = [result("c" + str(h) + str(i)) for i in range(UNIT_CHUNKS)]
        branch = issued(name + ".branch", sum(parts[1:], parts[0]))
        got = flip(branch[half:].astype(jnp.bfloat16), "col", 1)
        yield
        total = issued(name + ".total", branch[:half] + ordered(name + ".total", got))
        got = swap_x(total.astype(jnp.bfloat16))
        yield
        got = ordered(name + ".all", got)
        return issued(name + ".all", total + jnp.concatenate([got[piece:], got[:piece]], axis=0))

    chains, results = {"p": pick_steps()}, {}
    for h in range(HALVES):
        chains["t" + str(h)] = half_steps("t" + str(h), h)
        for i in range(UNIT_CHUNKS):
            chains["c" + str(h) + str(i)] = chunk_steps("c" + str(h) + str(i), h, i)
        chains["b" + str(h)] = branch_steps("b" + str(h), h)

    def advance(name):
        try:
            next(chains[name])
        except StopIteration as stop:
            results[name] = stop.value

    def result(name):
        while name not in results:
            advance(name)
        return results[name]

    result("p")
    for h in range(HALVES):
        result("b" + str(h))

    total = jnp.concatenate([results["b" + str(h)] for h in range(HALVES)])
    mixed = []
    for place, known in zip(places, (tokens, sibling)):
        put = place[:, None] == jnp.concatenate(mine)[None]
        moved = jnp.dot(put.astype(jnp.float32), total, precision=lax.Precision.HIGHEST)
        handled = jnp.any(put, axis=1)[:, None]
        mixed.append(jnp.where(handled, known.astype(jnp.float32) + moved, 0.0).astype(jnp.bfloat16))
    return mixed[0] + flip(mixed[1], "col", 1)


def general(tokens, lengths, gate_weight, up_weight, down_weight):
    c = lax.axis_index("col")
    slots = tokens.shape[0]
    whole = lax.all_gather(tokens, "row", axis=1, tiled=True)
    whole = lax.all_gather(whole, "col", axis=0, tiled=True)
    depth = gate_weight.shape[0]
    block = lax.dynamic_slice_in_dim(whole, c * depth, depth, axis=1)

    def summed(a, b):
        return lax.psum_scatter(dot(a, b), "col", scatter_dimension=0, tiled=True)

    hidden = (jax.nn.silu(summed(block, gate_weight)) * summed(block, up_weight)).astype(jnp.bfloat16)
    hidden = lax.all_gather(hidden, "row", axis=1, tiled=True)
    hidden = lax.all_gather(hidden, "col", axis=0, tiled=True)
    depth = down_weight.shape[0]
    branch = summed(lax.dynamic_slice_in_dim(hidden, c * depth, depth, axis=1), down_weight)
    valid = jnp.arange(slots, dtype=jnp.int32) < jnp.take(lengths, c)
    total = tokens.astype(jnp.float32) + branch
    return jnp.where(valid[:, None], total, jnp.float32(0.0)).astype(jnp.bfloat16)


def solution(mesh):
    square = mesh.shape["row"] == 4 and mesh.shape["col"] == 4
    in_specs = (
        P(("groups", "col"), "row"),
        P("groups"),
        P("col", "row"),
        P("col", "row"),
        P("col", "row"),
    )
    out_specs = P(("groups", "col"), "row")
    return jax.shard_map(
        stationary if square else general,
        mesh=mesh, in_specs=in_specs, out_specs=out_specs, check_vma=False,
    )
```

```python
import functools

import jax
import jax.numpy as jnp
from jax import lax
from jax.experimental import pallas as pl
from jax.experimental.pallas import tpu as pltpu
from jax.sharding import PartitionSpec as P

HALVES = 2
PARTS = ((14, 14), (18, 10))
EDGES = {
    "w.pull": ["t0.add"],
    "t0.halves": ["w.pull"],
    "t1.add": ["t0.halves"],
    "t1.halves": ["t0.columns"],
    "c00.dots": ["t1.columns"],
    "c01.dots": ["c00.sum"],
    "t1.cores": ["c01.sum"],
    "c00.hidden": ["c01.sum"],
    "c01.hidden": ["c10.sum"],
    "c11.dots": ["c10.sum"],
    "c00.halves": ["c01.hidden"],
    "c10.hidden": ["c11.sum"],
    "c01.halves": ["c10.hidden"],
    "c10.halves": ["c11.hidden"],
}


def dot(a, b):
    return jnp.dot(a, b, preferred_element_type=jnp.float32)


def flip(value, axis, bit):
    count = lax.axis_size(axis)
    return lax.ppermute(value, axis, [(i, i ^ bit) for i in range(count)])


def pull_kernel(first, end, tick_ref, gate_ref, up_ref, gate_here, up_here, done_ref, sems):
    del tick_ref
    columns = pl.ds(first, end - first)
    copies = [
        pltpu.make_async_copy(source.at[:, columns], here, sems.at[i])
        for i, (source, here) in enumerate(((gate_ref, gate_here), (up_ref, up_here)))
    ]
    for copy in copies:
        copy.start()
    for copy in copies:
        copy.wait()
    done_ref[...] = jnp.zeros_like(done_ref)


def pull(gate_weight, up_weight, first, end, tick):
    far = pl.BlockSpec(memory_space=pltpu.HBM)
    near = pl.BlockSpec(memory_space=pltpu.VMEM)
    here = pltpu.VMEM((gate_weight.shape[0], end - first), gate_weight.dtype)
    return pl.pallas_call(
        functools.partial(pull_kernel, first, end),
        in_specs=[pl.BlockSpec(memory_space=pltpu.SMEM), far, far],
        out_specs=[near, near, near],
        out_shape=[here, here, jax.ShapeDtypeStruct((8, 128), jnp.float32)],
        scratch_shapes=[pltpu.SemaphoreType.DMA((2,))],
        compiler_params=pltpu.CompilerParams(
            vmem_limit_bytes=4 * gate_weight.shape[0] * (end - first) + 2**20
        ),
        cost_estimate=pl.CostEstimate(flops=0, bytes_accessed=0, transcendentals=0),
    )(
        tick,
        pltpu.with_memory_space_constraint(gate_weight, pltpu.HBM),
        pltpu.with_memory_space_constraint(up_weight, pltpu.HBM),
    )


def stationary(tokens, lengths, gate_weight, up_weight, down_weight):
    slots, width = tokens.shape
    units = gate_weight.shape[1]
    col_count = lax.axis_size("col")
    c = lax.axis_index("col")
    r = lax.axis_index("row")
    x, k, zh, zl = c // 2, c % 2, r // 2, r % 2
    quarter = slots // 2
    piece = quarter // HALVES
    half = 2 * piece
    spans = []
    for sizes in PARTS:
        ends = [0]
        for size in sizes:
            ends.append(ends[-1] + units * size // sum(sizes))
        spans.append(list(zip(ends[:-1], ends[1:])))

    rows = jnp.arange(lengths.shape[0], dtype=jnp.int32)
    slot = jnp.arange(slots, dtype=jnp.int32)
    places = []
    for row in (c, c ^ 1):
        first = jnp.sum(jnp.where(rows < row, lengths, 0))
        count = jnp.sum(jnp.where(rows == row, lengths, 0))
        places.append(jnp.where(slot < count, slot + first, -1))
    inside = jnp.arange(piece, dtype=jnp.int32)
    mine = [
        jnp.concatenate([inside + quarter * c, inside + quarter * (c ^ 2)]) + h * piece
        for h in range(HALVES)
    ]

    devices = [(i // col_count, i % col_count) for i in range(lax.axis_size("row") * col_count)]

    def move(value, where_to):
        pairs = []
        for i, (row, col) in enumerate(devices):
            to = where_to(row // 2, row % 2, col // 2, col % 2)
            if to is not None:
                to_zh, to_zl, to_x, to_k = to
                pairs.append((i, (to_zh * 2 + to_zl) * col_count + to_x * 2 + to_k))
        return lax.ppermute(value, ("row", "col"), pairs)

    def one_step(value, stay, first_to, second_to):
        first, second = move(value, first_to), move(value, second_to)

        def finish(value):
            return jnp.concatenate(
                [jnp.where(stay, value, first), jnp.where(stay, first, second)], axis=0
            )

        return finish

    def to_cores(value):
        return one_step(
            value,
            zl == k,
            lambda zh, zl, x, k: (zh, 1 - zl, x, k) if k == zl else (zh, zl, x, 1 - k),
            lambda zh, zl, x, k: None if k == zl else (zh, 1 - zl, x, 1 - k),
        )

    sibling = flip(tokens, "col", 1)
    seen = {}

    def ordered(step, value):
        for name in EDGES.get(step, ()):
            while name not in seen:
                advance(name.split(".")[0])
        others = [seen[name] for name in EDGES.get(step, ())]
        return lax.optimization_barrier((value, *others))[0] if others else value

    def issued(step, value):
        seen[step] = value
        return value

    def swap_x(value):
        return flip(value, "col", 2)

    def spread_steps(name, value):
        other = flip(value, "row", 2)
        yield
        other = ordered(name + ".halves", other)
        keep = jnp.where(zh == x, value, other)
        send = issued(name + ".halves", jnp.where(zh == x, other, value))
        got = swap_x(send)
        yield
        got = ordered(name + ".columns", got)
        pair = issued(name + ".columns", jnp.concatenate([keep, got], axis=0))
        finish = to_cores(pair)
        yield
        return issued(name + ".cores", finish(ordered(name + ".cores", pair)))

    picked = {}

    def pick_steps():
        own = jnp.concatenate(mine)[:, None] == places[0][None]
        sib = jnp.concatenate(mine)[:, None] == places[1][None]
        rows = dot(own.astype(jnp.bfloat16), tokens) + dot(sib.astype(jnp.bfloat16), sibling)
        rows = rows.astype(jnp.bfloat16).reshape(HALVES, 2, piece, width)
        picked["got"] = swap_x(rows[:, 1])
        picked["rows"] = rows[:, 0]
        return None
        yield

    pulled = []

    def pull_steps():
        tick = ordered("w.pull", lengths)
        *both, done = pull(gate_weight, up_weight, *spans[0][0], tick)
        pulled.extend(both)
        issued("w.pull", done)
        return None
        yield

    def half_steps(name, h):
        own = issued(name + ".add", ordered(name + ".add", picked["rows"][h]) + picked["got"][h])
        return (yield from spread_steps(name, own))

    def chunk_steps(name, h, i):
        full = result("t" + str(h))
        part = slice(*spans[h][i])
        full = ordered(name + ".dots", full)
        if (h, i) == (0, 0):
            gate, up = dot(full, pulled[0]), dot(full, pulled[1])
        else:
            gate, up = dot(full, gate_weight[:, part]), dot(full, up_weight[:, part])
        send = issued(name + ".dots", jnp.stack([gate[half:], up[half:]]).astype(jnp.bfloat16))
        got = issued(name + ".cores_swapped", flip(send, "col", 1))
        yield
        got = ordered(name + ".sum", got)
        gate, up = gate[:half] + got[0], up[:half] + got[1]
        send = issued(name + ".sum", jnp.stack([gate[piece:], up[piece:]]).astype(jnp.bfloat16))
        got = swap_x(send)
        yield
        got = ordered(name + ".hidden", got)
        gate, up = gate[:piece] + got[0], up[:piece] + got[1]
        hidden = issued(name + ".hidden", (jax.nn.silu(gate) * up).astype(jnp.bfloat16))
        whole = yield from spread_steps(name, hidden)
        whole = ordered(name + ".down", whole)
        return issued(name + ".down", dot(whole, down_weight[part]))

    def branch_steps(name, h):
        parts = [result("c" + str(h) + str(i)) for i in range(len(spans[h]))]
        branch = issued(name + ".branch", sum(parts[1:], parts[0]))
        got = flip(branch[half:].astype(jnp.bfloat16), "col", 1)
        yield
        total = issued(name + ".total", branch[:half] + ordered(name + ".total", got))
        got = swap_x(total.astype(jnp.bfloat16))
        yield
        got = ordered(name + ".all", got)
        return issued(name + ".all", total + jnp.concatenate([got[piece:], got[:piece]], axis=0))

    chains, results = {"p": pick_steps(), "w": pull_steps()}, {}
    for h in range(HALVES):
        chains["t" + str(h)] = half_steps("t" + str(h), h)
        for i in range(len(spans[h])):
            chains["c" + str(h) + str(i)] = chunk_steps("c" + str(h) + str(i), h, i)
        chains["b" + str(h)] = branch_steps("b" + str(h), h)

    def advance(name):
        try:
            next(chains[name])
        except StopIteration as stop:
            results[name] = stop.value

    def result(name):
        while name not in results:
            advance(name)
        return results[name]

    result("p")
    result("w")
    for h in range(HALVES):
        result("b" + str(h))

    total = jnp.concatenate([results["b" + str(h)] for h in range(HALVES)])
    mixed = []
    for place, known in zip(places, (tokens, sibling)):
        put = place[:, None] == jnp.concatenate(mine)[None]
        moved = jnp.dot(put.astype(jnp.float32), total, precision=lax.Precision.HIGHEST)
        handled = jnp.any(put, axis=1)[:, None]
        mixed.append(jnp.where(handled, known.astype(jnp.float32) + moved, 0.0).astype(jnp.bfloat16))
    return mixed[0] + flip(mixed[1], "col", 1)


def general(tokens, lengths, gate_weight, up_weight, down_weight):
    c = lax.axis_index("col")
    slots = tokens.shape[0]
    whole = lax.all_gather(tokens, "row", axis=1, tiled=True)
    whole = lax.all_gather(whole, "col", axis=0, tiled=True)
    depth = gate_weight.shape[0]
    block = lax.dynamic_slice_in_dim(whole, c * depth, depth, axis=1)

    def summed(a, b):
        return lax.psum_scatter(dot(a, b), "col", scatter_dimension=0, tiled=True)

    hidden = (jax.nn.silu(summed(block, gate_weight)) * summed(block, up_weight)).astype(jnp.bfloat16)
    hidden = lax.all_gather(hidden, "row", axis=1, tiled=True)
    hidden = lax.all_gather(hidden, "col", axis=0, tiled=True)
    depth = down_weight.shape[0]
    branch = summed(lax.dynamic_slice_in_dim(hidden, c * depth, depth, axis=1), down_weight)
    valid = jnp.arange(slots, dtype=jnp.int32) < jnp.take(lengths, c)
    total = tokens.astype(jnp.float32) + branch
    return jnp.where(valid[:, None], total, jnp.float32(0.0)).astype(jnp.bfloat16)


def solution(mesh):
    square = mesh.shape["row"] == 4 and mesh.shape["col"] == 4
    in_specs = (
        P(("groups", "col"), "row"),
        P("groups"),
        P("col", "row"),
        P("col", "row"),
        P("col", "row"),
    )
    out_specs = P(("groups", "col"), "row")
    return jax.shard_map(
        stationary if square else general,
        mesh=mesh, in_specs=in_specs, out_specs=out_specs, check_vma=False,
    )
```

```python
import functools

import jax
import jax.numpy as jnp
from jax import lax
from jax.experimental import pallas as pl
from jax.experimental.pallas import tpu as pltpu
from jax.sharding import PartitionSpec as P

HALVES = 2
PARTS = ((14, 14), (18, 10))
EDGES = {
    "w.pull": ["t0.add"],
    "t0.halves": ["w.pull"],
    "t1.pick": ["t0.add"],
    "t1.add": ["t0.halves"],
    "t1.halves": ["t0.columns"],
    "c01.dots": ["c00.dots"],
    "c00.sum": ["c01.dots"],
    "t1.columns": ["c01.sum"],
    "c00.hidden": ["c01.sum"],
    "t1.cores": ["c00.hidden"],
    "c01.hidden": ["c10.dots"],
    "c10.sum": ["c01.hidden"],
    "c11.dots": ["c00.halves"],
    "c00.halves": ["c10.sum"],
    "c10.hidden": ["c11.sum"],
    "c01.halves": ["c11.sum"],
    "c10.halves": ["c11.hidden"],
    "c10.cores": ["b0.all"],
    "c11.cores": ["b0.total"],
}


def dot(a, b):
    return jnp.dot(a, b, preferred_element_type=jnp.float32)


def flip(value, axis, bit):
    count = lax.axis_size(axis)
    return lax.ppermute(value, axis, [(i, i ^ bit) for i in range(count)])


def pull_kernel(first, end, tick_ref, gate_ref, up_ref, gate_here, up_here, sems):
    del tick_ref
    columns = pl.ds(first, end - first)
    copies = [
        pltpu.make_async_copy(source.at[:, columns], here, sems.at[i])
        for i, (source, here) in enumerate(((gate_ref, gate_here), (up_ref, up_here)))
    ]
    for copy in copies:
        copy.start()
    for copy in copies:
        copy.wait()


def pull(gate_weight, up_weight, first, end, tick):
    far = pl.BlockSpec(memory_space=pltpu.HBM)
    near = pl.BlockSpec(memory_space=pltpu.VMEM)
    here = pltpu.VMEM((gate_weight.shape[0], end - first), gate_weight.dtype)
    return pl.pallas_call(
        functools.partial(pull_kernel, first, end),
        in_specs=[pl.BlockSpec(memory_space=pltpu.SMEM), far, far],
        out_specs=[near, near],
        out_shape=[here, here],
        scratch_shapes=[pltpu.SemaphoreType.DMA((2,))],
        compiler_params=pltpu.CompilerParams(
            vmem_limit_bytes=4 * gate_weight.shape[0] * (end - first) + 2**20
        ),
        cost_estimate=pl.CostEstimate(flops=0, bytes_accessed=0, transcendentals=0),
    )(
        tick,
        pltpu.with_memory_space_constraint(gate_weight, pltpu.HBM),
        pltpu.with_memory_space_constraint(up_weight, pltpu.HBM),
    )


def stationary(tokens, lengths, gate_weight, up_weight, down_weight):
    slots, width = tokens.shape
    units = gate_weight.shape[1]
    col_count = lax.axis_size("col")
    c = lax.axis_index("col")
    r = lax.axis_index("row")
    x, k, zh, zl = c // 2, c % 2, r // 2, r % 2
    quarter = slots // 2
    piece = quarter // HALVES
    half = 2 * piece
    spans = []
    for sizes in PARTS:
        ends = [0]
        for size in sizes:
            ends.append(ends[-1] + units * size // sum(sizes))
        spans.append(list(zip(ends[:-1], ends[1:])))

    rows = jnp.arange(lengths.shape[0], dtype=jnp.int32)
    slot = jnp.arange(slots, dtype=jnp.int32)
    places = []
    for row in (c, c ^ 1):
        first = jnp.sum(jnp.where(rows < row, lengths, 0))
        count = jnp.sum(jnp.where(rows == row, lengths, 0))
        places.append(jnp.where(slot < count, slot + first, -1))
    inside = jnp.arange(piece, dtype=jnp.int32)
    mine = [
        jnp.concatenate([inside + quarter * c, inside + quarter * (c ^ 2)]) + h * piece
        for h in range(HALVES)
    ]

    devices = [(i // col_count, i % col_count) for i in range(lax.axis_size("row") * col_count)]

    def move(value, where_to):
        pairs = []
        for i, (row, col) in enumerate(devices):
            to = where_to(row // 2, row % 2, col // 2, col % 2)
            if to is not None:
                to_zh, to_zl, to_x, to_k = to
                pairs.append((i, (to_zh * 2 + to_zl) * col_count + to_x * 2 + to_k))
        return lax.ppermute(value, ("row", "col"), pairs)

    def one_step(value, stay, first_to, second_to):
        first, second = move(value, first_to), move(value, second_to)

        def finish(value):
            return jnp.concatenate(
                [jnp.where(stay, value, first), jnp.where(stay, first, second)], axis=0
            )

        return finish

    def to_cores(value):
        return one_step(
            value,
            zl == k,
            lambda zh, zl, x, k: (zh, 1 - zl, x, k) if k == zl else (zh, zl, x, 1 - k),
            lambda zh, zl, x, k: None if k == zl else (zh, 1 - zl, x, 1 - k),
        )

    sibling = flip(tokens, "col", 1)
    seen = {}

    def ordered(step, value):
        for name in EDGES.get(step, ()):
            while name not in seen:
                advance(name.split(".")[0])
        others = [seen[name] for name in EDGES.get(step, ())]
        return lax.optimization_barrier((value, *others))[0] if others else value

    def issued(step, value):
        seen[step] = value
        return value

    def swap_x(value):
        return flip(value, "col", 2)

    def spread_steps(name, value):
        other = flip(value, "row", 2)
        yield
        other = ordered(name + ".halves", other)
        keep = jnp.where(zh == x, value, other)
        send = issued(name + ".halves", jnp.where(zh == x, other, value))
        got = swap_x(send)
        yield
        got = ordered(name + ".columns", got)
        pair = issued(name + ".columns", jnp.concatenate([keep, got], axis=0))
        finish = to_cores(pair)
        yield
        return issued(name + ".cores", finish(ordered(name + ".cores", pair)))

    def pick_steps(name, h):
        own = mine[h][:, None] == places[0][None]
        sib = mine[h][:, None] == places[1][None]
        rows = dot(own.astype(jnp.bfloat16), tokens)
        rows = rows + dot(ordered(name + ".pick", sib).astype(jnp.bfloat16), sibling)
        rows = issued(name + ".pick", rows.astype(jnp.bfloat16))
        got = swap_x(rows[piece:])
        yield
        return issued(name + ".add", ordered(name + ".add", rows[:piece]) + got)

    pulled = []

    def pull_steps():
        tick = ordered("w.pull", lengths)
        pulled.extend(pull(gate_weight, up_weight, *spans[0][0], tick))
        issued("w.pull", pulled[0])
        return None
        yield

    def half_steps(name, h):
        own = yield from pick_steps(name, h)
        return (yield from spread_steps(name, own))

    def chunk_steps(name, h, i):
        full = result("t" + str(h))
        part = slice(*spans[h][i])
        full = ordered(name + ".dots", full)
        if (h, i) == (0, 0):
            gate, up = dot(full, pulled[0]), dot(full, pulled[1])
        else:
            gate, up = dot(full, gate_weight[:, part]), dot(full, up_weight[:, part])
        send = issued(name + ".dots", jnp.stack([gate[half:], up[half:]]).astype(jnp.bfloat16))
        got = issued(name + ".cores_swapped", flip(send, "col", 1))
        yield
        got = ordered(name + ".sum", got)
        gate, up = gate[:half] + got[0], up[:half] + got[1]
        send = issued(name + ".sum", jnp.stack([gate[piece:], up[piece:]]).astype(jnp.bfloat16))
        got = swap_x(send)
        yield
        got = ordered(name + ".hidden", got)
        gate, up = gate[:piece] + got[0], up[:piece] + got[1]
        hidden = issued(name + ".hidden", (jax.nn.silu(gate) * up).astype(jnp.bfloat16))
        whole = yield from spread_steps(name, hidden)
        whole = ordered(name + ".down", whole)
        return issued(name + ".down", dot(whole, down_weight[part]))

    def branch_steps(name, h):
        parts = [result("c" + str(h) + str(i)) for i in range(len(spans[h]))]
        branch = issued(name + ".branch", sum(parts[1:], parts[0]))
        got = flip(branch[half:].astype(jnp.bfloat16), "col", 1)
        yield
        total = issued(name + ".total", branch[:half] + ordered(name + ".total", got))
        got = swap_x(total.astype(jnp.bfloat16))
        yield
        got = ordered(name + ".all", got)
        return issued(name + ".all", total + jnp.concatenate([got[piece:], got[:piece]], axis=0))

    chains, results = {"w": pull_steps()}, {}
    for h in range(HALVES):
        chains["t" + str(h)] = half_steps("t" + str(h), h)
        for i in range(len(spans[h])):
            chains["c" + str(h) + str(i)] = chunk_steps("c" + str(h) + str(i), h, i)
        chains["b" + str(h)] = branch_steps("b" + str(h), h)

    def advance(name):
        try:
            next(chains[name])
        except StopIteration as stop:
            results[name] = stop.value

    def result(name):
        while name not in results:
            advance(name)
        return results[name]

    result("w")
    for h in range(HALVES):
        result("b" + str(h))

    total = jnp.concatenate([results["b" + str(h)] for h in range(HALVES)])
    mixed = []
    for place, known in zip(places, (tokens, sibling)):
        put = place[:, None] == jnp.concatenate(mine)[None]
        moved = jnp.dot(put.astype(jnp.float32), total, precision=lax.Precision.HIGHEST)
        handled = jnp.any(put, axis=1)[:, None]
        mixed.append(jnp.where(handled, known.astype(jnp.float32) + moved, 0.0).astype(jnp.bfloat16))
    return mixed[0] + flip(mixed[1], "col", 1)


def general(tokens, lengths, gate_weight, up_weight, down_weight):
    c = lax.axis_index("col")
    slots = tokens.shape[0]
    whole = lax.all_gather(tokens, "row", axis=1, tiled=True)
    whole = lax.all_gather(whole, "col", axis=0, tiled=True)
    depth = gate_weight.shape[0]
    block = lax.dynamic_slice_in_dim(whole, c * depth, depth, axis=1)

    def summed(a, b):
        return lax.psum_scatter(dot(a, b), "col", scatter_dimension=0, tiled=True)

    hidden = (jax.nn.silu(summed(block, gate_weight)) * summed(block, up_weight)).astype(jnp.bfloat16)
    hidden = lax.all_gather(hidden, "row", axis=1, tiled=True)
    hidden = lax.all_gather(hidden, "col", axis=0, tiled=True)
    depth = down_weight.shape[0]
    branch = summed(lax.dynamic_slice_in_dim(hidden, c * depth, depth, axis=1), down_weight)
    valid = jnp.arange(slots, dtype=jnp.int32) < jnp.take(lengths, c)
    total = tokens.astype(jnp.float32) + branch
    return jnp.where(valid[:, None], total, jnp.float32(0.0)).astype(jnp.bfloat16)


def solution(mesh):
    square = mesh.shape["row"] == 4 and mesh.shape["col"] == 4
    in_specs = (
        P(("groups", "col"), "row"),
        P("groups"),
        P("col", "row"),
        P("col", "row"),
        P("col", "row"),
    )
    out_specs = P(("groups", "col"), "row")
    return jax.shard_map(
        stationary if square else general,
        mesh=mesh, in_specs=in_specs, out_specs=out_specs, check_vma=False,
    )
```

```python
import jax
import jax.numpy as jnp
from jax import lax
from jax.experimental import pallas as pl
from jax.experimental.pallas import tpu as pltpu
from jax.sharding import PartitionSpec as P

HALVES = 2
PARTS = ((14, 14), (18, 10))
EDGES = {
    "g.pull": ["t0.add"],
    "t0.halves": ["g.pull"],
    "u.pull": ["t0.columns"],
    "t0.cores": ["u.pull"],
    "t1.pick": ["t0.add"],
    "t1.add": ["t0.halves"],
    "t1.halves": ["t0.columns"],
    "c01.dots": ["c00.dots"],
    "c00.sum": ["c01.dots"],
    "t1.columns": ["c01.sum"],
    "c00.hidden": ["c01.sum"],
    "t1.cores": ["c00.hidden"],
    "c01.hidden": ["c10.dots"],
    "c10.sum": ["c01.hidden"],
    "c11.dots": ["c10.sum"],
    "c00.halves": ["c10.sum"],
    "c10.hidden": ["c11.sum"],
    "c01.halves": ["c11.sum"],
    "c10.halves": ["c11.hidden"],
    "c01.cores": ["c10.columns", "c11.columns"],
    "c00.down": ["c01.cores"],
    "c10.cores": ["b0.all"],
    "c11.cores": ["b0.total"],
}


def dot(a, b):
    return jnp.dot(a, b, preferred_element_type=jnp.float32)


def flip(value, axis, bit):
    count = lax.axis_size(axis)
    return lax.ppermute(value, axis, [(i, i ^ bit) for i in range(count)])


def pull_kernel(tick_ref, weight_ref, here_ref, sem):
    del tick_ref
    copy = pltpu.make_async_copy(weight_ref, here_ref, sem)
    copy.start()
    copy.wait()


def pull(weight, tick):
    return pl.pallas_call(
        pull_kernel,
        in_specs=[
            pl.BlockSpec(memory_space=pltpu.SMEM),
            pl.BlockSpec(memory_space=pltpu.HBM),
        ],
        out_specs=pl.BlockSpec(memory_space=pltpu.VMEM),
        out_shape=pltpu.VMEM(weight.shape, weight.dtype),
        scratch_shapes=[pltpu.SemaphoreType.DMA],
        compiler_params=pltpu.CompilerParams(vmem_limit_bytes=2 * weight.size + 2**20),
        cost_estimate=pl.CostEstimate(flops=0, bytes_accessed=0, transcendentals=0),
    )(tick, pltpu.with_memory_space_constraint(weight, pltpu.HBM))


def stationary(tokens, lengths, gate_weight, up_weight, down_weight):
    slots, width = tokens.shape
    units = gate_weight.shape[1]
    col_count = lax.axis_size("col")
    c = lax.axis_index("col")
    r = lax.axis_index("row")
    x, k, zh, zl = c // 2, c % 2, r // 2, r % 2
    quarter = slots // 2
    piece = quarter // HALVES
    half = 2 * piece
    spans = []
    for sizes in PARTS:
        ends = [0]
        for size in sizes:
            ends.append(ends[-1] + units * size // sum(sizes))
        spans.append(list(zip(ends[:-1], ends[1:])))

    rows = jnp.arange(lengths.shape[0], dtype=jnp.int32)
    slot = jnp.arange(slots, dtype=jnp.int32)
    places = []
    for row in (c, c ^ 1):
        first = jnp.sum(jnp.where(rows < row, lengths, 0))
        count = jnp.sum(jnp.where(rows == row, lengths, 0))
        places.append(jnp.where(slot < count, slot + first, -1))
    inside = jnp.arange(piece, dtype=jnp.int32)
    mine = [
        jnp.concatenate([inside + quarter * c, inside + quarter * (c ^ 2)]) + h * piece
        for h in range(HALVES)
    ]

    devices = [(i // col_count, i % col_count) for i in range(lax.axis_size("row") * col_count)]

    def move(value, where_to):
        pairs = []
        for i, (row, col) in enumerate(devices):
            to = where_to(row // 2, row % 2, col // 2, col % 2)
            if to is not None:
                to_zh, to_zl, to_x, to_k = to
                pairs.append((i, (to_zh * 2 + to_zl) * col_count + to_x * 2 + to_k))
        return lax.ppermute(value, ("row", "col"), pairs)

    def one_step(value, stay, first_to, second_to):
        first, second = move(value, first_to), move(value, second_to)

        def finish(value):
            return jnp.concatenate(
                [jnp.where(stay, value, first), jnp.where(stay, first, second)], axis=0
            )

        return finish

    def to_cores(value):
        return one_step(
            value,
            zl == k,
            lambda zh, zl, x, k: (zh, 1 - zl, x, k) if k == zl else (zh, zl, x, 1 - k),
            lambda zh, zl, x, k: None if k == zl else (zh, 1 - zl, x, 1 - k),
        )

    sibling = flip(tokens, "col", 1)
    seen = {}

    def ordered(step, value):
        for name in EDGES.get(step, ()):
            while name not in seen:
                advance(name.split(".")[0])
        others = [seen[name] for name in EDGES.get(step, ())]
        return lax.optimization_barrier((value, *others))[0] if others else value

    def issued(step, value):
        seen[step] = value
        return value

    def swap_x(value):
        return flip(value, "col", 2)

    def spread_steps(name, value):
        other = flip(value, "row", 2)
        yield
        other = ordered(name + ".halves", other)
        keep = jnp.where(zh == x, value, other)
        send = issued(name + ".halves", jnp.where(zh == x, other, value))
        got = swap_x(send)
        yield
        got = ordered(name + ".columns", got)
        pair = issued(name + ".columns", jnp.concatenate([keep, got], axis=0))
        finish = to_cores(pair)
        yield
        return issued(name + ".cores", finish(ordered(name + ".cores", pair)))

    def pick_steps(name, h):
        own = mine[h][:, None] == places[0][None]
        sib = mine[h][:, None] == places[1][None]
        rows = dot(own.astype(jnp.bfloat16), tokens)
        rows = rows + dot(ordered(name + ".pick", sib).astype(jnp.bfloat16), sibling)
        rows = issued(name + ".pick", rows.astype(jnp.bfloat16))
        got = swap_x(rows[piece:])
        yield
        return issued(name + ".add", ordered(name + ".add", rows[:piece]) + got)

    pulled = {}

    def pull_steps(name, weight):
        pulled[name] = issued(name + ".pull", pull(weight, ordered(name + ".pull", lengths)))
        return None
        yield

    def half_steps(name, h):
        own = yield from pick_steps(name, h)
        return (yield from spread_steps(name, own))

    def chunk_steps(name, h, i):
        full = result("t" + str(h))
        part = slice(*spans[h][i])
        full = ordered(name + ".dots", full)
        result("g")
        result("u")
        gate, up = dot(full, pulled["g"][:, part]), dot(full, pulled["u"][:, part])
        send = issued(name + ".dots", jnp.stack([gate[half:], up[half:]]).astype(jnp.bfloat16))
        got = issued(name + ".cores_swapped", flip(send, "col", 1))
        yield
        got = ordered(name + ".sum", got)
        gate, up = gate[:half] + got[0], up[:half] + got[1]
        send = issued(name + ".sum", jnp.stack([gate[piece:], up[piece:]]).astype(jnp.bfloat16))
        got = swap_x(send)
        yield
        got = ordered(name + ".hidden", got)
        gate, up = gate[:piece] + got[0], up[:piece] + got[1]
        hidden = issued(name + ".hidden", (jax.nn.silu(gate) * up).astype(jnp.bfloat16))
        whole = yield from spread_steps(name, hidden)
        whole = ordered(name + ".down", whole)
        return issued(name + ".down", dot(whole, down_weight[part]))

    def branch_steps(name, h):
        parts = [result("c" + str(h) + str(i)) for i in range(len(spans[h]))]
        branch = issued(name + ".branch", sum(parts[1:], parts[0]))
        got = flip(branch[half:].astype(jnp.bfloat16), "col", 1)
        yield
        total = issued(name + ".total", branch[:half] + ordered(name + ".total", got))
        got = swap_x(total.astype(jnp.bfloat16))
        yield
        got = ordered(name + ".all", got)
        return issued(name + ".all", total + jnp.concatenate([got[piece:], got[:piece]], axis=0))

    chains = {"g": pull_steps("g", gate_weight), "u": pull_steps("u", up_weight)}
    results = {}
    for h in range(HALVES):
        chains["t" + str(h)] = half_steps("t" + str(h), h)
        for i in range(len(spans[h])):
            chains["c" + str(h) + str(i)] = chunk_steps("c" + str(h) + str(i), h, i)
        chains["b" + str(h)] = branch_steps("b" + str(h), h)

    def advance(name):
        try:
            next(chains[name])
        except StopIteration as stop:
            results[name] = stop.value

    def result(name):
        while name not in results:
            advance(name)
        return results[name]

    for h in range(HALVES):
        result("b" + str(h))

    total = jnp.concatenate([results["b" + str(h)] for h in range(HALVES)])
    mixed = []
    for place, known in zip(places, (tokens, sibling)):
        put = place[:, None] == jnp.concatenate(mine)[None]
        moved = jnp.dot(put.astype(jnp.float32), total, precision=lax.Precision.HIGHEST)
        handled = jnp.any(put, axis=1)[:, None]
        mixed.append(jnp.where(handled, known.astype(jnp.float32) + moved, 0.0).astype(jnp.bfloat16))
    return mixed[0] + flip(mixed[1], "col", 1)


def general(tokens, lengths, gate_weight, up_weight, down_weight):
    c = lax.axis_index("col")
    slots = tokens.shape[0]
    whole = lax.all_gather(tokens, "row", axis=1, tiled=True)
    whole = lax.all_gather(whole, "col", axis=0, tiled=True)
    depth = gate_weight.shape[0]
    block = lax.dynamic_slice_in_dim(whole, c * depth, depth, axis=1)

    def summed(a, b):
        return lax.psum_scatter(dot(a, b), "col", scatter_dimension=0, tiled=True)

    hidden = (jax.nn.silu(summed(block, gate_weight)) * summed(block, up_weight)).astype(jnp.bfloat16)
    hidden = lax.all_gather(hidden, "row", axis=1, tiled=True)
    hidden = lax.all_gather(hidden, "col", axis=0, tiled=True)
    depth = down_weight.shape[0]
    branch = summed(lax.dynamic_slice_in_dim(hidden, c * depth, depth, axis=1), down_weight)
    valid = jnp.arange(slots, dtype=jnp.int32) < jnp.take(lengths, c)
    total = tokens.astype(jnp.float32) + branch
    return jnp.where(valid[:, None], total, jnp.float32(0.0)).astype(jnp.bfloat16)


def solution(mesh):
    square = mesh.shape["row"] == 4 and mesh.shape["col"] == 4
    in_specs = (
        P(("groups", "col"), "row"),
        P("groups"),
        P("col", "row"),
        P("col", "row"),
        P("col", "row"),
    )
    out_specs = P(("groups", "col"), "row")
    return jax.shard_map(
        stationary if square else general,
        mesh=mesh, in_specs=in_specs, out_specs=out_specs, check_vma=False,
    )
```

```python
import jax
import jax.numpy as jnp
from jax import lax
from jax.experimental import pallas as pl
from jax.experimental.pallas import tpu as pltpu
from jax.sharding import PartitionSpec as P

HALVES = 2
PARTS = ((14, 14), (18, 10))
EDGES = {
    "u.pull": ["t0.columns"],
    "t0.cores": ["u.pull"],
    "t1.add": ["t0.halves"],
    "t1.halves": ["t0.cores"],
    "c01.dots": ["c00.dots"],
    "c00.sum": ["c01.dots"],
    "t1.columns": ["c01.sum"],
    "c00.hidden": ["c01.sum"],
    "t1.cores": ["c00.hidden"],
    "c11.dots": ["c10.dots"],
    "c01.hidden": ["c11.dots"],
    "c10.sum": ["c01.hidden"],
    "c00.halves": ["c10.sum"],
    "c11.sum": ["c00.halves"],
    "c01.halves": ["c11.sum"],
    "c00.columns": ["c01.halves"],
    "c10.hidden": ["c00.columns"],
    "c01.columns": ["c10.hidden"],
    "c11.hidden": ["c01.columns"],
    "c10.halves": ["c11.hidden"],
    "c00.cores": ["c10.halves"],
    "c11.halves": ["c00.cores"],
    "c01.cores": ["c10.columns"],
    "c00.down": ["c01.cores"],
    "c10.cores": ["b0.all"],
    "c11.cores": ["b0.total"],
}


def dot(a, b):
    return jnp.dot(a, b, preferred_element_type=jnp.float32)


def flip(value, axis, bit):
    count = lax.axis_size(axis)
    return lax.ppermute(value, axis, [(i, i ^ bit) for i in range(count)])


def pull_kernel(tick_ref, weight_ref, here_ref, sem):
    del tick_ref
    copy = pltpu.make_async_copy(weight_ref, here_ref, sem)
    copy.start()
    copy.wait()


def pull(weight, tick):
    return pl.pallas_call(
        pull_kernel,
        in_specs=[
            pl.BlockSpec(memory_space=pltpu.SMEM),
            pl.BlockSpec(memory_space=pltpu.HBM),
        ],
        out_specs=pl.BlockSpec(memory_space=pltpu.VMEM),
        out_shape=pltpu.VMEM(weight.shape, weight.dtype),
        scratch_shapes=[pltpu.SemaphoreType.DMA],
        compiler_params=pltpu.CompilerParams(vmem_limit_bytes=2 * weight.size + 2**20),
        cost_estimate=pl.CostEstimate(flops=0, bytes_accessed=0, transcendentals=0),
    )(tick, pltpu.with_memory_space_constraint(weight, pltpu.HBM))


def stationary(tokens, lengths, gate_weight, up_weight, down_weight):
    slots, width = tokens.shape
    units = gate_weight.shape[1]
    col_count = lax.axis_size("col")
    c = lax.axis_index("col")
    r = lax.axis_index("row")
    x, k, zh, zl = c // 2, c % 2, r // 2, r % 2
    quarter = slots // 2
    piece = quarter // HALVES
    half = 2 * piece
    spans = []
    for sizes in PARTS:
        ends = [0]
        for size in sizes:
            ends.append(ends[-1] + units * size // sum(sizes))
        spans.append(list(zip(ends[:-1], ends[1:])))

    rows = jnp.arange(lengths.shape[0], dtype=jnp.int32)[None]
    slot = jnp.arange(slots, dtype=jnp.int32)[None]
    here = (c ^ jnp.arange(2, dtype=jnp.int32))[:, None]
    first = jnp.sum(jnp.where(rows < here, lengths[None], 0), axis=1, keepdims=True)
    count = jnp.sum(jnp.where(rows == here, lengths[None], 0), axis=1, keepdims=True)
    places = jnp.where(slot < count, slot + first, -1)
    inside = jnp.arange(piece, dtype=jnp.int32)
    mine = [
        jnp.concatenate([inside + quarter * c, inside + quarter * (c ^ 2)]) + h * piece
        for h in range(HALVES)
    ]

    devices = [(i // col_count, i % col_count) for i in range(lax.axis_size("row") * col_count)]

    def move(value, where_to):
        pairs = []
        for i, (row, col) in enumerate(devices):
            to = where_to(row // 2, row % 2, col // 2, col % 2)
            if to is not None:
                to_zh, to_zl, to_x, to_k = to
                pairs.append((i, (to_zh * 2 + to_zl) * col_count + to_x * 2 + to_k))
        return lax.ppermute(value, ("row", "col"), pairs)

    def one_step(value, stay, first_to, second_to):
        first, second = move(value, first_to), move(value, second_to)

        def finish(value):
            return jnp.concatenate(
                [jnp.where(stay, value, first), jnp.where(stay, first, second)], axis=0
            )

        return finish

    def to_cores(value):
        return one_step(
            value,
            zl == k,
            lambda zh, zl, x, k: (zh, 1 - zl, x, k) if k == zl else (zh, zl, x, 1 - k),
            lambda zh, zl, x, k: None if k == zl else (zh, 1 - zl, x, 1 - k),
        )

    sibling = flip(tokens, "col", 1)
    seen = {}

    def ordered(step, value):
        for name in EDGES.get(step, ()):
            while name not in seen:
                advance(name.split(".")[0])
        others = [seen[name] for name in EDGES.get(step, ())]
        return lax.optimization_barrier((value, *others))[0] if others else value

    def issued(step, value):
        seen[step] = value
        return value

    def swap_x(value):
        return flip(value, "col", 2)

    def spread_steps(name, value):
        other = flip(value, "row", 2)
        yield
        other = ordered(name + ".halves", other)
        keep = jnp.where(zh == x, value, other)
        send = issued(name + ".halves", jnp.where(zh == x, other, value))
        got = swap_x(send)
        yield
        got = ordered(name + ".columns", got)
        pair = issued(name + ".columns", jnp.concatenate([keep, got], axis=0))
        finish = to_cores(pair)
        yield
        return issued(name + ".cores", finish(ordered(name + ".cores", pair)))

    picked = {}

    def pick_steps():
        own = jnp.concatenate(mine)[:, None] == places[0][None]
        sib = jnp.concatenate(mine)[:, None] == places[1][None]
        rows = dot(own.astype(jnp.bfloat16), tokens) + dot(sib.astype(jnp.bfloat16), sibling)
        rows = rows.astype(jnp.bfloat16).reshape(HALVES, 2, piece, width)
        picked["got"] = swap_x(rows[:, 1])
        picked["rows"] = rows[:, 0]
        return None
        yield

    pulled = {}

    def pull_steps(name, weight):
        pulled[name] = issued(name + ".pull", pull(weight, ordered(name + ".pull", lengths)))
        return None
        yield

    def half_steps(name, h):
        own = issued(name + ".add", ordered(name + ".add", picked["rows"][h]) + picked["got"][h])
        return (yield from spread_steps(name, own))

    def chunk_steps(name, h, i):
        full = result("t" + str(h))
        part = slice(*spans[h][i])
        full = ordered(name + ".dots", full)
        result("u")
        gate, up = dot(full, gate_weight[:, part]), dot(full, pulled["u"][:, part])
        send = issued(name + ".dots", jnp.stack([gate[half:], up[half:]]).astype(jnp.bfloat16))
        got = issued(name + ".cores_swapped", flip(send, "col", 1))
        yield
        got = ordered(name + ".sum", got)
        gate, up = gate[:half] + got[0], up[:half] + got[1]
        send = issued(name + ".sum", jnp.stack([gate[piece:], up[piece:]]).astype(jnp.bfloat16))
        got = swap_x(send)
        yield
        got = ordered(name + ".hidden", got)
        gate, up = gate[:piece] + got[0], up[:piece] + got[1]
        hidden = issued(name + ".hidden", (jax.nn.silu(gate) * up).astype(jnp.bfloat16))
        whole = yield from spread_steps(name, hidden)
        whole = ordered(name + ".down", whole)
        return issued(name + ".down", dot(whole, down_weight[part]))

    def branch_steps(name, h):
        parts = [result("c" + str(h) + str(i)) for i in range(len(spans[h]))]
        branch = issued(name + ".branch", sum(parts[1:], parts[0]))
        got = flip(branch[half:].astype(jnp.bfloat16), "col", 1)
        yield
        total = issued(name + ".total", branch[:half] + ordered(name + ".total", got))
        got = swap_x(total.astype(jnp.bfloat16))
        yield
        got = ordered(name + ".all", got)
        return issued(name + ".all", total + jnp.concatenate([got[piece:], got[:piece]], axis=0))

    chains = {"p": pick_steps(), "u": pull_steps("u", up_weight)}
    results = {}
    for h in range(HALVES):
        chains["t" + str(h)] = half_steps("t" + str(h), h)
        for i in range(len(spans[h])):
            chains["c" + str(h) + str(i)] = chunk_steps("c" + str(h) + str(i), h, i)
        chains["b" + str(h)] = branch_steps("b" + str(h), h)

    def advance(name):
        try:
            next(chains[name])
        except StopIteration as stop:
            results[name] = stop.value

    def result(name):
        while name not in results:
            advance(name)
        return results[name]

    result("p")
    for h in range(HALVES):
        result("b" + str(h))

    total = jnp.concatenate([results["b" + str(h)] for h in range(HALVES)])
    mixed = []
    for place, known in zip(places, (tokens, sibling)):
        put = place[:, None] == jnp.concatenate(mine)[None]
        moved = jnp.dot(put.astype(jnp.float32), total, precision=lax.Precision.HIGHEST)
        handled = jnp.any(put, axis=1)[:, None]
        mixed.append(jnp.where(handled, known.astype(jnp.float32) + moved, 0.0).astype(jnp.bfloat16))
    return mixed[0] + flip(mixed[1], "col", 1)


def general(tokens, lengths, gate_weight, up_weight, down_weight):
    c = lax.axis_index("col")
    slots = tokens.shape[0]
    whole = lax.all_gather(tokens, "row", axis=1, tiled=True)
    whole = lax.all_gather(whole, "col", axis=0, tiled=True)
    depth = gate_weight.shape[0]
    block = lax.dynamic_slice_in_dim(whole, c * depth, depth, axis=1)

    def summed(a, b):
        return lax.psum_scatter(dot(a, b), "col", scatter_dimension=0, tiled=True)

    hidden = (jax.nn.silu(summed(block, gate_weight)) * summed(block, up_weight)).astype(jnp.bfloat16)
    hidden = lax.all_gather(hidden, "row", axis=1, tiled=True)
    hidden = lax.all_gather(hidden, "col", axis=0, tiled=True)
    depth = down_weight.shape[0]
    branch = summed(lax.dynamic_slice_in_dim(hidden, c * depth, depth, axis=1), down_weight)
    valid = jnp.arange(slots, dtype=jnp.int32) < jnp.take(lengths, c)
    total = tokens.astype(jnp.float32) + branch
    return jnp.where(valid[:, None], total, jnp.float32(0.0)).astype(jnp.bfloat16)


def solution(mesh):
    square = mesh.shape["row"] == 4 and mesh.shape["col"] == 4
    in_specs = (
        P(("groups", "col"), "row"),
        P("groups"),
        P("col", "row"),
        P("col", "row"),
        P("col", "row"),
    )
    out_specs = P(("groups", "col"), "row")
    return jax.shard_map(
        stationary if square else general,
        mesh=mesh, in_specs=in_specs, out_specs=out_specs, check_vma=False,
    )
```

```python
import functools

import jax
import jax.numpy as jnp
from jax import lax
from jax.experimental import pallas as pl
from jax.experimental.pallas import tpu as pltpu
from jax.sharding import PartitionSpec as P

HALVES = 2
PARTS = ((14, 14), (18, 10))
EDGES = {
    "w.pull": ["t0.columns"],
    "t1.add": ["t0.halves"],
    "t1.halves": ["t0.columns"],
    "c00.dots": ["t1.columns"],
    "c01.dots": ["c00.dots"],
    "c00.sum": ["c01.dots"],
    "c00.hidden": ["c01.sum"],
    "t1.cores": ["c00.hidden"],
    "c11.dots": ["c10.dots"],
    "c01.hidden": ["c11.dots"],
    "c10.sum": ["c01.hidden"],
    "c00.halves": ["c10.sum"],
    "c11.sum": ["c00.halves"],
    "c01.halves": ["c11.sum"],
    "c00.columns": ["c01.halves"],
    "c10.hidden": ["c00.columns"],
    "c01.columns": ["c10.hidden"],
    "c11.hidden": ["c01.columns"],
    "c10.halves": ["c11.hidden"],
    "c00.cores": ["c10.halves"],
    "c01.cores": ["c10.halves"],
    "c11.halves": ["c01.down"],
    "b0.total": ["c11.halves"],
    "c10.cores": ["b0.all"],
    "c11.cores": ["b0.total"],
}


def dot(a, b):
    return jnp.dot(a, b, preferred_element_type=jnp.float32)


def flip(value, axis, bit):
    count = lax.axis_size(axis)
    return lax.ppermute(value, axis, [(i, i ^ bit) for i in range(count)])


def pull_kernel(first, end, tick_ref, gate_ref, up_ref, gate_here, up_here, sems):
    del tick_ref
    columns = pl.ds(first, end - first)
    copies = [
        pltpu.make_async_copy(source.at[:, columns], here, sems.at[i])
        for i, (source, here) in enumerate(((gate_ref, gate_here), (up_ref, up_here)))
    ]
    for copy in copies:
        copy.start()
    for copy in copies:
        copy.wait()


def pull(gate_weight, up_weight, first, end, tick):
    far = pl.BlockSpec(memory_space=pltpu.HBM)
    near = pl.BlockSpec(memory_space=pltpu.VMEM)
    here = pltpu.VMEM((gate_weight.shape[0], end - first), gate_weight.dtype)
    return pl.pallas_call(
        functools.partial(pull_kernel, first, end),
        in_specs=[pl.BlockSpec(memory_space=pltpu.SMEM), far, far],
        out_specs=[near, near],
        out_shape=[here, here],
        scratch_shapes=[pltpu.SemaphoreType.DMA((2,))],
        compiler_params=pltpu.CompilerParams(
            vmem_limit_bytes=4 * gate_weight.shape[0] * (end - first) + 2**20
        ),
        cost_estimate=pl.CostEstimate(flops=0, bytes_accessed=0, transcendentals=0),
    )(
        tick,
        pltpu.with_memory_space_constraint(gate_weight, pltpu.HBM),
        pltpu.with_memory_space_constraint(up_weight, pltpu.HBM),
    )


def stationary(tokens, lengths, gate_weight, up_weight, down_weight):
    slots, width = tokens.shape
    units = gate_weight.shape[1]
    col_count = lax.axis_size("col")
    c = lax.axis_index("col")
    r = lax.axis_index("row")
    x, k, zh, zl = c // 2, c % 2, r // 2, r % 2
    quarter = slots // 2
    piece = quarter // HALVES
    half = 2 * piece
    spans = []
    for sizes in PARTS:
        ends = [0]
        for size in sizes:
            ends.append(ends[-1] + units * size // sum(sizes))
        spans.append(list(zip(ends[:-1], ends[1:])))

    rows = jnp.arange(lengths.shape[0], dtype=jnp.int32)[None]
    slot = jnp.arange(slots, dtype=jnp.int32)[None]
    here = (c ^ jnp.arange(2, dtype=jnp.int32))[:, None]
    first = jnp.sum(jnp.where(rows < here, lengths[None], 0), axis=1, keepdims=True)
    count = jnp.sum(jnp.where(rows == here, lengths[None], 0), axis=1, keepdims=True)
    places = jnp.where(slot < count, slot + first, -1)
    inside = jnp.arange(piece, dtype=jnp.int32)
    mine = [
        jnp.concatenate([inside + quarter * c, inside + quarter * (c ^ 2)]) + h * piece
        for h in range(HALVES)
    ]

    devices = [(i // col_count, i % col_count) for i in range(lax.axis_size("row") * col_count)]

    def move(value, where_to):
        pairs = []
        for i, (row, col) in enumerate(devices):
            to = where_to(row // 2, row % 2, col // 2, col % 2)
            if to is not None:
                to_zh, to_zl, to_x, to_k = to
                pairs.append((i, (to_zh * 2 + to_zl) * col_count + to_x * 2 + to_k))
        return lax.ppermute(value, ("row", "col"), pairs)

    def one_step(value, stay, first_to, second_to):
        first, second = move(value, first_to), move(value, second_to)

        def finish(value):
            return jnp.concatenate(
                [jnp.where(stay, value, first), jnp.where(stay, first, second)], axis=0
            )

        return finish

    def to_cores(value):
        return one_step(
            value,
            zl == k,
            lambda zh, zl, x, k: (zh, 1 - zl, x, k) if k == zl else (zh, zl, x, 1 - k),
            lambda zh, zl, x, k: None if k == zl else (zh, 1 - zl, x, 1 - k),
        )

    sibling = flip(tokens, "col", 1)
    seen = {}

    def ordered(step, value):
        for name in EDGES.get(step, ()):
            while name not in seen:
                advance(name.split(".")[0])
        others = [seen[name] for name in EDGES.get(step, ())]
        return lax.optimization_barrier((value, *others))[0] if others else value

    def issued(step, value):
        seen[step] = value
        return value

    def swap_x(value):
        return flip(value, "col", 2)

    def spread_steps(name, value):
        other = flip(value, "row", 2)
        yield
        other = ordered(name + ".halves", other)
        keep = jnp.where(zh == x, value, other)
        send = issued(name + ".halves", jnp.where(zh == x, other, value))
        got = swap_x(send)
        yield
        got = ordered(name + ".columns", got)
        pair = issued(name + ".columns", jnp.concatenate([keep, got], axis=0))
        finish = to_cores(pair)
        yield
        return issued(name + ".cores", finish(ordered(name + ".cores", pair)))

    picked = {}

    def pick_steps():
        own = jnp.concatenate(mine)[:, None] == places[0][None]
        sib = jnp.concatenate(mine)[:, None] == places[1][None]
        rows = dot(own.astype(jnp.bfloat16), tokens) + dot(sib.astype(jnp.bfloat16), sibling)
        rows = rows.astype(jnp.bfloat16).reshape(HALVES, 2, piece, width)
        picked["got"] = swap_x(rows[:, 1])
        picked["rows"] = rows[:, 0]
        return None
        yield

    pulled = []

    def pull_steps():
        tick = ordered("w.pull", lengths)
        pulled.extend(pull(gate_weight, up_weight, *spans[0][0], tick))
        issued("w.pull", pulled[0])
        return None
        yield

    def half_steps(name, h):
        own = issued(name + ".add", ordered(name + ".add", picked["rows"][h]) + picked["got"][h])
        return (yield from spread_steps(name, own))

    def chunk_steps(name, h, i):
        full = result("t" + str(h))
        part = slice(*spans[h][i])
        full = ordered(name + ".dots", full)
        if (h, i) == (0, 0):
            result("w")
            gate, up = dot(full, pulled[0]), dot(full, pulled[1])
        else:
            gate, up = dot(full, gate_weight[:, part]), dot(full, up_weight[:, part])
        send = issued(name + ".dots", jnp.stack([gate[half:], up[half:]]).astype(jnp.bfloat16))
        got = issued(name + ".cores_swapped", flip(send, "col", 1))
        yield
        got = ordered(name + ".sum", got)
        gate, up = gate[:half] + got[0], up[:half] + got[1]
        send = issued(name + ".sum", jnp.stack([gate[piece:], up[piece:]]).astype(jnp.bfloat16))
        got = swap_x(send)
        yield
        got = ordered(name + ".hidden", got)
        gate, up = gate[:piece] + got[0], up[:piece] + got[1]
        hidden = issued(name + ".hidden", (jax.nn.silu(gate) * up).astype(jnp.bfloat16))
        whole = yield from spread_steps(name, hidden)
        whole = ordered(name + ".down", whole)
        return issued(name + ".down", dot(whole, down_weight[part]))

    def branch_steps(name, h):
        parts = [result("c" + str(h) + str(i)) for i in range(len(spans[h]))]
        branch = issued(name + ".branch", sum(parts[1:], parts[0]))
        got = flip(branch[half:].astype(jnp.bfloat16), "col", 1)
        yield
        total = issued(name + ".total", branch[:half] + ordered(name + ".total", got))
        got = swap_x(total.astype(jnp.bfloat16))
        yield
        got = ordered(name + ".all", got)
        return issued(name + ".all", total + jnp.concatenate([got[piece:], got[:piece]], axis=0))

    chains = {"p": pick_steps(), "w": pull_steps()}
    results = {}
    for h in range(HALVES):
        chains["t" + str(h)] = half_steps("t" + str(h), h)
        for i in range(len(spans[h])):
            chains["c" + str(h) + str(i)] = chunk_steps("c" + str(h) + str(i), h, i)
        chains["b" + str(h)] = branch_steps("b" + str(h), h)

    def advance(name):
        try:
            next(chains[name])
        except StopIteration as stop:
            results[name] = stop.value

    def result(name):
        while name not in results:
            advance(name)
        return results[name]

    result("p")
    for h in range(HALVES):
        result("b" + str(h))

    total = jnp.concatenate([results["b" + str(h)] for h in range(HALVES)])
    mixed = []
    for place, known in zip(places, (tokens, sibling)):
        put = place[:, None] == jnp.concatenate(mine)[None]
        moved = jnp.dot(put.astype(jnp.float32), total, precision=lax.Precision.HIGHEST)
        handled = jnp.any(put, axis=1)[:, None]
        mixed.append(jnp.where(handled, known.astype(jnp.float32) + moved, 0.0).astype(jnp.bfloat16))
    return mixed[0] + flip(mixed[1], "col", 1)


def general(tokens, lengths, gate_weight, up_weight, down_weight):
    c = lax.axis_index("col")
    slots = tokens.shape[0]
    whole = lax.all_gather(tokens, "row", axis=1, tiled=True)
    whole = lax.all_gather(whole, "col", axis=0, tiled=True)
    depth = gate_weight.shape[0]
    block = lax.dynamic_slice_in_dim(whole, c * depth, depth, axis=1)

    def summed(a, b):
        return lax.psum_scatter(dot(a, b), "col", scatter_dimension=0, tiled=True)

    hidden = (jax.nn.silu(summed(block, gate_weight)) * summed(block, up_weight)).astype(jnp.bfloat16)
    hidden = lax.all_gather(hidden, "row", axis=1, tiled=True)
    hidden = lax.all_gather(hidden, "col", axis=0, tiled=True)
    depth = down_weight.shape[0]
    branch = summed(lax.dynamic_slice_in_dim(hidden, c * depth, depth, axis=1), down_weight)
    valid = jnp.arange(slots, dtype=jnp.int32) < jnp.take(lengths, c)
    total = tokens.astype(jnp.float32) + branch
    return jnp.where(valid[:, None], total, jnp.float32(0.0)).astype(jnp.bfloat16)


def solution(mesh):
    square = mesh.shape["row"] == 4 and mesh.shape["col"] == 4
    in_specs = (
        P(("groups", "col"), "row"),
        P("groups"),
        P("col", "row"),
        P("col", "row"),
        P("col", "row"),
    )
    out_specs = P(("groups", "col"), "row")
    return jax.shard_map(
        stationary if square else general,
        mesh=mesh, in_specs=in_specs, out_specs=out_specs, check_vma=False,
    )
```

```python
import functools

import jax
import jax.numpy as jnp
from jax import lax
from jax.experimental import pallas as pl
from jax.experimental.pallas import tpu as pltpu
from jax.sharding import PartitionSpec as P

HALVES = 2
PARTS = ((14, 14), (18, 10))
EDGES = {
    "t1.pick": ["t0.add"],
    "w.pull": ["t0.columns"],
    "t0.cores": ["w.pull"],
    "t1.columns": ["t0.cores"],
    "c00.dots": ["t1.columns"],
    "t1.cores": ["c00.dots"],
    "c01.dots": ["c00.sum"],
    "c10.dots": ["c01.sum"],
    "c00.hidden": ["c10.dots"],
    "c10.sum": ["c00.halves"],
    "c01.hidden": ["c10.sum"],
    "c11.dots": ["c01.hidden"],
    "c00.columns": ["c11.dots"],
    "c01.halves": ["c00.columns"],
    "c10.hidden": ["c01.halves"],
    "c11.sum": ["c10.hidden"],
    "c01.columns": ["c11.sum"],
    "c00.cores": ["c01.columns"],
    "c10.halves": ["c00.cores"],
    "c11.hidden": ["c10.halves"],
    "c00.down": ["c11.hidden"],
    "c01.cores": ["c00.down"],
    "c10.columns": ["c01.cores"],
    "c01.down": ["c10.columns"],
    "c11.halves": ["c01.down"],
    "c10.cores": ["c11.halves"],
    "c11.columns": ["c10.down"],
    "b0.total": ["c11.columns"],
    "c11.cores": ["b0.total"],
    "c11.down": ["b0.all"],
    "b1.total": ["c11.down"],
}


def dot(a, b):
    return jnp.dot(a, b, preferred_element_type=jnp.float32)


def flip(value, axis, bit):
    count = lax.axis_size(axis)
    return lax.ppermute(value, axis, [(i, i ^ bit) for i in range(count)])


def pull_kernel(first, end, tick_ref, gate_ref, up_ref, gate_here, up_here, sems):
    del tick_ref
    columns = pl.ds(first, end - first)
    copies = [
        pltpu.make_async_copy(source.at[:, columns], here, sems.at[i])
        for i, (source, here) in enumerate(((gate_ref, gate_here), (up_ref, up_here)))
    ]
    for copy in copies:
        copy.start()
    for copy in copies:
        copy.wait()


def pull(gate_weight, up_weight, first, end, tick):
    far = pl.BlockSpec(memory_space=pltpu.HBM)
    near = pl.BlockSpec(memory_space=pltpu.VMEM)
    here = pltpu.VMEM((gate_weight.shape[0], end - first), gate_weight.dtype)
    return pl.pallas_call(
        functools.partial(pull_kernel, first, end),
        in_specs=[pl.BlockSpec(memory_space=pltpu.SMEM), far, far],
        out_specs=[near, near],
        out_shape=[here, here],
        scratch_shapes=[pltpu.SemaphoreType.DMA((2,))],
        compiler_params=pltpu.CompilerParams(
            vmem_limit_bytes=4 * gate_weight.shape[0] * (end - first) + 2**20
        ),
        cost_estimate=pl.CostEstimate(flops=0, bytes_accessed=0, transcendentals=0),
    )(
        tick,
        pltpu.with_memory_space_constraint(gate_weight, pltpu.HBM),
        pltpu.with_memory_space_constraint(up_weight, pltpu.HBM),
    )


def stationary(tokens, lengths, gate_weight, up_weight, down_weight):
    slots, width = tokens.shape
    units = gate_weight.shape[1]
    col_count = lax.axis_size("col")
    c = lax.axis_index("col")
    r = lax.axis_index("row")
    x, k, zh, zl = c // 2, c % 2, r // 2, r % 2
    quarter = slots // 2
    piece = quarter // HALVES
    half = 2 * piece
    spans = []
    for sizes in PARTS:
        ends = [0]
        for size in sizes:
            ends.append(ends[-1] + units * size // sum(sizes))
        spans.append(list(zip(ends[:-1], ends[1:])))

    rows = jnp.arange(lengths.shape[0], dtype=jnp.int32)[None]
    slot = jnp.arange(slots, dtype=jnp.int32)[None]
    here = (c ^ jnp.arange(2, dtype=jnp.int32))[:, None]
    first = jnp.sum(jnp.where(rows < here, lengths[None], 0), axis=1, keepdims=True)
    count = jnp.sum(jnp.where(rows == here, lengths[None], 0), axis=1, keepdims=True)
    places = jnp.where(slot < count, slot + first, -1)
    inside = jnp.arange(piece, dtype=jnp.int32)

    def mine_of(c):
        both = jnp.concatenate([inside + quarter * c, inside + quarter * (c ^ 2)])
        return [both + h * piece for h in range(HALVES)]

    mine = mine_of(c)

    devices = [(i // col_count, i % col_count) for i in range(lax.axis_size("row") * col_count)]

    def move(value, where_to):
        pairs = []
        for i, (row, col) in enumerate(devices):
            to = where_to(row // 2, row % 2, col // 2, col % 2)
            if to is not None:
                to_zh, to_zl, to_x, to_k = to
                pairs.append((i, (to_zh * 2 + to_zl) * col_count + to_x * 2 + to_k))
        return lax.ppermute(value, ("row", "col"), pairs)

    def one_step(value, stay, first_to, second_to):
        first, second = move(value, first_to), move(value, second_to)

        def finish(value):
            return jnp.concatenate(
                [jnp.where(stay, value, first), jnp.where(stay, first, second)], axis=0
            )

        return finish

    def to_cores(value):
        return one_step(
            value,
            zl == k,
            lambda zh, zl, x, k: (zh, 1 - zl, x, k) if k == zl else (zh, zl, x, 1 - k),
            lambda zh, zl, x, k: None if k == zl else (zh, 1 - zl, x, 1 - k),
        )

    sibling = flip(tokens, "col", 1)
    seen = {}

    def ordered(step, value):
        for name in EDGES.get(step, ()):
            while name not in seen:
                advance(name.split(".")[0])
        others = [seen[name] for name in EDGES.get(step, ())]
        return lax.optimization_barrier((value, *others))[0] if others else value

    def issued(step, value):
        seen[step] = value
        return value

    def swap_x(value):
        return flip(value, "col", 2)

    def spread_steps(name, value):
        other = flip(value, "row", 2)
        yield
        other = ordered(name + ".halves", other)
        keep = jnp.where(zh == x, value, other)
        send = issued(name + ".halves", jnp.where(zh == x, other, value))
        got = swap_x(send)
        yield
        got = ordered(name + ".columns", got)
        pair = issued(name + ".columns", jnp.concatenate([keep, got], axis=0))
        finish = to_cores(pair)
        yield
        return issued(name + ".cores", finish(ordered(name + ".cores", pair)))

    def pick_steps(name, h):
        spots = ordered(name + ".pick", mine[h])
        own = spots[:, None] == places[0][None]
        sib = spots[:, None] == places[1][None]
        rows = dot(own.astype(jnp.bfloat16), tokens) + dot(sib.astype(jnp.bfloat16), sibling)
        rows = issued(name + ".pick", rows.astype(jnp.bfloat16))
        got = swap_x(rows[piece:])
        yield
        return issued(name + ".add", ordered(name + ".add", rows[:piece]) + got)

    pulled = []

    def pull_steps():
        tick = ordered("w.pull", lengths)
        pulled.extend(pull(gate_weight, up_weight, *spans[0][0], tick))
        issued("w.pull", pulled[0])
        return None
        yield

    def half_steps(name, h):
        own = yield from pick_steps(name, h)
        return (yield from spread_steps(name, own))

    def chunk_steps(name, h, i):
        full = result("t" + str(h))
        part = slice(*spans[h][i])
        full = ordered(name + ".dots", full)
        if (h, i) == (0, 0):
            result("w")
            gate, up = dot(full, pulled[0]), dot(full, pulled[1])
        else:
            gate, up = dot(full, gate_weight[:, part]), dot(full, up_weight[:, part])
        send = issued(name + ".dots", jnp.stack([gate[half:], up[half:]]).astype(jnp.bfloat16))
        got = issued(name + ".cores_swapped", flip(send, "col", 1))
        yield
        got = ordered(name + ".sum", got)
        gate, up = gate[:half] + got[0], up[:half] + got[1]
        send = issued(name + ".sum", jnp.stack([gate[piece:], up[piece:]]).astype(jnp.bfloat16))
        got = swap_x(send)
        yield
        got = ordered(name + ".hidden", got)
        gate, up = gate[:piece] + got[0], up[:piece] + got[1]
        hidden = issued(name + ".hidden", (jax.nn.silu(gate) * up).astype(jnp.bfloat16))
        whole = yield from spread_steps(name, hidden)
        yield
        whole = ordered(name + ".down", whole)
        return issued(name + ".down", dot(whole, down_weight[part]))

    def branch_steps(name, h):
        parts = [result("c" + str(h) + str(i)) for i in range(len(spans[h]))]
        branch = issued(name + ".branch", sum(parts[1:], parts[0]))
        got = flip(branch[half:].astype(jnp.bfloat16), "col", 1)
        yield
        total = issued(name + ".total", branch[:half] + ordered(name + ".total", got))
        got = swap_x(total.astype(jnp.bfloat16))
        yield
        got = ordered(name + ".all", got)
        return issued(name + ".all", total + jnp.concatenate([got[piece:], got[:piece]], axis=0))

    chains = {"w": pull_steps()}
    results = {}
    for h in range(HALVES):
        chains["t" + str(h)] = half_steps("t" + str(h), h)
        for i in range(len(spans[h])):
            chains["c" + str(h) + str(i)] = chunk_steps("c" + str(h) + str(i), h, i)
        chains["b" + str(h)] = branch_steps("b" + str(h), h)

    def advance(name):
        try:
            next(chains[name])
        except StopIteration as stop:
            results[name] = stop.value

    def result(name):
        while name not in results:
            advance(name)
        return results[name]

    for name in EDGES:
        while name not in seen:
            advance(name.split(".")[0])
    for h in range(HALVES):
        result("b" + str(h))

    totals = [results["b" + str(h)] for h in range(HALVES)]
    theirs = [flip(total.astype(jnp.bfloat16), "col", 1) for total in totals]
    put = places[0][:, None] == jnp.concatenate(mine)[None]
    moved = jnp.dot(
        put.astype(jnp.float32), jnp.concatenate(totals), precision=lax.Precision.HIGHEST
    )
    put = places[0][:, None] == jnp.concatenate(mine_of(c ^ 1))[None]
    moved = moved + dot(put.astype(jnp.bfloat16), jnp.concatenate(theirs))
    used = (places[0] >= 0)[:, None]
    return jnp.where(used, tokens.astype(jnp.float32) + moved, 0.0).astype(jnp.bfloat16)


def general(tokens, lengths, gate_weight, up_weight, down_weight):
    c = lax.axis_index("col")
    slots = tokens.shape[0]
    whole = lax.all_gather(tokens, "row", axis=1, tiled=True)
    whole = lax.all_gather(whole, "col", axis=0, tiled=True)
    depth = gate_weight.shape[0]
    block = lax.dynamic_slice_in_dim(whole, c * depth, depth, axis=1)

    def summed(a, b):
        return lax.psum_scatter(dot(a, b), "col", scatter_dimension=0, tiled=True)

    hidden = (jax.nn.silu(summed(block, gate_weight)) * summed(block, up_weight)).astype(jnp.bfloat16)
    hidden = lax.all_gather(hidden, "row", axis=1, tiled=True)
    hidden = lax.all_gather(hidden, "col", axis=0, tiled=True)
    depth = down_weight.shape[0]
    branch = summed(lax.dynamic_slice_in_dim(hidden, c * depth, depth, axis=1), down_weight)
    valid = jnp.arange(slots, dtype=jnp.int32) < jnp.take(lengths, c)
    total = tokens.astype(jnp.float32) + branch
    return jnp.where(valid[:, None], total, jnp.float32(0.0)).astype(jnp.bfloat16)


def solution(mesh):
    square = mesh.shape["row"] == 4 and mesh.shape["col"] == 4
    in_specs = (
        P(("groups", "col"), "row"),
        P("groups"),
        P("col", "row"),
        P("col", "row"),
        P("col", "row"),
    )
    out_specs = P(("groups", "col"), "row")
    return jax.shard_map(
        stationary if square else general,
        mesh=mesh, in_specs=in_specs, out_specs=out_specs, check_vma=False,
    )
```

```python
import functools

import jax
import jax.numpy as jnp
from jax import lax
from jax.experimental import pallas as pl
from jax.experimental.pallas import tpu as pltpu
from jax.sharding import PartitionSpec as P

HALVES = 2
PIECES = (1, 1)
PARTS = ((14, 14), (12, 10, 6))
EDGES = {
    "t1.pick": ["t0.add"],
    "t1.halves": ["t0.columns"],
    "w.pull": ["t1.halves"],
    "t0.cores": ["w.pull"],
    "t1.columns": ["t0.cores"],
    "c00.dots": ["t1.columns"],
    "t1.cores": ["c00.dots"],
    "c01.dots": ["c00.sum"],
    "c10.dots": ["c01.dots"],
    "c01.sum": ["c10.dots"],
    "c00.hidden": ["c01.sum"],
    "c10.sum": ["c00.halves"],
    "c01.hidden": ["c10.sum"],
    "c11.dots": ["c01.hidden"],
    "c00.columns": ["c11.dots"],
    "c01.halves": ["c00.columns"],
    "c12.dots": ["c01.halves"],
    "c10.hidden": ["c12.dots"],
    "c11.sum": ["c10.hidden"],
    "c01.columns": ["c11.sum"],
    "c00.cores": ["c01.columns"],
    "c12.sum": ["c00.down"],
    "c10.halves": ["c12.sum"],
    "c11.hidden": ["c10.halves"],
    "c01.cores": ["c11.hidden"],
    "c12.hidden": ["c01.cores"],
    "c10.columns": ["c12.hidden"],
    "c01.down": ["c10.columns"],
    "b0.total": ["c11.halves"],
    "c10.cores": ["b0.total"],
    "c12.halves": ["c10.down"],
    "c11.columns": ["c12.halves"],
    "c12.columns": ["c11.cores"],
    "c12.cores": ["c11.down"],
    "b1.total": ["c12.down"],
}


def dot(a, b):
    return jnp.dot(a, b, preferred_element_type=jnp.float32)


def flip(value, axis, bit):
    count = lax.axis_size(axis)
    return lax.ppermute(value, axis, [(i, i ^ bit) for i in range(count)])


def pull_kernel(first, end, tick_ref, gate_ref, up_ref, gate_here, up_here, sems):
    del tick_ref
    columns = pl.ds(first, end - first)
    copies = [
        pltpu.make_async_copy(source.at[:, columns], here, sems.at[i])
        for i, (source, here) in enumerate(((gate_ref, gate_here), (up_ref, up_here)))
    ]
    for copy in copies:
        copy.start()
    for copy in copies:
        copy.wait()


def pull(gate_weight, up_weight, first, end, tick):
    far = pl.BlockSpec(memory_space=pltpu.HBM)
    near = pl.BlockSpec(memory_space=pltpu.VMEM)
    here = pltpu.VMEM((gate_weight.shape[0], end - first), gate_weight.dtype)
    return pl.pallas_call(
        functools.partial(pull_kernel, first, end),
        in_specs=[pl.BlockSpec(memory_space=pltpu.SMEM), far, far],
        out_specs=[near, near],
        out_shape=[here, here],
        scratch_shapes=[pltpu.SemaphoreType.DMA((2,))],
        compiler_params=pltpu.CompilerParams(
            vmem_limit_bytes=4 * gate_weight.shape[0] * (end - first) + 2**20
        ),
        cost_estimate=pl.CostEstimate(flops=0, bytes_accessed=0, transcendentals=0),
    )(
        tick,
        pltpu.with_memory_space_constraint(gate_weight, pltpu.HBM),
        pltpu.with_memory_space_constraint(up_weight, pltpu.HBM),
    )


def stationary(tokens, lengths, gate_weight, up_weight, down_weight):
    slots, width = tokens.shape
    units = gate_weight.shape[1]
    col_count = lax.axis_size("col")
    c = lax.axis_index("col")
    r = lax.axis_index("row")
    x, k, zh, zl = c // 2, c % 2, r // 2, r % 2
    quarter = slots // 2
    pieces = [quarter * share // sum(PIECES) for share in PIECES]
    spans = []
    for sizes in PARTS:
        ends = [0]
        for size in sizes:
            ends.append(ends[-1] + units * size // sum(sizes))
        spans.append(list(zip(ends[:-1], ends[1:])))

    rows = jnp.arange(lengths.shape[0], dtype=jnp.int32)[None]
    slot = jnp.arange(slots, dtype=jnp.int32)[None]
    here = (c ^ jnp.arange(2, dtype=jnp.int32))[:, None]
    first = jnp.sum(jnp.where(rows < here, lengths[None], 0), axis=1, keepdims=True)
    count = jnp.sum(jnp.where(rows == here, lengths[None], 0), axis=1, keepdims=True)
    places = jnp.where(slot < count, slot + first, -1)
    def mine_of(c):
        found = []
        for h, piece in enumerate(pieces):
            inside = jnp.arange(piece, dtype=jnp.int32) + sum(pieces[:h])
            found.append(jnp.concatenate([inside + quarter * c, inside + quarter * (c ^ 2)]))
        return found

    mine = mine_of(c)

    devices = [(i // col_count, i % col_count) for i in range(lax.axis_size("row") * col_count)]

    def move(value, where_to):
        pairs = []
        for i, (row, col) in enumerate(devices):
            to = where_to(row // 2, row % 2, col // 2, col % 2)
            if to is not None:
                to_zh, to_zl, to_x, to_k = to
                pairs.append((i, (to_zh * 2 + to_zl) * col_count + to_x * 2 + to_k))
        return lax.ppermute(value, ("row", "col"), pairs)

    def one_step(value, stay, first_to, second_to):
        first, second = move(value, first_to), move(value, second_to)

        def finish(value):
            return jnp.concatenate(
                [jnp.where(stay, value, first), jnp.where(stay, first, second)], axis=0
            )

        return finish

    def to_cores(value):
        return one_step(
            value,
            zl == k,
            lambda zh, zl, x, k: (zh, 1 - zl, x, k) if k == zl else (zh, zl, x, 1 - k),
            lambda zh, zl, x, k: None if k == zl else (zh, 1 - zl, x, 1 - k),
        )

    sibling = flip(tokens, "col", 1)
    seen = {}

    def ordered(step, value):
        for name in EDGES.get(step, ()):
            while name not in seen:
                advance(name.split(".")[0])
        others = [seen[name] for name in EDGES.get(step, ())]
        return lax.optimization_barrier((value, *others))[0] if others else value

    def issued(step, value):
        seen[step] = value
        return value

    def swap_x(value):
        return flip(value, "col", 2)

    def spread_steps(name, value):
        other = flip(value, "row", 2)
        yield
        other = ordered(name + ".halves", other)
        keep = jnp.where(zh == x, value, other)
        send = issued(name + ".halves", jnp.where(zh == x, other, value))
        got = swap_x(send)
        yield
        got = ordered(name + ".columns", got)
        pair = issued(name + ".columns", jnp.concatenate([keep, got], axis=0))
        finish = to_cores(pair)
        yield
        return issued(name + ".cores", finish(ordered(name + ".cores", pair)))

    def pick_steps(name, h):
        piece = pieces[h]
        spots = ordered(name + ".pick", mine[h])
        own = spots[:, None] == places[0][None]
        sib = spots[:, None] == places[1][None]
        rows = dot(own.astype(jnp.bfloat16), tokens) + dot(sib.astype(jnp.bfloat16), sibling)
        rows = issued(name + ".pick", rows.astype(jnp.bfloat16))
        got = swap_x(rows[piece:])
        yield
        return issued(name + ".add", ordered(name + ".add", rows[:piece]) + got)

    pulled = []

    def pull_steps():
        tick = ordered("w.pull", lengths)
        pulled.extend(pull(gate_weight, up_weight, *spans[0][0], tick))
        issued("w.pull", pulled[0])
        return None
        yield

    def half_steps(name, h):
        own = yield from pick_steps(name, h)
        return (yield from spread_steps(name, own))

    def chunk_steps(name, h, i):
        full = result("t" + str(h))
        part = slice(*spans[h][i])
        piece, half = pieces[h], 2 * pieces[h]
        full = ordered(name + ".dots", full)
        if (h, i) == (0, 0):
            result("w")
            gate, up = dot(full, pulled[0]), dot(full, pulled[1])
        else:
            gate, up = dot(full, gate_weight[:, part]), dot(full, up_weight[:, part])
        send = issued(name + ".dots", jnp.stack([gate[half:], up[half:]]).astype(jnp.bfloat16))
        got = issued(name + ".cores_swapped", flip(send, "col", 1))
        yield
        got = ordered(name + ".sum", got)
        gate, up = gate[:half] + got[0], up[:half] + got[1]
        send = issued(name + ".sum", jnp.stack([gate[piece:], up[piece:]]).astype(jnp.bfloat16))
        got = swap_x(send)
        yield
        got = ordered(name + ".hidden", got)
        gate, up = gate[:piece] + got[0], up[:piece] + got[1]
        hidden = issued(name + ".hidden", (jax.nn.silu(gate) * up).astype(jnp.bfloat16))
        whole = yield from spread_steps(name, hidden)
        yield
        whole = ordered(name + ".down", whole)
        return issued(name + ".down", dot(whole, down_weight[part]))

    def branch_steps(name, h):
        parts = [result("c" + str(h) + str(i)) for i in range(len(spans[h]))]
        piece, half = pieces[h], 2 * pieces[h]
        branch = issued(name + ".branch", sum(parts[1:], parts[0]))
        got = flip(branch[half:].astype(jnp.bfloat16), "col", 1)
        yield
        total = issued(name + ".total", branch[:half] + ordered(name + ".total", got))
        got = swap_x(total.astype(jnp.bfloat16))
        yield
        got = ordered(name + ".all", got)
        return issued(name + ".all", total + jnp.concatenate([got[piece:], got[:piece]], axis=0))

    chains = {"w": pull_steps()}
    results = {}
    for h in range(HALVES):
        chains["t" + str(h)] = half_steps("t" + str(h), h)
        for i in range(len(spans[h])):
            chains["c" + str(h) + str(i)] = chunk_steps("c" + str(h) + str(i), h, i)
        chains["b" + str(h)] = branch_steps("b" + str(h), h)

    def advance(name):
        try:
            next(chains[name])
        except StopIteration as stop:
            results[name] = stop.value

    def result(name):
        while name not in results:
            advance(name)
        return results[name]

    for name in EDGES:
        while name not in seen:
            advance(name.split(".")[0])
    for h in range(HALVES):
        result("b" + str(h))

    totals = [results["b" + str(h)] for h in range(HALVES)]
    theirs = [flip(total.astype(jnp.bfloat16), "col", 1) for total in totals]
    put = places[0][:, None] == jnp.concatenate(mine)[None]
    moved = jnp.dot(
        put.astype(jnp.float32), jnp.concatenate(totals), precision=lax.Precision.HIGHEST
    )
    put = places[0][:, None] == jnp.concatenate(mine_of(c ^ 1))[None]
    moved = moved + dot(put.astype(jnp.bfloat16), jnp.concatenate(theirs))
    used = (places[0] >= 0)[:, None]
    return jnp.where(used, tokens.astype(jnp.float32) + moved, 0.0).astype(jnp.bfloat16)


def general(tokens, lengths, gate_weight, up_weight, down_weight):
    c = lax.axis_index("col")
    slots = tokens.shape[0]
    whole = lax.all_gather(tokens, "row", axis=1, tiled=True)
    whole = lax.all_gather(whole, "col", axis=0, tiled=True)
    depth = gate_weight.shape[0]
    block = lax.dynamic_slice_in_dim(whole, c * depth, depth, axis=1)

    def summed(a, b):
        return lax.psum_scatter(dot(a, b), "col", scatter_dimension=0, tiled=True)

    hidden = (jax.nn.silu(summed(block, gate_weight)) * summed(block, up_weight)).astype(jnp.bfloat16)
    hidden = lax.all_gather(hidden, "row", axis=1, tiled=True)
    hidden = lax.all_gather(hidden, "col", axis=0, tiled=True)
    depth = down_weight.shape[0]
    branch = summed(lax.dynamic_slice_in_dim(hidden, c * depth, depth, axis=1), down_weight)
    valid = jnp.arange(slots, dtype=jnp.int32) < jnp.take(lengths, c)
    total = tokens.astype(jnp.float32) + branch
    return jnp.where(valid[:, None], total, jnp.float32(0.0)).astype(jnp.bfloat16)


def solution(mesh):
    square = mesh.shape["row"] == 4 and mesh.shape["col"] == 4
    in_specs = (
        P(("groups", "col"), "row"),
        P("groups"),
        P("col", "row"),
        P("col", "row"),
        P("col", "row"),
    )
    out_specs = P(("groups", "col"), "row")
    return jax.shard_map(
        stationary if square else general,
        mesh=mesh, in_specs=in_specs, out_specs=out_specs, check_vma=False,
    )
```

```python
import functools

import jax
import jax.numpy as jnp
from jax import lax
from jax.experimental import pallas as pl
from jax.experimental.pallas import tpu as pltpu
from jax.sharding import PartitionSpec as P

HALVES = 2
PIECES = (1, 1)
PARTS = ((14, 14), (18, 10))
EDGES = {
    "t1.pick": ["t0.pick"],
    "t0.add": ["t1.pick"],
    "t1.add": ["t0.add"],
    "w.pull": ["t0.columns"],
    "t0.cores": ["w.pull"],
    "t1.columns": ["t0.cores"],
    "c00.dots": ["t1.columns"],
    "c01.dots": ["c00.dots"],
    "t1.cores": ["c01.dots"],
    "c01.sum": ["c00.sum"],
    "c10.dots": ["c01.sum"],
    "c00.hidden": ["c10.dots"],
    "c10.sum": ["c00.halves"],
    "c01.hidden": ["c10.sum"],
    "c11.dots": ["c01.hidden"],
    "c00.columns": ["c11.dots"],
    "c01.halves": ["c00.columns"],
    "c10.hidden": ["c01.halves"],
    "c01.columns": ["c10.hidden"],
    "c11.sum": ["c01.columns"],
    "c00.cores": ["c11.sum"],
    "c11.hidden": ["c10.halves"],
    "c00.down": ["c11.hidden"],
    "c01.cores": ["c00.down"],
    "c11.halves": ["c10.columns"],
    "c01.down": ["c11.halves"],
    "c11.columns": ["c10.down"],
    "b0.total": ["c11.columns"],
    "c11.cores": ["b0.total"],
    "b1.total": ["b0.all"],
}


def dot(a, b):
    return jnp.dot(a, b, preferred_element_type=jnp.float32)


def flip(value, axis, bit):
    count = lax.axis_size(axis)
    return lax.ppermute(value, axis, [(i, i ^ bit) for i in range(count)])


def pull_kernel(first, end, tick_ref, gate_ref, up_ref, gate_here, up_here, sems):
    del tick_ref
    columns = pl.ds(first, end - first)
    copies = [
        pltpu.make_async_copy(source.at[:, columns], here, sems.at[i])
        for i, (source, here) in enumerate(((gate_ref, gate_here), (up_ref, up_here)))
    ]
    for copy in copies:
        copy.start()
    for copy in copies:
        copy.wait()


def pull(gate_weight, up_weight, first, end, tick):
    far = pl.BlockSpec(memory_space=pltpu.HBM)
    near = pl.BlockSpec(memory_space=pltpu.VMEM)
    here = pltpu.VMEM((gate_weight.shape[0], end - first), gate_weight.dtype)
    return pl.pallas_call(
        functools.partial(pull_kernel, first, end),
        in_specs=[pl.BlockSpec(memory_space=pltpu.SMEM), far, far],
        out_specs=[near, near],
        out_shape=[here, here],
        scratch_shapes=[pltpu.SemaphoreType.DMA((2,))],
        compiler_params=pltpu.CompilerParams(
            vmem_limit_bytes=4 * gate_weight.shape[0] * (end - first) + 2**20
        ),
        cost_estimate=pl.CostEstimate(flops=0, bytes_accessed=0, transcendentals=0),
    )(
        tick,
        pltpu.with_memory_space_constraint(gate_weight, pltpu.HBM),
        pltpu.with_memory_space_constraint(up_weight, pltpu.HBM),
    )


def stationary(tokens, lengths, gate_weight, up_weight, down_weight):
    slots, width = tokens.shape
    units = gate_weight.shape[1]
    col_count = lax.axis_size("col")
    c = lax.axis_index("col")
    r = lax.axis_index("row")
    x, k, zh, zl = c // 2, c % 2, r // 2, r % 2
    quarter = slots // 2
    pieces = [quarter * share // sum(PIECES) for share in PIECES]
    spans = []
    for sizes in PARTS:
        ends = [0]
        for size in sizes:
            ends.append(ends[-1] + units * size // sum(sizes))
        spans.append(list(zip(ends[:-1], ends[1:])))

    rows = jnp.arange(lengths.shape[0], dtype=jnp.int32)[None]
    slot = jnp.arange(slots, dtype=jnp.int32)[None]
    here = (c ^ jnp.arange(2, dtype=jnp.int32))[:, None]
    first = jnp.sum(jnp.where(rows < here, lengths[None], 0), axis=1, keepdims=True)
    count = jnp.sum(jnp.where(rows == here, lengths[None], 0), axis=1, keepdims=True)
    places = jnp.where(slot < count, slot + first, -1)
    def mine_of(c):
        found = []
        for h, piece in enumerate(pieces):
            inside = jnp.arange(piece, dtype=jnp.int32) + sum(pieces[:h])
            found.append(jnp.concatenate([inside + quarter * c, inside + quarter * (c ^ 2)]))
        return found

    mine = mine_of(c)

    devices = [(i // col_count, i % col_count) for i in range(lax.axis_size("row") * col_count)]

    def move(value, where_to):
        pairs = []
        for i, (row, col) in enumerate(devices):
            to = where_to(row // 2, row % 2, col // 2, col % 2)
            if to is not None:
                to_zh, to_zl, to_x, to_k = to
                pairs.append((i, (to_zh * 2 + to_zl) * col_count + to_x * 2 + to_k))
        return lax.ppermute(value, ("row", "col"), pairs)

    def one_step(value, stay, first_to, second_to):
        first, second = move(value, first_to), move(value, second_to)

        def finish(value):
            return jnp.concatenate(
                [jnp.where(stay, value, first), jnp.where(stay, first, second)], axis=0
            )

        return finish

    def to_cores(value):
        return one_step(
            value,
            zl == k,
            lambda zh, zl, x, k: (zh, 1 - zl, x, k) if k == zl else (zh, zl, x, 1 - k),
            lambda zh, zl, x, k: None if k == zl else (zh, 1 - zl, x, 1 - k),
        )

    sibling = flip(tokens, "col", 1)
    seen = {}

    def ordered(step, value):
        for name in EDGES.get(step, ()):
            while name not in seen:
                advance(name.split(".")[0])
        others = [seen[name] for name in EDGES.get(step, ())]
        return lax.optimization_barrier((value, *others))[0] if others else value

    def issued(step, value):
        seen[step] = value
        return value

    def swap_x(value):
        return flip(value, "col", 2)

    def spread_steps(name, value):
        other = flip(value, "row", 2)
        yield
        other = ordered(name + ".halves", other)
        keep = jnp.where(zh == x, value, other)
        send = issued(name + ".halves", jnp.where(zh == x, other, value))
        got = swap_x(send)
        yield
        got = ordered(name + ".columns", got)
        pair = issued(name + ".columns", jnp.concatenate([keep, got], axis=0))
        finish = to_cores(pair)
        yield
        return issued(name + ".cores", finish(ordered(name + ".cores", pair)))

    def pick_steps(name, h):
        piece = pieces[h]
        spots = ordered(name + ".pick", mine[h])
        own = spots[:, None] == places[0][None]
        sib = spots[:, None] == places[1][None]
        rows = dot(own.astype(jnp.bfloat16), tokens) + dot(sib.astype(jnp.bfloat16), sibling)
        rows = issued(name + ".pick", rows.astype(jnp.bfloat16))
        got = swap_x(rows[piece:])
        yield
        return issued(name + ".add", ordered(name + ".add", rows[:piece]) + got)

    pulled = []

    def pull_steps():
        tick = ordered("w.pull", lengths)
        pulled.extend(pull(gate_weight, up_weight, *spans[0][0], tick))
        issued("w.pull", pulled[0])
        return None
        yield

    def half_steps(name, h):
        own = yield from pick_steps(name, h)
        return (yield from spread_steps(name, own))

    def chunk_steps(name, h, i):
        full = result("t" + str(h))
        part = slice(*spans[h][i])
        piece, half = pieces[h], 2 * pieces[h]
        full = ordered(name + ".dots", full)
        if (h, i) == (0, 0):
            result("w")
            gate, up = dot(full, pulled[0]), dot(full, pulled[1])
        else:
            gate, up = dot(full, gate_weight[:, part]), dot(full, up_weight[:, part])
        send = issued(name + ".dots", jnp.stack([gate[half:], up[half:]]).astype(jnp.bfloat16))
        got = issued(name + ".cores_swapped", flip(send, "col", 1))
        yield
        got = ordered(name + ".sum", got)
        gate, up = gate[:half] + got[0], up[:half] + got[1]
        send = issued(name + ".sum", jnp.stack([gate[piece:], up[piece:]]).astype(jnp.bfloat16))
        got = swap_x(send)
        yield
        got = ordered(name + ".hidden", got)
        gate, up = gate[:piece] + got[0], up[:piece] + got[1]
        hidden = issued(name + ".hidden", (jax.nn.silu(gate) * up).astype(jnp.bfloat16))
        whole = yield from spread_steps(name, hidden)
        yield
        whole = ordered(name + ".down", whole)
        return issued(name + ".down", dot(whole, down_weight[part]))

    def branch_steps(name, h):
        parts = [result("c" + str(h) + str(i)) for i in range(len(spans[h]))]
        piece, half = pieces[h], 2 * pieces[h]
        branch = issued(name + ".branch", sum(parts[1:], parts[0]))
        got = flip(branch[half:].astype(jnp.bfloat16), "col", 1)
        yield
        total = issued(name + ".total", branch[:half] + ordered(name + ".total", got))
        got = swap_x(total.astype(jnp.bfloat16))
        yield
        got = ordered(name + ".all", got)
        return issued(name + ".all", total + jnp.concatenate([got[piece:], got[:piece]], axis=0))

    chains = {"w": pull_steps()}
    results = {}
    for h in range(HALVES):
        chains["t" + str(h)] = half_steps("t" + str(h), h)
        for i in range(len(spans[h])):
            chains["c" + str(h) + str(i)] = chunk_steps("c" + str(h) + str(i), h, i)
        chains["b" + str(h)] = branch_steps("b" + str(h), h)

    def advance(name):
        try:
            next(chains[name])
        except StopIteration as stop:
            results[name] = stop.value

    def result(name):
        while name not in results:
            advance(name)
        return results[name]

    for name in EDGES:
        while name not in seen:
            advance(name.split(".")[0])
    for h in range(HALVES):
        result("b" + str(h))

    totals = [results["b" + str(h)] for h in range(HALVES)]
    theirs = [flip(total.astype(jnp.bfloat16), "col", 1) for total in totals]
    put = places[0][:, None] == jnp.concatenate(mine)[None]
    moved = jnp.dot(
        put.astype(jnp.float32), jnp.concatenate(totals), precision=lax.Precision.HIGHEST
    )
    put = places[0][:, None] == jnp.concatenate(mine_of(c ^ 1))[None]
    moved = moved + dot(put.astype(jnp.bfloat16), jnp.concatenate(theirs))
    used = (places[0] >= 0)[:, None]
    return jnp.where(used, tokens.astype(jnp.float32) + moved, 0.0).astype(jnp.bfloat16)


def general(tokens, lengths, gate_weight, up_weight, down_weight):
    c = lax.axis_index("col")
    slots = tokens.shape[0]
    whole = lax.all_gather(tokens, "row", axis=1, tiled=True)
    whole = lax.all_gather(whole, "col", axis=0, tiled=True)
    depth = gate_weight.shape[0]
    block = lax.dynamic_slice_in_dim(whole, c * depth, depth, axis=1)

    def summed(a, b):
        return lax.psum_scatter(dot(a, b), "col", scatter_dimension=0, tiled=True)

    hidden = (jax.nn.silu(summed(block, gate_weight)) * summed(block, up_weight)).astype(jnp.bfloat16)
    hidden = lax.all_gather(hidden, "row", axis=1, tiled=True)
    hidden = lax.all_gather(hidden, "col", axis=0, tiled=True)
    depth = down_weight.shape[0]
    branch = summed(lax.dynamic_slice_in_dim(hidden, c * depth, depth, axis=1), down_weight)
    valid = jnp.arange(slots, dtype=jnp.int32) < jnp.take(lengths, c)
    total = tokens.astype(jnp.float32) + branch
    return jnp.where(valid[:, None], total, jnp.float32(0.0)).astype(jnp.bfloat16)


def solution(mesh):
    square = mesh.shape["row"] == 4 and mesh.shape["col"] == 4
    in_specs = (
        P(("groups", "col"), "row"),
        P("groups"),
        P("col", "row"),
        P("col", "row"),
        P("col", "row"),
    )
    out_specs = P(("groups", "col"), "row")
    return jax.shard_map(
        stationary if square else general,
        mesh=mesh, in_specs=in_specs, out_specs=out_specs, check_vma=False,
    )
```

```python
import functools

import jax
import jax.numpy as jnp
from jax import lax
from jax.experimental import pallas as pl
from jax.experimental.pallas import tpu as pltpu
from jax.sharding import PartitionSpec as P

HALVES = 2
PARTS = ((14, 14), (18, 10))
EDGES = {
    "t1.pick": ["t0.add"],
    "w.pull": ["t0.columns"],
    "t0.cores": ["w.pull"],
    "t1.columns": ["t0.cores"],
    "c00.dots": ["t1.columns"],
    "t1.cores": ["c00.dots"],
    "c01.dots": ["c00.sum"],
    "c10.dots": ["c01.sum"],
    "c00.hidden": ["c10.dots"],
    "c10.sum": ["c00.halves"],
    "c01.hidden": ["c10.sum"],
    "c11.dots": ["c01.hidden"],
    "c00.columns": ["c11.dots"],
    "c01.halves": ["c00.columns"],
    "c10.hidden": ["c01.halves"],
    "c11.sum": ["c10.hidden"],
    "c01.columns": ["c11.sum"],
    "c00.cores": ["c01.columns"],
    "c10.halves": ["c00.cores"],
    "c11.hidden": ["c10.halves"],
    "c00.down": ["c11.hidden"],
    "c01.cores": ["c00.down"],
    "c10.columns": ["c01.cores"],
    "c01.down": ["c10.columns"],
    "c11.halves": ["c01.down"],
    "c10.cores": ["c11.halves"],
    "c11.columns": ["c10.down"],
    "b0.total": ["c11.columns"],
    "c11.cores": ["b0.total"],
    "c11.down": ["b0.total"],
    "b1.total": ["c11.down"],
}


def dot(a, b):
    return jnp.dot(a, b, preferred_element_type=jnp.float32)


def flip(value, axis, bit):
    count = lax.axis_size(axis)
    return lax.ppermute(value, axis, [(i, i ^ bit) for i in range(count)])


def pull_kernel(first, end, tick_ref, gate_ref, up_ref, gate_here, up_here, sems):
    del tick_ref
    columns = pl.ds(first, end - first)
    copies = [
        pltpu.make_async_copy(source.at[:, columns], here, sems.at[i])
        for i, (source, here) in enumerate(((gate_ref, gate_here), (up_ref, up_here)))
    ]
    for copy in copies:
        copy.start()
    for copy in copies:
        copy.wait()


def pull(gate_weight, up_weight, first, end, tick):
    far = pl.BlockSpec(memory_space=pltpu.HBM)
    near = pl.BlockSpec(memory_space=pltpu.VMEM)
    here = pltpu.VMEM((gate_weight.shape[0], end - first), gate_weight.dtype)
    return pl.pallas_call(
        functools.partial(pull_kernel, first, end),
        in_specs=[pl.BlockSpec(memory_space=pltpu.SMEM), far, far],
        out_specs=[near, near],
        out_shape=[here, here],
        scratch_shapes=[pltpu.SemaphoreType.DMA((2,))],
        compiler_params=pltpu.CompilerParams(
            vmem_limit_bytes=4 * gate_weight.shape[0] * (end - first) + 2**20
        ),
        cost_estimate=pl.CostEstimate(flops=0, bytes_accessed=0, transcendentals=0),
    )(
        tick,
        pltpu.with_memory_space_constraint(gate_weight, pltpu.HBM),
        pltpu.with_memory_space_constraint(up_weight, pltpu.HBM),
    )


def stationary(tokens, lengths, gate_weight, up_weight, down_weight):
    slots, width = tokens.shape
    units = gate_weight.shape[1]
    col_count = lax.axis_size("col")
    c = lax.axis_index("col")
    r = lax.axis_index("row")
    x, k, zh, zl = c // 2, c % 2, r // 2, r % 2
    quarter = slots // 2
    piece = quarter // HALVES
    half = 2 * piece
    spans = []
    for sizes in PARTS:
        ends = [0]
        for size in sizes:
            ends.append(ends[-1] + units * size // sum(sizes))
        spans.append(list(zip(ends[:-1], ends[1:])))

    rows = jnp.arange(lengths.shape[0], dtype=jnp.int32)[None]
    slot = jnp.arange(slots, dtype=jnp.int32)[None]
    here = (c ^ jnp.arange(2, dtype=jnp.int32))[:, None]
    first = jnp.sum(jnp.where(rows < here, lengths[None], 0), axis=1, keepdims=True)
    count = jnp.sum(jnp.where(rows == here, lengths[None], 0), axis=1, keepdims=True)
    places = jnp.where(slot < count, slot + first, -1)
    inside = jnp.arange(piece, dtype=jnp.int32)

    def mine_of(c):
        both = jnp.concatenate([inside + quarter * c, inside + quarter * (c ^ 2)])
        return [both + h * piece for h in range(HALVES)]

    mine = mine_of(c)

    devices = [(i // col_count, i % col_count) for i in range(lax.axis_size("row") * col_count)]

    def move(value, where_to):
        pairs = []
        for i, (row, col) in enumerate(devices):
            to = where_to(row // 2, row % 2, col // 2, col % 2)
            if to is not None:
                to_zh, to_zl, to_x, to_k = to
                pairs.append((i, (to_zh * 2 + to_zl) * col_count + to_x * 2 + to_k))
        return lax.ppermute(value, ("row", "col"), pairs)

    def one_step(value, stay, first_to, second_to):
        first, second = move(value, first_to), move(value, second_to)

        def finish(value):
            return jnp.concatenate(
                [jnp.where(stay, value, first), jnp.where(stay, first, second)], axis=0
            )

        return finish

    def to_cores(value):
        return one_step(
            value,
            zl == k,
            lambda zh, zl, x, k: (zh, 1 - zl, x, k) if k == zl else (zh, zl, x, 1 - k),
            lambda zh, zl, x, k: None if k == zl else (zh, 1 - zl, x, 1 - k),
        )

    sibling = flip(tokens, "col", 1)
    seen = {}

    def ordered(step, value):
        for name in EDGES.get(step, ()):
            while name not in seen:
                advance(name.split(".")[0])
        others = [seen[name] for name in EDGES.get(step, ())]
        return lax.optimization_barrier((value, *others))[0] if others else value

    def issued(step, value):
        seen[step] = value
        return value

    def swap_x(value):
        return flip(value, "col", 2)

    def spread_steps(name, value):
        other = flip(value, "row", 2)
        yield
        other = ordered(name + ".halves", other)
        keep = jnp.where(zh == x, value, other)
        send = issued(name + ".halves", jnp.where(zh == x, other, value))
        got = swap_x(send)
        yield
        got = ordered(name + ".columns", got)
        pair = issued(name + ".columns", jnp.concatenate([keep, got], axis=0))
        finish = to_cores(pair)
        yield
        return issued(name + ".cores", finish(ordered(name + ".cores", pair)))

    def pick_steps(name, h):
        spots = ordered(name + ".pick", mine[h])
        own = spots[:, None] == places[0][None]
        sib = spots[:, None] == places[1][None]
        rows = dot(own.astype(jnp.bfloat16), tokens) + dot(sib.astype(jnp.bfloat16), sibling)
        rows = issued(name + ".pick", rows.astype(jnp.bfloat16))
        got = swap_x(rows[piece:])
        yield
        return issued(name + ".add", ordered(name + ".add", rows[:piece]) + got)

    pulled = []

    def pull_steps():
        tick = ordered("w.pull", lengths)
        pulled.extend(pull(gate_weight, up_weight, *spans[0][0], tick))
        issued("w.pull", pulled[0])
        return None
        yield

    def half_steps(name, h):
        own = yield from pick_steps(name, h)
        return (yield from spread_steps(name, own))

    def chunk_steps(name, h, i):
        full = result("t" + str(h))
        part = slice(*spans[h][i])
        full = ordered(name + ".dots", full)
        if (h, i) == (0, 0):
            result("w")
            gate, up = dot(full, pulled[0]), dot(full, pulled[1])
        else:
            gate, up = dot(full, gate_weight[:, part]), dot(full, up_weight[:, part])
        send = issued(name + ".dots", jnp.stack([gate[half:], up[half:]]).astype(jnp.bfloat16))
        got = issued(name + ".cores_swapped", flip(send, "col", 1))
        yield
        got = ordered(name + ".sum", got)
        gate, up = gate[:half] + got[0], up[:half] + got[1]
        send = issued(name + ".sum", jnp.stack([gate[piece:], up[piece:]]).astype(jnp.bfloat16))
        got = swap_x(send)
        yield
        got = ordered(name + ".hidden", got)
        gate, up = gate[:piece] + got[0], up[:piece] + got[1]
        hidden = issued(name + ".hidden", (jax.nn.silu(gate) * up).astype(jnp.bfloat16))
        whole = yield from spread_steps(name, hidden)
        yield
        whole = ordered(name + ".down", whole)
        return issued(name + ".down", dot(whole, down_weight[part]))

    def branch_steps(name, h):
        parts = [result("c" + str(h) + str(i)) for i in range(len(spans[h]))]
        branch = issued(name + ".branch", sum(parts[1:], parts[0]))
        got = flip(branch[half:].astype(jnp.bfloat16), "col", 1)
        yield
        total = issued(name + ".total", branch[:half] + ordered(name + ".total", got))
        got = swap_x(total.astype(jnp.bfloat16))
        yield
        got = ordered(name + ".all", got)
        return issued(name + ".all", total + jnp.concatenate([got[piece:], got[:piece]], axis=0))

    chains = {"w": pull_steps()}
    results = {}
    for h in range(HALVES):
        chains["t" + str(h)] = half_steps("t" + str(h), h)
        for i in range(len(spans[h])):
            chains["c" + str(h) + str(i)] = chunk_steps("c" + str(h) + str(i), h, i)
        chains["b" + str(h)] = branch_steps("b" + str(h), h)

    def advance(name):
        try:
            next(chains[name])
        except StopIteration as stop:
            results[name] = stop.value

    def result(name):
        while name not in results:
            advance(name)
        return results[name]

    for name in EDGES:
        while name not in seen:
            advance(name.split(".")[0])
    for h in range(HALVES):
        result("b" + str(h))

    totals = [results["b" + str(h)] for h in range(HALVES)]
    theirs = [flip(total.astype(jnp.bfloat16), "col", 1) for total in totals]
    put = places[0][:, None] == jnp.concatenate(mine)[None]
    moved = jnp.dot(
        put.astype(jnp.float32), jnp.concatenate(totals), precision=lax.Precision.HIGHEST
    )
    put = places[0][:, None] == jnp.concatenate(mine_of(c ^ 1))[None]
    moved = moved + dot(put.astype(jnp.bfloat16), jnp.concatenate(theirs))
    used = (places[0] >= 0)[:, None]
    return jnp.where(used, tokens.astype(jnp.float32) + moved, 0.0).astype(jnp.bfloat16)


def general(tokens, lengths, gate_weight, up_weight, down_weight):
    c = lax.axis_index("col")
    slots = tokens.shape[0]
    whole = lax.all_gather(tokens, "row", axis=1, tiled=True)
    whole = lax.all_gather(whole, "col", axis=0, tiled=True)
    depth = gate_weight.shape[0]
    block = lax.dynamic_slice_in_dim(whole, c * depth, depth, axis=1)

    def summed(a, b):
        return lax.psum_scatter(dot(a, b), "col", scatter_dimension=0, tiled=True)

    hidden = (jax.nn.silu(summed(block, gate_weight)) * summed(block, up_weight)).astype(jnp.bfloat16)
    hidden = lax.all_gather(hidden, "row", axis=1, tiled=True)
    hidden = lax.all_gather(hidden, "col", axis=0, tiled=True)
    depth = down_weight.shape[0]
    branch = summed(lax.dynamic_slice_in_dim(hidden, c * depth, depth, axis=1), down_weight)
    valid = jnp.arange(slots, dtype=jnp.int32) < jnp.take(lengths, c)
    total = tokens.astype(jnp.float32) + branch
    return jnp.where(valid[:, None], total, jnp.float32(0.0)).astype(jnp.bfloat16)


def solution(mesh):
    square = mesh.shape["row"] == 4 and mesh.shape["col"] == 4
    in_specs = (
        P(("groups", "col"), "row"),
        P("groups"),
        P("col", "row"),
        P("col", "row"),
        P("col", "row"),
    )
    out_specs = P(("groups", "col"), "row")
    return jax.shard_map(
        stationary if square else general,
        mesh=mesh, in_specs=in_specs, out_specs=out_specs, check_vma=False,
    )
```

```python
import functools

import jax
import jax.numpy as jnp
from jax import lax
from jax.experimental import pallas as pl
from jax.experimental.pallas import tpu as pltpu
from jax.sharding import PartitionSpec as P

HALVES = 2
PARTS = ((12, 16), (18, 10))
EDGES = {
    "t1.pick": ["t0.add"],
    "w.pull": ["t0.columns"],
    "t0.cores": ["w.pull"],
    "t1.columns": ["t0.cores"],
    "c00.dots": ["t1.columns"],
    "t1.cores": ["c00.dots"],
    "c01.dots": ["c00.sum"],
    "c10.dots": ["c01.sum"],
    "c00.hidden": ["c10.dots"],
    "c10.sum": ["c00.halves"],
    "c01.hidden": ["c10.sum"],
    "c11.dots": ["c01.hidden"],
    "c00.columns": ["c11.dots"],
    "c01.halves": ["c00.columns"],
    "c10.hidden": ["c01.halves"],
    "c11.sum": ["c10.hidden"],
    "c01.columns": ["c11.sum"],
    "c00.cores": ["c01.columns"],
    "c10.halves": ["c00.cores"],
    "c11.hidden": ["c10.halves"],
    "c00.down": ["c11.hidden"],
    "c01.cores": ["c00.down"],
    "c10.columns": ["c01.cores"],
    "c01.down": ["c10.columns"],
    "c11.halves": ["c01.down"],
    "c10.cores": ["c11.halves"],
    "c11.columns": ["c10.down"],
    "b0.total": ["c11.columns"],
    "c11.cores": ["b0.total"],
    "c11.down": ["b0.total"],
    "b1.total": ["c11.down"],
}


def dot(a, b):
    return jnp.dot(a, b, preferred_element_type=jnp.float32)


def flip(value, axis, bit):
    count = lax.axis_size(axis)
    return lax.ppermute(value, axis, [(i, i ^ bit) for i in range(count)])


def pull_kernel(first, end, tick_ref, gate_ref, up_ref, gate_here, up_here, sems):
    del tick_ref
    columns = pl.ds(first, end - first)
    copies = [
        pltpu.make_async_copy(source.at[:, columns], here, sems.at[i])
        for i, (source, here) in enumerate(((gate_ref, gate_here), (up_ref, up_here)))
    ]
    for copy in copies:
        copy.start()
    for copy in copies:
        copy.wait()


def pull(gate_weight, up_weight, first, end, tick):
    far = pl.BlockSpec(memory_space=pltpu.HBM)
    near = pl.BlockSpec(memory_space=pltpu.VMEM)
    here = pltpu.VMEM((gate_weight.shape[0], end - first), gate_weight.dtype)
    return pl.pallas_call(
        functools.partial(pull_kernel, first, end),
        in_specs=[pl.BlockSpec(memory_space=pltpu.SMEM), far, far],
        out_specs=[near, near],
        out_shape=[here, here],
        scratch_shapes=[pltpu.SemaphoreType.DMA((2,))],
        compiler_params=pltpu.CompilerParams(
            vmem_limit_bytes=4 * gate_weight.shape[0] * (end - first) + 2**20
        ),
        cost_estimate=pl.CostEstimate(flops=0, bytes_accessed=0, transcendentals=0),
    )(
        tick,
        pltpu.with_memory_space_constraint(gate_weight, pltpu.HBM),
        pltpu.with_memory_space_constraint(up_weight, pltpu.HBM),
    )


def stationary(tokens, lengths, gate_weight, up_weight, down_weight):
    slots, width = tokens.shape
    units = gate_weight.shape[1]
    col_count = lax.axis_size("col")
    c = lax.axis_index("col")
    r = lax.axis_index("row")
    x, k, zh, zl = c // 2, c % 2, r // 2, r % 2
    quarter = slots // 2
    piece = quarter // HALVES
    half = 2 * piece
    spans = []
    for sizes in PARTS:
        ends = [0]
        for size in sizes:
            ends.append(ends[-1] + units * size // sum(sizes))
        spans.append(list(zip(ends[:-1], ends[1:])))

    rows = jnp.arange(lengths.shape[0], dtype=jnp.int32)[None]
    slot = jnp.arange(slots, dtype=jnp.int32)[None]
    here = (c ^ jnp.arange(2, dtype=jnp.int32))[:, None]
    first = jnp.sum(jnp.where(rows < here, lengths[None], 0), axis=1, keepdims=True)
    count = jnp.sum(jnp.where(rows == here, lengths[None], 0), axis=1, keepdims=True)
    places = jnp.where(slot < count, slot + first, -1)
    inside = jnp.arange(piece, dtype=jnp.int32)

    def mine_of(c):
        both = jnp.concatenate([inside + quarter * c, inside + quarter * (c ^ 2)])
        return [both + h * piece for h in range(HALVES)]

    mine = mine_of(c)

    devices = [(i // col_count, i % col_count) for i in range(lax.axis_size("row") * col_count)]

    def move(value, where_to):
        pairs = []
        for i, (row, col) in enumerate(devices):
            to = where_to(row // 2, row % 2, col // 2, col % 2)
            if to is not None:
                to_zh, to_zl, to_x, to_k = to
                pairs.append((i, (to_zh * 2 + to_zl) * col_count + to_x * 2 + to_k))
        return lax.ppermute(value, ("row", "col"), pairs)

    def one_step(value, stay, first_to, second_to):
        first, second = move(value, first_to), move(value, second_to)

        def finish(value):
            return jnp.concatenate(
                [jnp.where(stay, value, first), jnp.where(stay, first, second)], axis=0
            )

        return finish

    def to_cores(value):
        return one_step(
            value,
            zl == k,
            lambda zh, zl, x, k: (zh, 1 - zl, x, k) if k == zl else (zh, zl, x, 1 - k),
            lambda zh, zl, x, k: None if k == zl else (zh, 1 - zl, x, 1 - k),
        )

    sibling = flip(tokens, "col", 1)
    seen = {}

    def ordered(step, value):
        for name in EDGES.get(step, ()):
            while name not in seen:
                advance(name.split(".")[0])
        others = [seen[name] for name in EDGES.get(step, ())]
        return lax.optimization_barrier((value, *others))[0] if others else value

    def issued(step, value):
        seen[step] = value
        return value

    def swap_x(value):
        return flip(value, "col", 2)

    def spread_steps(name, value):
        other = flip(value, "row", 2)
        yield
        other = ordered(name + ".halves", other)
        keep = jnp.where(zh == x, value, other)
        send = issued(name + ".halves", jnp.where(zh == x, other, value))
        got = swap_x(send)
        yield
        got = ordered(name + ".columns", got)
        pair = issued(name + ".columns", jnp.concatenate([keep, got], axis=0))
        finish = to_cores(pair)
        yield
        return issued(name + ".cores", finish(ordered(name + ".cores", pair)))

    def pick_steps(name, h):
        spots = ordered(name + ".pick", mine[h])
        own = spots[:, None] == places[0][None]
        sib = spots[:, None] == places[1][None]
        rows = dot(own.astype(jnp.bfloat16), tokens) + dot(sib.astype(jnp.bfloat16), sibling)
        rows = issued(name + ".pick", rows.astype(jnp.bfloat16))
        got = swap_x(rows[piece:])
        yield
        return issued(name + ".add", ordered(name + ".add", rows[:piece]) + got)

    pulled = []

    def pull_steps():
        tick = ordered("w.pull", lengths)
        pulled.extend(pull(gate_weight, up_weight, *spans[0][0], tick))
        issued("w.pull", pulled[0])
        return None
        yield

    def half_steps(name, h):
        own = yield from pick_steps(name, h)
        return (yield from spread_steps(name, own))

    def chunk_steps(name, h, i):
        full = result("t" + str(h))
        part = slice(*spans[h][i])
        full = ordered(name + ".dots", full)
        if (h, i) == (0, 0):
            result("w")
            gate, up = dot(full, pulled[0]), dot(full, pulled[1])
        else:
            gate, up = dot(full, gate_weight[:, part]), dot(full, up_weight[:, part])
        send = issued(name + ".dots", jnp.stack([gate[half:], up[half:]]).astype(jnp.bfloat16))
        got = issued(name + ".cores_swapped", flip(send, "col", 1))
        yield
        got = ordered(name + ".sum", got)
        gate, up = gate[:half] + got[0], up[:half] + got[1]
        send = issued(name + ".sum", jnp.stack([gate[piece:], up[piece:]]).astype(jnp.bfloat16))
        got = swap_x(send)
        yield
        got = ordered(name + ".hidden", got)
        gate, up = gate[:piece] + got[0], up[:piece] + got[1]
        hidden = issued(name + ".hidden", (jax.nn.silu(gate) * up).astype(jnp.bfloat16))
        whole = yield from spread_steps(name, hidden)
        yield
        whole = ordered(name + ".down", whole)
        return issued(name + ".down", dot(whole, down_weight[part]))

    def branch_steps(name, h):
        parts = [result("c" + str(h) + str(i)) for i in range(len(spans[h]))]
        branch = issued(name + ".branch", sum(parts[1:], parts[0]))
        got = flip(branch[half:].astype(jnp.bfloat16), "col", 1)
        yield
        total = issued(name + ".total", branch[:half] + ordered(name + ".total", got))
        got = swap_x(total.astype(jnp.bfloat16))
        yield
        got = ordered(name + ".all", got)
        return issued(name + ".all", total + jnp.concatenate([got[piece:], got[:piece]], axis=0))

    chains = {"w": pull_steps()}
    results = {}
    for h in range(HALVES):
        chains["t" + str(h)] = half_steps("t" + str(h), h)
        for i in range(len(spans[h])):
            chains["c" + str(h) + str(i)] = chunk_steps("c" + str(h) + str(i), h, i)
        chains["b" + str(h)] = branch_steps("b" + str(h), h)

    def advance(name):
        try:
            next(chains[name])
        except StopIteration as stop:
            results[name] = stop.value

    def result(name):
        while name not in results:
            advance(name)
        return results[name]

    for name in EDGES:
        while name not in seen:
            advance(name.split(".")[0])
    for h in range(HALVES):
        result("b" + str(h))

    totals = [results["b" + str(h)] for h in range(HALVES)]
    theirs = [flip(total.astype(jnp.bfloat16), "col", 1) for total in totals]
    put = places[0][:, None] == jnp.concatenate(mine)[None]
    moved = jnp.dot(
        put.astype(jnp.float32), jnp.concatenate(totals), precision=lax.Precision.HIGHEST
    )
    put = places[0][:, None] == jnp.concatenate(mine_of(c ^ 1))[None]
    moved = moved + dot(put.astype(jnp.bfloat16), jnp.concatenate(theirs))
    used = (places[0] >= 0)[:, None]
    return jnp.where(used, tokens.astype(jnp.float32) + moved, 0.0).astype(jnp.bfloat16)


def general(tokens, lengths, gate_weight, up_weight, down_weight):
    c = lax.axis_index("col")
    slots = tokens.shape[0]
    whole = lax.all_gather(tokens, "row", axis=1, tiled=True)
    whole = lax.all_gather(whole, "col", axis=0, tiled=True)
    depth = gate_weight.shape[0]
    block = lax.dynamic_slice_in_dim(whole, c * depth, depth, axis=1)

    def summed(a, b):
        return lax.psum_scatter(dot(a, b), "col", scatter_dimension=0, tiled=True)

    hidden = (jax.nn.silu(summed(block, gate_weight)) * summed(block, up_weight)).astype(jnp.bfloat16)
    hidden = lax.all_gather(hidden, "row", axis=1, tiled=True)
    hidden = lax.all_gather(hidden, "col", axis=0, tiled=True)
    depth = down_weight.shape[0]
    branch = summed(lax.dynamic_slice_in_dim(hidden, c * depth, depth, axis=1), down_weight)
    valid = jnp.arange(slots, dtype=jnp.int32) < jnp.take(lengths, c)
    total = tokens.astype(jnp.float32) + branch
    return jnp.where(valid[:, None], total, jnp.float32(0.0)).astype(jnp.bfloat16)


def solution(mesh):
    square = mesh.shape["row"] == 4 and mesh.shape["col"] == 4
    in_specs = (
        P(("groups", "col"), "row"),
        P("groups"),
        P("col", "row"),
        P("col", "row"),
        P("col", "row"),
    )
    out_specs = P(("groups", "col"), "row")
    return jax.shard_map(
        stationary if square else general,
        mesh=mesh, in_specs=in_specs, out_specs=out_specs, check_vma=False,
    )
```

```python
import functools

import jax
import jax.numpy as jnp
from jax import lax
from jax.experimental import pallas as pl
from jax.experimental.pallas import tpu as pltpu
from jax.sharding import PartitionSpec as P

HALVES = 2
PARTS = ((14, 14), (18, 10))
EDGES = {
    "t1.pick": ["t0.add"],
    "w.pull": ["t0.columns"],
    "t0.cores": ["w.pull"],
    "t1.columns": ["t0.cores"],
    "c00.dots": ["t1.columns"],
    "t1.cores": ["c00.dots"],
    "c01.dots": ["c00.sum"],
    "c10.dots": ["c01.sum"],
    "c00.hidden": ["c11.dots"],
    "c10.sum": ["c00.halves"],
    "c01.hidden": ["c10.sum"],
    "c11.dots": ["c10.dots"],
    "c00.columns": ["c01.hidden"],
    "c01.halves": ["c00.columns"],
    "c10.hidden": ["c01.halves"],
    "c11.sum": ["c10.hidden"],
    "c01.columns": ["c11.sum"],
    "c00.cores": ["c01.columns"],
    "c10.halves": ["c00.cores"],
    "c11.hidden": ["c10.halves"],
    "c00.down": ["c11.hidden"],
    "c01.cores": ["c00.down"],
    "c10.columns": ["c01.cores"],
    "c01.down": ["c10.columns"],
    "c11.halves": ["c01.down"],
    "c10.cores": ["c11.halves"],
    "c11.columns": ["c10.down"],
    "b0.total": ["c11.columns"],
    "c11.cores": ["b0.total"],
    "c11.down": ["b0.total"],
    "b1.total": ["c11.down"],
}


def dot(a, b):
    return jnp.dot(a, b, preferred_element_type=jnp.float32)


def flip(value, axis, bit):
    count = lax.axis_size(axis)
    return lax.ppermute(value, axis, [(i, i ^ bit) for i in range(count)])


def pull_kernel(first, end, tick_ref, gate_ref, up_ref, gate_here, up_here, sems):
    del tick_ref
    columns = pl.ds(first, end - first)
    copies = [
        pltpu.make_async_copy(source.at[:, columns], here, sems.at[i])
        for i, (source, here) in enumerate(((gate_ref, gate_here), (up_ref, up_here)))
    ]
    for copy in copies:
        copy.start()
    for copy in copies:
        copy.wait()


def pull(gate_weight, up_weight, first, end, tick):
    far = pl.BlockSpec(memory_space=pltpu.HBM)
    near = pl.BlockSpec(memory_space=pltpu.VMEM)
    here = pltpu.VMEM((gate_weight.shape[0], end - first), gate_weight.dtype)
    return pl.pallas_call(
        functools.partial(pull_kernel, first, end),
        in_specs=[pl.BlockSpec(memory_space=pltpu.SMEM), far, far],
        out_specs=[near, near],
        out_shape=[here, here],
        scratch_shapes=[pltpu.SemaphoreType.DMA((2,))],
        compiler_params=pltpu.CompilerParams(
            vmem_limit_bytes=4 * gate_weight.shape[0] * (end - first) + 2**20
        ),
        cost_estimate=pl.CostEstimate(flops=0, bytes_accessed=0, transcendentals=0),
    )(
        tick,
        pltpu.with_memory_space_constraint(gate_weight, pltpu.HBM),
        pltpu.with_memory_space_constraint(up_weight, pltpu.HBM),
    )


def stationary(tokens, lengths, gate_weight, up_weight, down_weight):
    slots, width = tokens.shape
    units = gate_weight.shape[1]
    col_count = lax.axis_size("col")
    c = lax.axis_index("col")
    r = lax.axis_index("row")
    x, k, zh, zl = c // 2, c % 2, r // 2, r % 2
    quarter = slots // 2
    piece = quarter // HALVES
    half = 2 * piece
    spans = []
    for sizes in PARTS:
        ends = [0]
        for size in sizes:
            ends.append(ends[-1] + units * size // sum(sizes))
        spans.append(list(zip(ends[:-1], ends[1:])))

    rows = jnp.arange(lengths.shape[0], dtype=jnp.int32)[None]
    slot = jnp.arange(slots, dtype=jnp.int32)[None]
    here = (c ^ jnp.arange(2, dtype=jnp.int32))[:, None]
    first = jnp.sum(jnp.where(rows < here, lengths[None], 0), axis=1, keepdims=True)
    count = jnp.sum(jnp.where(rows == here, lengths[None], 0), axis=1, keepdims=True)
    places = jnp.where(slot < count, slot + first, -1)
    inside = jnp.arange(piece, dtype=jnp.int32)

    def mine_of(c):
        both = jnp.concatenate([inside + quarter * c, inside + quarter * (c ^ 2)])
        return [both + h * piece for h in range(HALVES)]

    mine = mine_of(c)

    devices = [(i // col_count, i % col_count) for i in range(lax.axis_size("row") * col_count)]

    def move(value, where_to):
        pairs = []
        for i, (row, col) in enumerate(devices):
            to = where_to(row // 2, row % 2, col // 2, col % 2)
            if to is not None:
                to_zh, to_zl, to_x, to_k = to
                pairs.append((i, (to_zh * 2 + to_zl) * col_count + to_x * 2 + to_k))
        return lax.ppermute(value, ("row", "col"), pairs)

    def one_step(value, stay, first_to, second_to):
        first, second = move(value, first_to), move(value, second_to)

        def finish(value):
            return jnp.concatenate(
                [jnp.where(stay, value, first), jnp.where(stay, first, second)], axis=0
            )

        return finish

    def to_cores(value):
        return one_step(
            value,
            zl == k,
            lambda zh, zl, x, k: (zh, 1 - zl, x, k) if k == zl else (zh, zl, x, 1 - k),
            lambda zh, zl, x, k: None if k == zl else (zh, 1 - zl, x, 1 - k),
        )

    sibling = flip(tokens, "col", 1)
    seen = {}

    def ordered(step, value):
        for name in EDGES.get(step, ()):
            while name not in seen:
                advance(name.split(".")[0])
        others = [seen[name] for name in EDGES.get(step, ())]
        return lax.optimization_barrier((value, *others))[0] if others else value

    def issued(step, value):
        seen[step] = value
        return value

    def swap_x(value):
        return flip(value, "col", 2)

    def spread_steps(name, value):
        other = flip(value, "row", 2)
        yield
        other = ordered(name + ".halves", other)
        keep = jnp.where(zh == x, value, other)
        send = issued(name + ".halves", jnp.where(zh == x, other, value))
        got = swap_x(send)
        yield
        got = ordered(name + ".columns", got)
        pair = issued(name + ".columns", jnp.concatenate([keep, got], axis=0))
        finish = to_cores(pair)
        yield
        return issued(name + ".cores", finish(ordered(name + ".cores", pair)))

    def pick_steps(name, h):
        spots = ordered(name + ".pick", mine[h])
        own = spots[:, None] == places[0][None]
        sib = spots[:, None] == places[1][None]
        rows = dot(own.astype(jnp.bfloat16), tokens) + dot(sib.astype(jnp.bfloat16), sibling)
        rows = issued(name + ".pick", rows.astype(jnp.bfloat16))
        got = swap_x(rows[piece:])
        yield
        return issued(name + ".add", ordered(name + ".add", rows[:piece]) + got)

    pulled = []

    def pull_steps():
        tick = ordered("w.pull", lengths)
        pulled.extend(pull(gate_weight, up_weight, *spans[0][0], tick))
        issued("w.pull", pulled[0])
        return None
        yield

    def half_steps(name, h):
        own = yield from pick_steps(name, h)
        return (yield from spread_steps(name, own))

    def chunk_steps(name, h, i):
        full = result("t" + str(h))
        part = slice(*spans[h][i])
        full = ordered(name + ".dots", full)
        if (h, i) == (0, 0):
            result("w")
            gate, up = dot(full, pulled[0]), dot(full, pulled[1])
        else:
            gate, up = dot(full, gate_weight[:, part]), dot(full, up_weight[:, part])
        send = issued(name + ".dots", jnp.stack([gate[half:], up[half:]]).astype(jnp.bfloat16))
        got = issued(name + ".cores_swapped", flip(send, "col", 1))
        yield
        got = ordered(name + ".sum", got)
        gate, up = gate[:half] + got[0], up[:half] + got[1]
        send = issued(name + ".sum", jnp.stack([gate[piece:], up[piece:]]).astype(jnp.bfloat16))
        got = swap_x(send)
        yield
        got = ordered(name + ".hidden", got)
        gate, up = gate[:piece] + got[0], up[:piece] + got[1]
        hidden = issued(name + ".hidden", (jax.nn.silu(gate) * up).astype(jnp.bfloat16))
        whole = yield from spread_steps(name, hidden)
        yield
        whole = ordered(name + ".down", whole)
        return issued(name + ".down", dot(whole, down_weight[part]))

    def branch_steps(name, h):
        parts = [result("c" + str(h) + str(i)) for i in range(len(spans[h]))]
        branch = issued(name + ".branch", sum(parts[1:], parts[0]))
        got = flip(branch[half:].astype(jnp.bfloat16), "col", 1)
        yield
        total = issued(name + ".total", branch[:half] + ordered(name + ".total", got))
        got = swap_x(total.astype(jnp.bfloat16))
        yield
        got = ordered(name + ".all", got)
        return issued(name + ".all", total + jnp.concatenate([got[piece:], got[:piece]], axis=0))

    chains = {"w": pull_steps()}
    results = {}
    for h in range(HALVES):
        chains["t" + str(h)] = half_steps("t" + str(h), h)
        for i in range(len(spans[h])):
            chains["c" + str(h) + str(i)] = chunk_steps("c" + str(h) + str(i), h, i)
        chains["b" + str(h)] = branch_steps("b" + str(h), h)

    def advance(name):
        try:
            next(chains[name])
        except StopIteration as stop:
            results[name] = stop.value

    def result(name):
        while name not in results:
            advance(name)
        return results[name]

    for name in EDGES:
        while name not in seen:
            advance(name.split(".")[0])
    for h in range(HALVES):
        result("b" + str(h))

    totals = [results["b" + str(h)] for h in range(HALVES)]
    theirs = [flip(total.astype(jnp.bfloat16), "col", 1) for total in totals]
    put = places[0][:, None] == jnp.concatenate(mine)[None]
    moved = jnp.dot(
        put.astype(jnp.float32), jnp.concatenate(totals), precision=lax.Precision.HIGHEST
    )
    put = places[0][:, None] == jnp.concatenate(mine_of(c ^ 1))[None]
    moved = moved + dot(put.astype(jnp.bfloat16), jnp.concatenate(theirs))
    used = (places[0] >= 0)[:, None]
    return jnp.where(used, tokens.astype(jnp.float32) + moved, 0.0).astype(jnp.bfloat16)


def general(tokens, lengths, gate_weight, up_weight, down_weight):
    c = lax.axis_index("col")
    slots = tokens.shape[0]
    whole = lax.all_gather(tokens, "row", axis=1, tiled=True)
    whole = lax.all_gather(whole, "col", axis=0, tiled=True)
    depth = gate_weight.shape[0]
    block = lax.dynamic_slice_in_dim(whole, c * depth, depth, axis=1)

    def summed(a, b):
        return lax.psum_scatter(dot(a, b), "col", scatter_dimension=0, tiled=True)

    hidden = (jax.nn.silu(summed(block, gate_weight)) * summed(block, up_weight)).astype(jnp.bfloat16)
    hidden = lax.all_gather(hidden, "row", axis=1, tiled=True)
    hidden = lax.all_gather(hidden, "col", axis=0, tiled=True)
    depth = down_weight.shape[0]
    branch = summed(lax.dynamic_slice_in_dim(hidden, c * depth, depth, axis=1), down_weight)
    valid = jnp.arange(slots, dtype=jnp.int32) < jnp.take(lengths, c)
    total = tokens.astype(jnp.float32) + branch
    return jnp.where(valid[:, None], total, jnp.float32(0.0)).astype(jnp.bfloat16)


def solution(mesh):
    square = mesh.shape["row"] == 4 and mesh.shape["col"] == 4
    in_specs = (
        P(("groups", "col"), "row"),
        P("groups"),
        P("col", "row"),
        P("col", "row"),
        P("col", "row"),
    )
    out_specs = P(("groups", "col"), "row")
    return jax.shard_map(
        stationary if square else general,
        mesh=mesh, in_specs=in_specs, out_specs=out_specs, check_vma=False,
    )
```

```python
import functools

import jax
import jax.numpy as jnp
from jax import lax
from jax.experimental import pallas as pl
from jax.experimental.pallas import tpu as pltpu
from jax.sharding import PartitionSpec as P

HALVES = 2
PARTS = ((14, 14), (18, 10))
EDGES = {
    "t1.pick": ["t0.add"],
    "w.pull": ["t0.columns"],
    "t0.cores": ["w.pull"],
    "t1.columns": ["t0.cores"],
    "c00.dots": ["t1.columns"],
    "t1.cores": ["c00.dots"],
    "c01.dots": ["c00.sum"],
    "c10.dots": ["c01.sum"],
    "c00.hidden": ["c11.dots"],
    "c10.sum": ["c00.halves"],
    "c01.hidden": ["c10.sum"],
    "c11.dots": ["c10.dots"],
    "c00.columns": ["c01.hidden"],
    "c01.halves": ["c00.columns"],
    "c10.hidden": ["c01.halves"],
    "c11.sum": ["c10.hidden"],
    "c01.columns": ["c11.sum"],
    "c00.cores": ["c01.columns"],
    "c10.halves": ["c00.cores"],
    "c11.hidden": ["c10.halves"],
    "c00.down": ["c11.hidden"],
    "c01.cores": ["c00.down"],
    "c10.columns": ["c01.cores"],
    "c01.down": ["c10.columns"],
    "c11.halves": ["c01.down"],
    "c10.cores": ["c11.halves"],
    "c11.columns": ["c10.down"],
    "b0.total": ["c11.columns"],
    "c11.cores": ["b0.total"],
    "c11.down": ["b0.total"],
    "b1.total": ["c11.down"],
    "d.pull": ["c00.hidden"],
    "c00.halves": ["d.pull"],
}


def dot(a, b):
    return jnp.dot(a, b, preferred_element_type=jnp.float32)


def flip(value, axis, bit):
    count = lax.axis_size(axis)
    return lax.ppermute(value, axis, [(i, i ^ bit) for i in range(count)])


def pull_kernel(first, end, tick_ref, *refs):
    del tick_ref
    *refs, sems = refs
    count = len(refs) // 2
    columns = pl.ds(first, end - first)
    copies = [
        pltpu.make_async_copy(source.at[:, columns], here, sems.at[i])
        for i, (source, here) in enumerate(zip(refs[:count], refs[count:]))
    ]
    for copy in copies:
        copy.start()
    for copy in copies:
        copy.wait()


def pull(weights, first, end, tick):
    far = pl.BlockSpec(memory_space=pltpu.HBM)
    near = pl.BlockSpec(memory_space=pltpu.VMEM)
    here = [pltpu.VMEM((weight.shape[0], end - first), weight.dtype) for weight in weights]
    size = sum(2 * weight.shape[0] * (end - first) for weight in weights)
    return pl.pallas_call(
        functools.partial(pull_kernel, first, end),
        in_specs=[pl.BlockSpec(memory_space=pltpu.SMEM)] + [far] * len(weights),
        out_specs=[near] * len(weights),
        out_shape=here,
        scratch_shapes=[pltpu.SemaphoreType.DMA((len(weights),))],
        compiler_params=pltpu.CompilerParams(vmem_limit_bytes=size + 2**20),
        cost_estimate=pl.CostEstimate(flops=0, bytes_accessed=0, transcendentals=0),
    )(tick, *[pltpu.with_memory_space_constraint(weight, pltpu.HBM) for weight in weights])


def stationary(tokens, lengths, gate_weight, up_weight, down_weight):
    slots, width = tokens.shape
    units = gate_weight.shape[1]
    col_count = lax.axis_size("col")
    c = lax.axis_index("col")
    r = lax.axis_index("row")
    x, k, zh, zl = c // 2, c % 2, r // 2, r % 2
    quarter = slots // 2
    piece = quarter // HALVES
    half = 2 * piece
    spans = []
    for sizes in PARTS:
        ends = [0]
        for size in sizes:
            ends.append(ends[-1] + units * size // sum(sizes))
        spans.append(list(zip(ends[:-1], ends[1:])))

    rows = jnp.arange(lengths.shape[0], dtype=jnp.int32)[None]
    slot = jnp.arange(slots, dtype=jnp.int32)[None]
    here = (c ^ jnp.arange(2, dtype=jnp.int32))[:, None]
    first = jnp.sum(jnp.where(rows < here, lengths[None], 0), axis=1, keepdims=True)
    count = jnp.sum(jnp.where(rows == here, lengths[None], 0), axis=1, keepdims=True)
    places = jnp.where(slot < count, slot + first, -1)
    inside = jnp.arange(piece, dtype=jnp.int32)

    def mine_of(c):
        both = jnp.concatenate([inside + quarter * c, inside + quarter * (c ^ 2)])
        return [both + h * piece for h in range(HALVES)]

    mine = mine_of(c)

    devices = [(i // col_count, i % col_count) for i in range(lax.axis_size("row") * col_count)]

    def move(value, where_to):
        pairs = []
        for i, (row, col) in enumerate(devices):
            to = where_to(row // 2, row % 2, col // 2, col % 2)
            if to is not None:
                to_zh, to_zl, to_x, to_k = to
                pairs.append((i, (to_zh * 2 + to_zl) * col_count + to_x * 2 + to_k))
        return lax.ppermute(value, ("row", "col"), pairs)

    def one_step(value, stay, first_to, second_to):
        first, second = move(value, first_to), move(value, second_to)

        def finish(value):
            return jnp.concatenate(
                [jnp.where(stay, value, first), jnp.where(stay, first, second)], axis=0
            )

        return finish

    def to_cores(value):
        return one_step(
            value,
            zl == k,
            lambda zh, zl, x, k: (zh, 1 - zl, x, k) if k == zl else (zh, zl, x, 1 - k),
            lambda zh, zl, x, k: None if k == zl else (zh, 1 - zl, x, 1 - k),
        )

    sibling = flip(tokens, "col", 1)
    seen = {}

    def ordered(step, value):
        for name in EDGES.get(step, ()):
            while name not in seen:
                advance(name.split(".")[0])
        others = [seen[name] for name in EDGES.get(step, ())]
        return lax.optimization_barrier((value, *others))[0] if others else value

    def issued(step, value):
        seen[step] = value
        return value

    def swap_x(value):
        return flip(value, "col", 2)

    def spread_steps(name, value):
        other = flip(value, "row", 2)
        yield
        other = ordered(name + ".halves", other)
        keep = jnp.where(zh == x, value, other)
        send = issued(name + ".halves", jnp.where(zh == x, other, value))
        got = swap_x(send)
        yield
        got = ordered(name + ".columns", got)
        pair = issued(name + ".columns", jnp.concatenate([keep, got], axis=0))
        finish = to_cores(pair)
        yield
        return issued(name + ".cores", finish(ordered(name + ".cores", pair)))

    def pick_steps(name, h):
        spots = ordered(name + ".pick", mine[h])
        own = spots[:, None] == places[0][None]
        sib = spots[:, None] == places[1][None]
        rows = dot(own.astype(jnp.bfloat16), tokens) + dot(sib.astype(jnp.bfloat16), sibling)
        rows = issued(name + ".pick", rows.astype(jnp.bfloat16))
        got = swap_x(rows[piece:])
        yield
        return issued(name + ".add", ordered(name + ".add", rows[:piece]) + got)

    pulled = {}

    def pull_steps(name, weights, first, end):
        tick = ordered(name + ".pull", lengths)
        pulled[name] = pull(weights, first, end, tick)
        issued(name + ".pull", pulled[name][0])
        return None
        yield

    def half_steps(name, h):
        own = yield from pick_steps(name, h)
        return (yield from spread_steps(name, own))

    def chunk_steps(name, h, i):
        full = result("t" + str(h))
        part = slice(*spans[h][i])
        full = ordered(name + ".dots", full)
        if (h, i) == (0, 0):
            result("w")
            gate, up = (dot(full, weight) for weight in pulled["w"])
        else:
            gate, up = dot(full, gate_weight[:, part]), dot(full, up_weight[:, part])
        send = issued(name + ".dots", jnp.stack([gate[half:], up[half:]]).astype(jnp.bfloat16))
        got = issued(name + ".cores_swapped", flip(send, "col", 1))
        yield
        got = ordered(name + ".sum", got)
        gate, up = gate[:half] + got[0], up[:half] + got[1]
        send = issued(name + ".sum", jnp.stack([gate[piece:], up[piece:]]).astype(jnp.bfloat16))
        got = swap_x(send)
        yield
        got = ordered(name + ".hidden", got)
        gate, up = gate[:piece] + got[0], up[:piece] + got[1]
        hidden = issued(name + ".hidden", (jax.nn.silu(gate) * up).astype(jnp.bfloat16))
        whole = yield from spread_steps(name, hidden)
        yield
        result("d")
        whole = ordered(name + ".down", whole)
        return issued(name + ".down", dot(whole, pulled["d"][0][part]))

    def branch_steps(name, h):
        parts = [result("c" + str(h) + str(i)) for i in range(len(spans[h]))]
        branch = issued(name + ".branch", sum(parts[1:], parts[0]))
        got = flip(branch[half:].astype(jnp.bfloat16), "col", 1)
        yield
        total = issued(name + ".total", branch[:half] + ordered(name + ".total", got))
        got = swap_x(total.astype(jnp.bfloat16))
        yield
        got = ordered(name + ".all", got)
        return issued(name + ".all", total + jnp.concatenate([got[piece:], got[:piece]], axis=0))

    chains = {
        "w": pull_steps("w", (gate_weight, up_weight), *spans[0][0]),
        "d": pull_steps("d", (down_weight,), 0, down_weight.shape[1]),
    }
    results = {}
    for h in range(HALVES):
        chains["t" + str(h)] = half_steps("t" + str(h), h)
        for i in range(len(spans[h])):
            chains["c" + str(h) + str(i)] = chunk_steps("c" + str(h) + str(i), h, i)
        chains["b" + str(h)] = branch_steps("b" + str(h), h)

    def advance(name):
        try:
            next(chains[name])
        except StopIteration as stop:
            results[name] = stop.value

    def result(name):
        while name not in results:
            advance(name)
        return results[name]

    for name in EDGES:
        while name not in seen:
            advance(name.split(".")[0])
    for h in range(HALVES):
        result("b" + str(h))

    totals = [results["b" + str(h)] for h in range(HALVES)]
    theirs = [flip(total.astype(jnp.bfloat16), "col", 1) for total in totals]
    put = places[0][:, None] == jnp.concatenate(mine)[None]
    moved = jnp.dot(
        put.astype(jnp.float32), jnp.concatenate(totals), precision=lax.Precision.HIGHEST
    )
    put = places[0][:, None] == jnp.concatenate(mine_of(c ^ 1))[None]
    moved = moved + dot(put.astype(jnp.bfloat16), jnp.concatenate(theirs))
    used = (places[0] >= 0)[:, None]
    return jnp.where(used, tokens.astype(jnp.float32) + moved, 0.0).astype(jnp.bfloat16)


def general(tokens, lengths, gate_weight, up_weight, down_weight):
    c = lax.axis_index("col")
    slots = tokens.shape[0]
    whole = lax.all_gather(tokens, "row", axis=1, tiled=True)
    whole = lax.all_gather(whole, "col", axis=0, tiled=True)
    depth = gate_weight.shape[0]
    block = lax.dynamic_slice_in_dim(whole, c * depth, depth, axis=1)

    def summed(a, b):
        return lax.psum_scatter(dot(a, b), "col", scatter_dimension=0, tiled=True)

    hidden = (jax.nn.silu(summed(block, gate_weight)) * summed(block, up_weight)).astype(jnp.bfloat16)
    hidden = lax.all_gather(hidden, "row", axis=1, tiled=True)
    hidden = lax.all_gather(hidden, "col", axis=0, tiled=True)
    depth = down_weight.shape[0]
    branch = summed(lax.dynamic_slice_in_dim(hidden, c * depth, depth, axis=1), down_weight)
    valid = jnp.arange(slots, dtype=jnp.int32) < jnp.take(lengths, c)
    total = tokens.astype(jnp.float32) + branch
    return jnp.where(valid[:, None], total, jnp.float32(0.0)).astype(jnp.bfloat16)


def solution(mesh):
    square = mesh.shape["row"] == 4 and mesh.shape["col"] == 4
    in_specs = (
        P(("groups", "col"), "row"),
        P("groups"),
        P("col", "row"),
        P("col", "row"),
        P("col", "row"),
    )
    out_specs = P(("groups", "col"), "row")
    return jax.shard_map(
        stationary if square else general,
        mesh=mesh, in_specs=in_specs, out_specs=out_specs, check_vma=False,
    )
```

```python
import functools

import jax
import jax.numpy as jnp
from jax import lax
from jax.experimental import pallas as pl
from jax.experimental.pallas import tpu as pltpu
from jax.sharding import PartitionSpec as P

HALVES = 2
PARTS = ((14, 14), (18, 10))
EDGES = {
    "t1.pick": ["t0.add"],
    "w.pull": ["t0.columns"],
    "t0.cores": ["w.pull"],
    "t1.columns": ["t0.cores"],
    "c00.dots": ["t1.columns"],
    "t1.cores": ["c00.dots"],
    "c01.dots": ["c00.sum"],
    "c10.dots": ["c01.sum"],
    "c00.hidden": ["c10.dots"],
    "c10.sum": ["c00.halves"],
    "c01.hidden": ["c10.sum"],
    "c11.dots": ["c01.hidden"],
    "c00.columns": ["c11.dots"],
    "c01.halves": ["c00.columns"],
    "c10.hidden": ["c01.halves"],
    "c11.sum": ["c10.hidden"],
    "c01.columns": ["c11.sum"],
    "c00.cores": ["c01.columns"],
    "c10.halves": ["c00.cores"],
    "c11.hidden": ["c10.halves"],
    "c00.down": ["c11.hidden"],
    "c01.cores": ["c00.down"],
    "c10.columns": ["c01.cores"],
    "c01.down": ["c10.columns"],
    "c11.halves": ["c01.down"],
    "c10.cores": ["b0.total"],
    "c11.columns": ["c10.down"],
    "b0.total": ["c11.halves"],
    "b1.total": ["c11.down"],
}


def dot(a, b):
    return jnp.dot(a, b, preferred_element_type=jnp.float32)


def flip(value, axis, bit):
    count = lax.axis_size(axis)
    return lax.ppermute(value, axis, [(i, i ^ bit) for i in range(count)])


def pull_kernel(first, end, tick_ref, gate_ref, up_ref, gate_here, up_here, sems):
    del tick_ref
    columns = pl.ds(first, end - first)
    copies = [
        pltpu.make_async_copy(source.at[:, columns], here, sems.at[i])
        for i, (source, here) in enumerate(((gate_ref, gate_here), (up_ref, up_here)))
    ]
    for copy in copies:
        copy.start()
    for copy in copies:
        copy.wait()


def pull(gate_weight, up_weight, first, end, tick):
    far = pl.BlockSpec(memory_space=pltpu.HBM)
    near = pl.BlockSpec(memory_space=pltpu.VMEM)
    here = pltpu.VMEM((gate_weight.shape[0], end - first), gate_weight.dtype)
    return pl.pallas_call(
        functools.partial(pull_kernel, first, end),
        in_specs=[pl.BlockSpec(memory_space=pltpu.SMEM), far, far],
        out_specs=[near, near],
        out_shape=[here, here],
        scratch_shapes=[pltpu.SemaphoreType.DMA((2,))],
        compiler_params=pltpu.CompilerParams(
            vmem_limit_bytes=4 * gate_weight.shape[0] * (end - first) + 2**20
        ),
        cost_estimate=pl.CostEstimate(flops=0, bytes_accessed=0, transcendentals=0),
    )(
        tick,
        pltpu.with_memory_space_constraint(gate_weight, pltpu.HBM),
        pltpu.with_memory_space_constraint(up_weight, pltpu.HBM),
    )


def stationary(tokens, lengths, gate_weight, up_weight, down_weight):
    slots, width = tokens.shape
    units = gate_weight.shape[1]
    col_count = lax.axis_size("col")
    c = lax.axis_index("col")
    r = lax.axis_index("row")
    x, k, zh, zl = c // 2, c % 2, r // 2, r % 2
    quarter = slots // 2
    piece = quarter // HALVES
    half = 2 * piece
    spans = []
    for sizes in PARTS:
        ends = [0]
        for size in sizes:
            ends.append(ends[-1] + units * size // sum(sizes))
        spans.append(list(zip(ends[:-1], ends[1:])))

    rows = jnp.arange(lengths.shape[0], dtype=jnp.int32)[None]
    slot = jnp.arange(slots, dtype=jnp.int32)[None]
    here = (c ^ jnp.arange(2, dtype=jnp.int32))[:, None]
    first = jnp.sum(jnp.where(rows < here, lengths[None], 0), axis=1, keepdims=True)
    count = jnp.sum(jnp.where(rows == here, lengths[None], 0), axis=1, keepdims=True)
    places = jnp.where(slot < count, slot + first, -1)
    inside = jnp.arange(piece, dtype=jnp.int32)

    def mine_of(c):
        both = jnp.concatenate([inside + quarter * c, inside + quarter * (c ^ 2)])
        return [both + h * piece for h in range(HALVES)]

    mine = mine_of(c)

    devices = [(i // col_count, i % col_count) for i in range(lax.axis_size("row") * col_count)]

    def move(value, where_to):
        pairs = []
        for i, (row, col) in enumerate(devices):
            to = where_to(row // 2, row % 2, col // 2, col % 2)
            if to is not None:
                to_zh, to_zl, to_x, to_k = to
                pairs.append((i, (to_zh * 2 + to_zl) * col_count + to_x * 2 + to_k))
        return lax.ppermute(value, ("row", "col"), pairs)

    def one_step(value, stay, first_to, second_to):
        first, second = move(value, first_to), move(value, second_to)

        def finish(value):
            return jnp.concatenate(
                [jnp.where(stay, value, first), jnp.where(stay, first, second)], axis=0
            )

        return finish

    def to_cores(value):
        return one_step(
            value,
            zl == k,
            lambda zh, zl, x, k: (zh, 1 - zl, x, k) if k == zl else (zh, zl, x, 1 - k),
            lambda zh, zl, x, k: None if k == zl else (zh, 1 - zl, x, 1 - k),
        )

    sibling = flip(tokens, "col", 1)
    seen = {}

    def ordered(step, value):
        for name in EDGES.get(step, ()):
            while name not in seen:
                advance(name.split(".")[0])
        others = [seen[name] for name in EDGES.get(step, ())]
        return lax.optimization_barrier((value, *others))[0] if others else value

    def issued(step, value):
        seen[step] = value
        return value

    def swap_x(value):
        return flip(value, "col", 2)

    def spread_steps(name, value):
        other = flip(value, "row", 2)
        yield
        other = ordered(name + ".halves", other)
        keep = jnp.where(zh == x, value, other)
        send = issued(name + ".halves", jnp.where(zh == x, other, value))
        got = swap_x(send)
        yield
        got = ordered(name + ".columns", got)
        pair = issued(name + ".columns", jnp.concatenate([keep, got], axis=0))
        finish = to_cores(pair)
        yield
        return issued(name + ".cores", finish(ordered(name + ".cores", pair)))

    def pick_steps(name, h):
        spots = ordered(name + ".pick", mine[h])
        own = spots[:, None] == places[0][None]
        sib = spots[:, None] == places[1][None]
        rows = dot(own.astype(jnp.bfloat16), tokens) + dot(sib.astype(jnp.bfloat16), sibling)
        rows = issued(name + ".pick", rows.astype(jnp.bfloat16))
        got = swap_x(rows[piece:])
        yield
        return issued(name + ".add", ordered(name + ".add", rows[:piece]) + got)

    pulled = []

    def pull_steps():
        tick = ordered("w.pull", lengths)
        pulled.extend(pull(gate_weight, up_weight, *spans[0][0], tick))
        issued("w.pull", pulled[0])
        return None
        yield

    def half_steps(name, h):
        own = yield from pick_steps(name, h)
        return (yield from spread_steps(name, own))

    def chunk_steps(name, h, i):
        full = result("t" + str(h))
        part = slice(*spans[h][i])
        full = ordered(name + ".dots", full)
        if (h, i) == (0, 0):
            result("w")
            gate, up = dot(full, pulled[0]), dot(full, pulled[1])
        else:
            gate, up = dot(full, gate_weight[:, part]), dot(full, up_weight[:, part])
        send = issued(name + ".dots", jnp.stack([gate[half:], up[half:]]).astype(jnp.bfloat16))
        got = issued(name + ".cores_swapped", flip(send, "col", 1))
        yield
        got = ordered(name + ".sum", got)
        gate, up = gate[:half] + got[0], up[:half] + got[1]
        send = issued(name + ".sum", jnp.stack([gate[piece:], up[piece:]]).astype(jnp.bfloat16))
        got = swap_x(send)
        yield
        got = ordered(name + ".hidden", got)
        gate, up = gate[:piece] + got[0], up[:piece] + got[1]
        hidden = issued(name + ".hidden", (jax.nn.silu(gate) * up).astype(jnp.bfloat16))
        whole = yield from spread_steps(name, hidden)
        yield
        whole = ordered(name + ".down", whole)
        return issued(name + ".down", dot(whole, down_weight[part]))

    def branch_steps(name, h):
        parts = [result("c" + str(h) + str(i)) for i in range(len(spans[h]))]
        branch = issued(name + ".branch", sum(parts[1:], parts[0]))
        got = flip(branch[half:].astype(jnp.bfloat16), "col", 1)
        yield
        total = issued(name + ".total", branch[:half] + ordered(name + ".total", got))
        got = swap_x(total.astype(jnp.bfloat16))
        yield
        got = ordered(name + ".all", got)
        return issued(name + ".all", total + jnp.concatenate([got[piece:], got[:piece]], axis=0))

    chains = {"w": pull_steps()}
    results = {}
    for h in range(HALVES):
        chains["t" + str(h)] = half_steps("t" + str(h), h)
        for i in range(len(spans[h])):
            chains["c" + str(h) + str(i)] = chunk_steps("c" + str(h) + str(i), h, i)
        chains["b" + str(h)] = branch_steps("b" + str(h), h)

    def advance(name):
        try:
            next(chains[name])
        except StopIteration as stop:
            results[name] = stop.value

    def result(name):
        while name not in results:
            advance(name)
        return results[name]

    for name in EDGES:
        while name not in seen:
            advance(name.split(".")[0])
    for h in range(HALVES):
        result("b" + str(h))

    totals = [results["b" + str(h)] for h in range(HALVES)]
    theirs = [flip(total.astype(jnp.bfloat16), "col", 1) for total in totals]
    put = places[0][:, None] == jnp.concatenate(mine)[None]
    moved = jnp.dot(
        put.astype(jnp.float32), jnp.concatenate(totals), precision=lax.Precision.HIGHEST
    )
    put = places[0][:, None] == jnp.concatenate(mine_of(c ^ 1))[None]
    moved = moved + dot(put.astype(jnp.bfloat16), jnp.concatenate(theirs))
    used = (places[0] >= 0)[:, None]
    return jnp.where(used, tokens.astype(jnp.float32) + moved, 0.0).astype(jnp.bfloat16)


def general(tokens, lengths, gate_weight, up_weight, down_weight):
    c = lax.axis_index("col")
    slots = tokens.shape[0]
    whole = lax.all_gather(tokens, "row", axis=1, tiled=True)
    whole = lax.all_gather(whole, "col", axis=0, tiled=True)
    depth = gate_weight.shape[0]
    block = lax.dynamic_slice_in_dim(whole, c * depth, depth, axis=1)

    def summed(a, b):
        return lax.psum_scatter(dot(a, b), "col", scatter_dimension=0, tiled=True)

    hidden = (jax.nn.silu(summed(block, gate_weight)) * summed(block, up_weight)).astype(jnp.bfloat16)
    hidden = lax.all_gather(hidden, "row", axis=1, tiled=True)
    hidden = lax.all_gather(hidden, "col", axis=0, tiled=True)
    depth = down_weight.shape[0]
    branch = summed(lax.dynamic_slice_in_dim(hidden, c * depth, depth, axis=1), down_weight)
    valid = jnp.arange(slots, dtype=jnp.int32) < jnp.take(lengths, c)
    total = tokens.astype(jnp.float32) + branch
    return jnp.where(valid[:, None], total, jnp.float32(0.0)).astype(jnp.bfloat16)


def solution(mesh):
    square = mesh.shape["row"] == 4 and mesh.shape["col"] == 4
    in_specs = (
        P(("groups", "col"), "row"),
        P("groups"),
        P("col", "row"),
        P("col", "row"),
        P("col", "row"),
    )
    out_specs = P(("groups", "col"), "row")
    return jax.shard_map(
        stationary if square else general,
        mesh=mesh, in_specs=in_specs, out_specs=out_specs, check_vma=False,
    )
```

```python
import functools

import jax
import jax.numpy as jnp
from jax import lax
from jax.experimental import pallas as pl
from jax.experimental.pallas import tpu as pltpu
from jax.sharding import PartitionSpec as P

HALVES = 2
PARTS = ((14, 14), (18, 10))
EDGES = {
    "t1.pick": ["t0.add"],
    "w.pull": ["t0.columns"],
    "t0.cores": ["w.pull"],
    "t1.columns": ["t0.cores"],
    "c00.dots": ["t1.columns"],
    "t1.cores": ["c00.dots"],
    "c01.dots": ["c00.sum"],
    "c10.dots": ["c01.sum"],
    "c00.hidden": ["c10.dots"],
    "c10.sum": ["c00.halves"],
    "c01.hidden": ["c10.sum"],
    "c11.dots": ["c01.hidden"],
    "c00.columns": ["c11.dots"],
    "c01.halves": ["c00.columns"],
    "c10.hidden": ["c01.halves"],
    "c11.sum": ["c10.hidden"],
    "c01.columns": ["c11.sum"],
    "c00.cores": ["c01.columns"],
    "c10.halves": ["c00.cores"],
    "c11.hidden": ["c10.halves"],
    "c00.down": ["c11.hidden"],
    "c01.cores": ["c00.down"],
    "c10.columns": ["c01.cores"],
    "c01.down": ["c10.columns"],
    "c11.halves": ["c01.down"],
    "c10.cores": ["b0.total"],
    "c11.columns": ["c10.down"],
    "b0.total": ["c11.halves"],
    "c11.cores": ["b0.all"],
    "c11.down": ["b0.all"],
    "b1.total": ["c11.down"],
}


def dot(a, b):
    return jnp.dot(a, b, preferred_element_type=jnp.float32)


def flip(value, axis, bit):
    count = lax.axis_size(axis)
    return lax.ppermute(value, axis, [(i, i ^ bit) for i in range(count)])


def pull_kernel(first, end, tick_ref, gate_ref, up_ref, gate_here, up_here, sems):
    del tick_ref
    columns = pl.ds(first, end - first)
    copies = [
        pltpu.make_async_copy(source.at[:, columns], here, sems.at[i])
        for i, (source, here) in enumerate(((gate_ref, gate_here), (up_ref, up_here)))
    ]
    for copy in copies:
        copy.start()
    for copy in copies:
        copy.wait()


def pull(gate_weight, up_weight, first, end, tick):
    far = pl.BlockSpec(memory_space=pltpu.HBM)
    near = pl.BlockSpec(memory_space=pltpu.VMEM)
    here = pltpu.VMEM((gate_weight.shape[0], end - first), gate_weight.dtype)
    return pl.pallas_call(
        functools.partial(pull_kernel, first, end),
        in_specs=[pl.BlockSpec(memory_space=pltpu.SMEM), far, far],
        out_specs=[near, near],
        out_shape=[here, here],
        scratch_shapes=[pltpu.SemaphoreType.DMA((2,))],
        compiler_params=pltpu.CompilerParams(
            vmem_limit_bytes=4 * gate_weight.shape[0] * (end - first) + 2**20
        ),
        cost_estimate=pl.CostEstimate(flops=0, bytes_accessed=0, transcendentals=0),
    )(
        tick,
        pltpu.with_memory_space_constraint(gate_weight, pltpu.HBM),
        pltpu.with_memory_space_constraint(up_weight, pltpu.HBM),
    )


def stationary(tokens, lengths, gate_weight, up_weight, down_weight):
    slots, width = tokens.shape
    units = gate_weight.shape[1]
    col_count = lax.axis_size("col")
    c = lax.axis_index("col")
    r = lax.axis_index("row")
    x, k, zh, zl = c // 2, c % 2, r // 2, r % 2
    quarter = slots // 2
    piece = quarter // HALVES
    half = 2 * piece
    spans = []
    for sizes in PARTS:
        ends = [0]
        for size in sizes:
            ends.append(ends[-1] + units * size // sum(sizes))
        spans.append(list(zip(ends[:-1], ends[1:])))

    rows = jnp.arange(lengths.shape[0], dtype=jnp.int32)[None]
    slot = jnp.arange(slots, dtype=jnp.int32)[None]
    here = (c ^ jnp.arange(2, dtype=jnp.int32))[:, None]
    first = jnp.sum(jnp.where(rows < here, lengths[None], 0), axis=1, keepdims=True)
    count = jnp.sum(jnp.where(rows == here, lengths[None], 0), axis=1, keepdims=True)
    places = jnp.where(slot < count, slot + first, -1)
    inside = jnp.arange(piece, dtype=jnp.int32)

    def mine_of(c):
        both = jnp.concatenate([inside + quarter * c, inside + quarter * (c ^ 2)])
        return [both + h * piece for h in range(HALVES)]

    mine = mine_of(c)

    devices = [(i // col_count, i % col_count) for i in range(lax.axis_size("row") * col_count)]

    def move(value, where_to):
        pairs = []
        for i, (row, col) in enumerate(devices):
            to = where_to(row // 2, row % 2, col // 2, col % 2)
            if to is not None:
                to_zh, to_zl, to_x, to_k = to
                pairs.append((i, (to_zh * 2 + to_zl) * col_count + to_x * 2 + to_k))
        return lax.ppermute(value, ("row", "col"), pairs)

    def one_step(value, stay, first_to, second_to):
        first, second = move(value, first_to), move(value, second_to)

        def finish(value):
            return jnp.concatenate(
                [jnp.where(stay, value, first), jnp.where(stay, first, second)], axis=0
            )

        return finish

    def to_cores(value):
        return one_step(
            value,
            zl == k,
            lambda zh, zl, x, k: (zh, 1 - zl, x, k) if k == zl else (zh, zl, x, 1 - k),
            lambda zh, zl, x, k: None if k == zl else (zh, 1 - zl, x, 1 - k),
        )

    sibling = flip(tokens, "col", 1)
    seen = {}

    def ordered(step, value):
        for name in EDGES.get(step, ()):
            while name not in seen:
                advance(name.split(".")[0])
        others = [seen[name] for name in EDGES.get(step, ())]
        return lax.optimization_barrier((value, *others))[0] if others else value

    def issued(step, value):
        seen[step] = value
        return value

    def swap_x(value):
        return flip(value, "col", 2)

    def spread_steps(name, value):
        other = flip(value, "row", 2)
        yield
        other = ordered(name + ".halves", other)
        keep = jnp.where(zh == x, value, other)
        send = issued(name + ".halves", jnp.where(zh == x, other, value))
        got = swap_x(send)
        yield
        got = ordered(name + ".columns", got)
        pair = issued(name + ".columns", jnp.concatenate([keep, got], axis=0))
        finish = to_cores(pair)
        yield
        return issued(name + ".cores", finish(ordered(name + ".cores", pair)))

    def pick_steps(name, h):
        spots = ordered(name + ".pick", mine[h])
        own = spots[:, None] == places[0][None]
        sib = spots[:, None] == places[1][None]
        rows = dot(own.astype(jnp.bfloat16), tokens) + dot(sib.astype(jnp.bfloat16), sibling)
        rows = issued(name + ".pick", rows.astype(jnp.bfloat16))
        got = swap_x(rows[piece:])
        yield
        return issued(name + ".add", ordered(name + ".add", rows[:piece]) + got)

    pulled = []

    def pull_steps():
        tick = ordered("w.pull", lengths)
        pulled.extend(pull(gate_weight, up_weight, *spans[0][0], tick))
        issued("w.pull", pulled[0])
        return None
        yield

    def half_steps(name, h):
        own = yield from pick_steps(name, h)
        return (yield from spread_steps(name, own))

    def chunk_steps(name, h, i):
        full = result("t" + str(h))
        part = slice(*spans[h][i])
        full = ordered(name + ".dots", full)
        if (h, i) == (0, 0):
            result("w")
            gate, up = dot(full, pulled[0]), dot(full, pulled[1])
        else:
            gate, up = dot(full, gate_weight[:, part]), dot(full, up_weight[:, part])
        send = issued(name + ".dots", jnp.stack([gate[half:], up[half:]]).astype(jnp.bfloat16))
        got = issued(name + ".cores_swapped", flip(send, "col", 1))
        yield
        got = ordered(name + ".sum", got)
        gate, up = gate[:half] + got[0], up[:half] + got[1]
        send = issued(name + ".sum", jnp.stack([gate[piece:], up[piece:]]).astype(jnp.bfloat16))
        got = swap_x(send)
        yield
        got = ordered(name + ".hidden", got)
        gate, up = gate[:piece] + got[0], up[:piece] + got[1]
        hidden = issued(name + ".hidden", (jax.nn.silu(gate) * up).astype(jnp.bfloat16))
        whole = yield from spread_steps(name, hidden)
        yield
        whole = ordered(name + ".down", whole)
        return issued(name + ".down", dot(whole, down_weight[part]))

    def branch_steps(name, h):
        parts = [result("c" + str(h) + str(i)) for i in range(len(spans[h]))]
        branch = issued(name + ".branch", sum(parts[1:], parts[0]))
        got = flip(branch[half:].astype(jnp.bfloat16), "col", 1)
        yield
        total = issued(name + ".total", branch[:half] + ordered(name + ".total", got))
        got = swap_x(total.astype(jnp.bfloat16))
        yield
        got = ordered(name + ".all", got)
        return issued(name + ".all", total + jnp.concatenate([got[piece:], got[:piece]], axis=0))

    chains = {"w": pull_steps()}
    results = {}
    for h in range(HALVES):
        chains["t" + str(h)] = half_steps("t" + str(h), h)
        for i in range(len(spans[h])):
            chains["c" + str(h) + str(i)] = chunk_steps("c" + str(h) + str(i), h, i)
        chains["b" + str(h)] = branch_steps("b" + str(h), h)

    def advance(name):
        try:
            next(chains[name])
        except StopIteration as stop:
            results[name] = stop.value

    def result(name):
        while name not in results:
            advance(name)
        return results[name]

    for name in EDGES:
        while name not in seen:
            advance(name.split(".")[0])
    for h in range(HALVES):
        result("b" + str(h))

    totals = [results["b" + str(h)] for h in range(HALVES)]
    theirs = [flip(total.astype(jnp.bfloat16), "col", 1) for total in totals]
    put = places[0][:, None] == jnp.concatenate(mine)[None]
    moved = jnp.dot(
        put.astype(jnp.float32), jnp.concatenate(totals), precision=lax.Precision.HIGHEST
    )
    put = places[0][:, None] == jnp.concatenate(mine_of(c ^ 1))[None]
    moved = moved + dot(put.astype(jnp.bfloat16), jnp.concatenate(theirs))
    used = (places[0] >= 0)[:, None]
    return jnp.where(used, tokens.astype(jnp.float32) + moved, 0.0).astype(jnp.bfloat16)


def general(tokens, lengths, gate_weight, up_weight, down_weight):
    c = lax.axis_index("col")
    slots = tokens.shape[0]
    whole = lax.all_gather(tokens, "row", axis=1, tiled=True)
    whole = lax.all_gather(whole, "col", axis=0, tiled=True)
    depth = gate_weight.shape[0]
    block = lax.dynamic_slice_in_dim(whole, c * depth, depth, axis=1)

    def summed(a, b):
        return lax.psum_scatter(dot(a, b), "col", scatter_dimension=0, tiled=True)

    hidden = (jax.nn.silu(summed(block, gate_weight)) * summed(block, up_weight)).astype(jnp.bfloat16)
    hidden = lax.all_gather(hidden, "row", axis=1, tiled=True)
    hidden = lax.all_gather(hidden, "col", axis=0, tiled=True)
    depth = down_weight.shape[0]
    branch = summed(lax.dynamic_slice_in_dim(hidden, c * depth, depth, axis=1), down_weight)
    valid = jnp.arange(slots, dtype=jnp.int32) < jnp.take(lengths, c)
    total = tokens.astype(jnp.float32) + branch
    return jnp.where(valid[:, None], total, jnp.float32(0.0)).astype(jnp.bfloat16)


def solution(mesh):
    square = mesh.shape["row"] == 4 and mesh.shape["col"] == 4
    in_specs = (
        P(("groups", "col"), "row"),
        P("groups"),
        P("col", "row"),
        P("col", "row"),
        P("col", "row"),
    )
    out_specs = P(("groups", "col"), "row")
    return jax.shard_map(
        stationary if square else general,
        mesh=mesh, in_specs=in_specs, out_specs=out_specs, check_vma=False,
    )
```

```python
import functools

import jax
import jax.numpy as jnp
from jax import lax
from jax.experimental import pallas as pl
from jax.experimental.pallas import tpu as pltpu
from jax.sharding import PartitionSpec as P

HALVES = 2
PARTS = ((13, 15), (18, 10))
EDGES = {
    "t1.pick": ["t0.add"],
    "w.pull": ["t0.columns"],
    "t0.cores": ["w.pull"],
    "t1.columns": ["t0.cores"],
    "c00.dots": ["t1.columns"],
    "t1.cores": ["c00.dots"],
    "c01.dots": ["c00.sum"],
    "c10.dots": ["c01.sum"],
    "c00.hidden": ["c10.dots"],
    "c10.sum": ["c00.halves"],
    "c01.hidden": ["c10.sum"],
    "c11.dots": ["c01.hidden"],
    "c00.columns": ["c11.dots"],
    "c01.halves": ["c00.columns"],
    "c10.hidden": ["c01.halves"],
    "c11.sum": ["c10.hidden"],
    "c01.columns": ["c11.sum"],
    "c00.cores": ["c01.columns"],
    "c10.halves": ["c00.cores"],
    "c11.hidden": ["c10.halves"],
    "c00.down": ["c11.hidden"],
    "c01.cores": ["c00.down"],
    "c10.columns": ["c01.cores"],
    "c01.down": ["c10.columns"],
    "c11.halves": ["c01.down"],
    "c10.cores": ["b0.total"],
    "c11.columns": ["c10.down"],
    "b0.total": ["c11.halves"],
    "c11.cores": ["b0.all"],
    "c11.down": ["b0.all"],
    "b1.total": ["c11.down"],
}


def dot(a, b):
    return jnp.dot(a, b, preferred_element_type=jnp.float32)


def flip(value, axis, bit):
    count = lax.axis_size(axis)
    return lax.ppermute(value, axis, [(i, i ^ bit) for i in range(count)])


def pull_kernel(first, end, tick_ref, gate_ref, up_ref, gate_here, up_here, sems):
    del tick_ref
    columns = pl.ds(first, end - first)
    copies = [
        pltpu.make_async_copy(source.at[:, columns], here, sems.at[i])
        for i, (source, here) in enumerate(((gate_ref, gate_here), (up_ref, up_here)))
    ]
    for copy in copies:
        copy.start()
    for copy in copies:
        copy.wait()


def pull(gate_weight, up_weight, first, end, tick):
    far = pl.BlockSpec(memory_space=pltpu.HBM)
    near = pl.BlockSpec(memory_space=pltpu.VMEM)
    here = pltpu.VMEM((gate_weight.shape[0], end - first), gate_weight.dtype)
    return pl.pallas_call(
        functools.partial(pull_kernel, first, end),
        in_specs=[pl.BlockSpec(memory_space=pltpu.SMEM), far, far],
        out_specs=[near, near],
        out_shape=[here, here],
        scratch_shapes=[pltpu.SemaphoreType.DMA((2,))],
        compiler_params=pltpu.CompilerParams(
            vmem_limit_bytes=4 * gate_weight.shape[0] * (end - first) + 2**20
        ),
        cost_estimate=pl.CostEstimate(flops=0, bytes_accessed=0, transcendentals=0),
    )(
        tick,
        pltpu.with_memory_space_constraint(gate_weight, pltpu.HBM),
        pltpu.with_memory_space_constraint(up_weight, pltpu.HBM),
    )


def stationary(tokens, lengths, gate_weight, up_weight, down_weight):
    slots, width = tokens.shape
    units = gate_weight.shape[1]
    col_count = lax.axis_size("col")
    c = lax.axis_index("col")
    r = lax.axis_index("row")
    x, k, zh, zl = c // 2, c % 2, r // 2, r % 2
    quarter = slots // 2
    piece = quarter // HALVES
    half = 2 * piece
    spans = []
    for sizes in PARTS:
        ends = [0]
        for size in sizes:
            ends.append(ends[-1] + units * size // sum(sizes))
        spans.append(list(zip(ends[:-1], ends[1:])))

    rows = jnp.arange(lengths.shape[0], dtype=jnp.int32)[None]
    slot = jnp.arange(slots, dtype=jnp.int32)[None]
    here = (c ^ jnp.arange(2, dtype=jnp.int32))[:, None]
    first = jnp.sum(jnp.where(rows < here, lengths[None], 0), axis=1, keepdims=True)
    count = jnp.sum(jnp.where(rows == here, lengths[None], 0), axis=1, keepdims=True)
    places = jnp.where(slot < count, slot + first, -1)
    inside = jnp.arange(piece, dtype=jnp.int32)

    def mine_of(c):
        both = jnp.concatenate([inside + quarter * c, inside + quarter * (c ^ 2)])
        return [both + h * piece for h in range(HALVES)]

    mine = mine_of(c)

    devices = [(i // col_count, i % col_count) for i in range(lax.axis_size("row") * col_count)]

    def move(value, where_to):
        pairs = []
        for i, (row, col) in enumerate(devices):
            to = where_to(row // 2, row % 2, col // 2, col % 2)
            if to is not None:
                to_zh, to_zl, to_x, to_k = to
                pairs.append((i, (to_zh * 2 + to_zl) * col_count + to_x * 2 + to_k))
        return lax.ppermute(value, ("row", "col"), pairs)

    def one_step(value, stay, first_to, second_to):
        first, second = move(value, first_to), move(value, second_to)

        def finish(value):
            return jnp.concatenate(
                [jnp.where(stay, value, first), jnp.where(stay, first, second)], axis=0
            )

        return finish

    def to_cores(value):
        return one_step(
            value,
            zl == k,
            lambda zh, zl, x, k: (zh, 1 - zl, x, k) if k == zl else (zh, zl, x, 1 - k),
            lambda zh, zl, x, k: None if k == zl else (zh, 1 - zl, x, 1 - k),
        )

    sibling = flip(tokens, "col", 1)
    seen = {}

    def ordered(step, value):
        for name in EDGES.get(step, ()):
            while name not in seen:
                advance(name.split(".")[0])
        others = [seen[name] for name in EDGES.get(step, ())]
        return lax.optimization_barrier((value, *others))[0] if others else value

    def issued(step, value):
        seen[step] = value
        return value

    def swap_x(value):
        return flip(value, "col", 2)

    def spread_steps(name, value):
        other = flip(value, "row", 2)
        yield
        other = ordered(name + ".halves", other)
        keep = jnp.where(zh == x, value, other)
        send = issued(name + ".halves", jnp.where(zh == x, other, value))
        got = swap_x(send)
        yield
        got = ordered(name + ".columns", got)
        pair = issued(name + ".columns", jnp.concatenate([keep, got], axis=0))
        finish = to_cores(pair)
        yield
        return issued(name + ".cores", finish(ordered(name + ".cores", pair)))

    def pick_steps(name, h):
        spots = ordered(name + ".pick", mine[h])
        own = spots[:, None] == places[0][None]
        sib = spots[:, None] == places[1][None]
        rows = dot(own.astype(jnp.bfloat16), tokens) + dot(sib.astype(jnp.bfloat16), sibling)
        rows = issued(name + ".pick", rows.astype(jnp.bfloat16))
        got = swap_x(rows[piece:])
        yield
        return issued(name + ".add", ordered(name + ".add", rows[:piece]) + got)

    pulled = []

    def pull_steps():
        tick = ordered("w.pull", lengths)
        pulled.extend(pull(gate_weight, up_weight, *spans[0][0], tick))
        issued("w.pull", pulled[0])
        return None
        yield

    def half_steps(name, h):
        own = yield from pick_steps(name, h)
        return (yield from spread_steps(name, own))

    def chunk_steps(name, h, i):
        full = result("t" + str(h))
        part = slice(*spans[h][i])
        full = ordered(name + ".dots", full)
        if (h, i) == (0, 0):
            result("w")
            gate, up = dot(full, pulled[0]), dot(full, pulled[1])
        else:
            gate, up = dot(full, gate_weight[:, part]), dot(full, up_weight[:, part])
        send = issued(name + ".dots", jnp.stack([gate[half:], up[half:]]).astype(jnp.bfloat16))
        got = issued(name + ".cores_swapped", flip(send, "col", 1))
        yield
        got = ordered(name + ".sum", got)
        gate, up = gate[:half] + got[0], up[:half] + got[1]
        send = issued(name + ".sum", jnp.stack([gate[piece:], up[piece:]]).astype(jnp.bfloat16))
        got = swap_x(send)
        yield
        got = ordered(name + ".hidden", got)
        gate, up = gate[:piece] + got[0], up[:piece] + got[1]
        hidden = issued(name + ".hidden", (jax.nn.silu(gate) * up).astype(jnp.bfloat16))
        whole = yield from spread_steps(name, hidden)
        yield
        whole = ordered(name + ".down", whole)
        return issued(name + ".down", dot(whole, down_weight[part]))

    def branch_steps(name, h):
        parts = [result("c" + str(h) + str(i)) for i in range(len(spans[h]))]
        branch = issued(name + ".branch", sum(parts[1:], parts[0]))
        got = flip(branch[half:].astype(jnp.bfloat16), "col", 1)
        yield
        total = issued(name + ".total", branch[:half] + ordered(name + ".total", got))
        got = swap_x(total.astype(jnp.bfloat16))
        yield
        got = ordered(name + ".all", got)
        return issued(name + ".all", total + jnp.concatenate([got[piece:], got[:piece]], axis=0))

    chains = {"w": pull_steps()}
    results = {}
    for h in range(HALVES):
        chains["t" + str(h)] = half_steps("t" + str(h), h)
        for i in range(len(spans[h])):
            chains["c" + str(h) + str(i)] = chunk_steps("c" + str(h) + str(i), h, i)
        chains["b" + str(h)] = branch_steps("b" + str(h), h)

    def advance(name):
        try:
            next(chains[name])
        except StopIteration as stop:
            results[name] = stop.value

    def result(name):
        while name not in results:
            advance(name)
        return results[name]

    for name in EDGES:
        while name not in seen:
            advance(name.split(".")[0])
    for h in range(HALVES):
        result("b" + str(h))

    totals = [results["b" + str(h)] for h in range(HALVES)]
    theirs = [flip(total.astype(jnp.bfloat16), "col", 1) for total in totals]
    put = places[0][:, None] == jnp.concatenate(mine)[None]
    moved = jnp.dot(
        put.astype(jnp.float32), jnp.concatenate(totals), precision=lax.Precision.HIGHEST
    )
    put = places[0][:, None] == jnp.concatenate(mine_of(c ^ 1))[None]
    moved = moved + dot(put.astype(jnp.bfloat16), jnp.concatenate(theirs))
    used = (places[0] >= 0)[:, None]
    return jnp.where(used, tokens.astype(jnp.float32) + moved, 0.0).astype(jnp.bfloat16)


def general(tokens, lengths, gate_weight, up_weight, down_weight):
    c = lax.axis_index("col")
    slots = tokens.shape[0]
    whole = lax.all_gather(tokens, "row", axis=1, tiled=True)
    whole = lax.all_gather(whole, "col", axis=0, tiled=True)
    depth = gate_weight.shape[0]
    block = lax.dynamic_slice_in_dim(whole, c * depth, depth, axis=1)

    def summed(a, b):
        return lax.psum_scatter(dot(a, b), "col", scatter_dimension=0, tiled=True)

    hidden = (jax.nn.silu(summed(block, gate_weight)) * summed(block, up_weight)).astype(jnp.bfloat16)
    hidden = lax.all_gather(hidden, "row", axis=1, tiled=True)
    hidden = lax.all_gather(hidden, "col", axis=0, tiled=True)
    depth = down_weight.shape[0]
    branch = summed(lax.dynamic_slice_in_dim(hidden, c * depth, depth, axis=1), down_weight)
    valid = jnp.arange(slots, dtype=jnp.int32) < jnp.take(lengths, c)
    total = tokens.astype(jnp.float32) + branch
    return jnp.where(valid[:, None], total, jnp.float32(0.0)).astype(jnp.bfloat16)


def solution(mesh):
    square = mesh.shape["row"] == 4 and mesh.shape["col"] == 4
    in_specs = (
        P(("groups", "col"), "row"),
        P("groups"),
        P("col", "row"),
        P("col", "row"),
        P("col", "row"),
    )
    out_specs = P(("groups", "col"), "row")
    return jax.shard_map(
        stationary if square else general,
        mesh=mesh, in_specs=in_specs, out_specs=out_specs, check_vma=False,
    )
```

```python
import functools

import jax
import jax.numpy as jnp
from jax import lax
from jax.experimental import pallas as pl
from jax.experimental.pallas import tpu as pltpu
from jax.sharding import PartitionSpec as P

HALVES = 2
PARTS = ((13, 15), (18, 10))
EDGES = {
    "t1.pick": ["t0.add"],
    "w.pull": ["t0.columns"],
    "t0.cores": ["w.pull"],
    "t1.columns": ["t0.cores"],
    "c00.dots": ["t1.columns"],
    "c01.dots": ["c00.sum"],
    "c10.dots": ["c01.sum"],
    "c00.hidden": ["c10.dots"],
    "c10.sum": ["c00.halves"],
    "c01.hidden": ["c10.sum"],
    "c11.dots": ["c01.hidden"],
    "c00.columns": ["c11.dots"],
    "c01.halves": ["c00.columns"],
    "c10.hidden": ["c01.halves"],
    "c11.sum": ["c10.hidden"],
    "c01.columns": ["c11.sum"],
    "c00.cores": ["c01.columns"],
    "c10.halves": ["c00.cores"],
    "c11.hidden": ["c10.halves"],
    "c00.down": ["c11.hidden"],
    "c01.cores": ["c00.down"],
    "c10.columns": ["c01.cores"],
    "c01.down": ["c10.columns"],
    "c11.halves": ["c01.down"],
    "b0.total": ["c11.halves"],
    "c11.columns": ["c10.down"],
    "c11.cores": ["b0.all"],
    "b1.total": ["c11.down"],
}


def dot(a, b):
    return jnp.dot(a, b, preferred_element_type=jnp.float32)


def flip(value, axis, bit):
    count = lax.axis_size(axis)
    return lax.ppermute(value, axis, [(i, i ^ bit) for i in range(count)])


def pull_kernel(first, end, tick_ref, gate_ref, up_ref, gate_here, up_here, sems):
    del tick_ref
    columns = pl.ds(first, end - first)
    copies = [
        pltpu.make_async_copy(source.at[:, columns], here, sems.at[i])
        for i, (source, here) in enumerate(((gate_ref, gate_here), (up_ref, up_here)))
    ]
    for copy in copies:
        copy.start()
    for copy in copies:
        copy.wait()


def pull(gate_weight, up_weight, first, end, tick):
    far = pl.BlockSpec(memory_space=pltpu.HBM)
    near = pl.BlockSpec(memory_space=pltpu.VMEM)
    here = pltpu.VMEM((gate_weight.shape[0], end - first), gate_weight.dtype)
    return pl.pallas_call(
        functools.partial(pull_kernel, first, end),
        in_specs=[pl.BlockSpec(memory_space=pltpu.SMEM), far, far],
        out_specs=[near, near],
        out_shape=[here, here],
        scratch_shapes=[pltpu.SemaphoreType.DMA((2,))],
        compiler_params=pltpu.CompilerParams(
            vmem_limit_bytes=4 * gate_weight.shape[0] * (end - first) + 2**20
        ),
        cost_estimate=pl.CostEstimate(flops=0, bytes_accessed=0, transcendentals=0),
    )(
        tick,
        pltpu.with_memory_space_constraint(gate_weight, pltpu.HBM),
        pltpu.with_memory_space_constraint(up_weight, pltpu.HBM),
    )


def stationary(tokens, lengths, gate_weight, up_weight, down_weight):
    slots, width = tokens.shape
    units = gate_weight.shape[1]
    col_count = lax.axis_size("col")
    c = lax.axis_index("col")
    r = lax.axis_index("row")
    x, k, zh, zl = c // 2, c % 2, r // 2, r % 2
    quarter = slots // 2
    piece = quarter // HALVES
    half = 2 * piece
    spans = []
    for sizes in PARTS:
        ends = [0]
        for size in sizes:
            ends.append(ends[-1] + units * size // sum(sizes))
        spans.append(list(zip(ends[:-1], ends[1:])))

    rows = jnp.arange(lengths.shape[0], dtype=jnp.int32)[None]
    slot = jnp.arange(slots, dtype=jnp.int32)[None]
    here = (c ^ jnp.arange(2, dtype=jnp.int32))[:, None]
    first = jnp.sum(jnp.where(rows < here, lengths[None], 0), axis=1, keepdims=True)
    count = jnp.sum(jnp.where(rows == here, lengths[None], 0), axis=1, keepdims=True)
    places = jnp.where(slot < count, slot + first, -1)
    inside = jnp.arange(piece, dtype=jnp.int32)

    def mine_of(c):
        both = jnp.concatenate([inside + quarter * c, inside + quarter * (c ^ 2)])
        return [both + h * piece for h in range(HALVES)]

    mine = mine_of(c)

    devices = [(i // col_count, i % col_count) for i in range(lax.axis_size("row") * col_count)]

    def move(value, where_to):
        pairs = []
        for i, (row, col) in enumerate(devices):
            to = where_to(row // 2, row % 2, col // 2, col % 2)
            if to is not None:
                to_zh, to_zl, to_x, to_k = to
                pairs.append((i, (to_zh * 2 + to_zl) * col_count + to_x * 2 + to_k))
        return lax.ppermute(value, ("row", "col"), pairs)

    def one_step(value, stay, first_to, second_to):
        first, second = move(value, first_to), move(value, second_to)

        def finish(value):
            return jnp.concatenate(
                [jnp.where(stay, value, first), jnp.where(stay, first, second)], axis=0
            )

        return finish

    def to_cores(value):
        return one_step(
            value,
            zl == k,
            lambda zh, zl, x, k: (zh, 1 - zl, x, k) if k == zl else (zh, zl, x, 1 - k),
            lambda zh, zl, x, k: None if k == zl else (zh, 1 - zl, x, 1 - k),
        )

    sibling = flip(tokens, "col", 1)
    seen = {}

    def ordered(step, value):
        for name in EDGES.get(step, ()):
            while name not in seen:
                advance(name.split(".")[0])
        others = [seen[name] for name in EDGES.get(step, ())]
        return lax.optimization_barrier((value, *others))[0] if others else value

    def issued(step, value):
        seen[step] = value
        return value

    def swap_x(value):
        return flip(value, "col", 2)

    def spread_steps(name, value):
        other = flip(value, "row", 2)
        yield
        other = ordered(name + ".halves", other)
        keep = jnp.where(zh == x, value, other)
        send = issued(name + ".halves", jnp.where(zh == x, other, value))
        got = swap_x(send)
        yield
        got = ordered(name + ".columns", got)
        pair = issued(name + ".columns", jnp.concatenate([keep, got], axis=0))
        finish = to_cores(pair)
        yield
        return issued(name + ".cores", finish(ordered(name + ".cores", pair)))

    def pick_steps(name, h):
        spots = ordered(name + ".pick", mine[h])
        own = spots[:, None] == places[0][None]
        sib = spots[:, None] == places[1][None]
        rows = dot(own.astype(jnp.bfloat16), tokens) + dot(sib.astype(jnp.bfloat16), sibling)
        rows = issued(name + ".pick", rows.astype(jnp.bfloat16))
        got = swap_x(rows[piece:])
        yield
        return issued(name + ".add", ordered(name + ".add", rows[:piece]) + got)

    pulled = []

    def pull_steps():
        tick = ordered("w.pull", lengths)
        pulled.extend(pull(gate_weight, up_weight, *spans[0][0], tick))
        issued("w.pull", pulled[0])
        return None
        yield

    def half_steps(name, h):
        own = yield from pick_steps(name, h)
        return (yield from spread_steps(name, own))

    def chunk_steps(name, h, i):
        full = result("t" + str(h))
        part = slice(*spans[h][i])
        full = ordered(name + ".dots", full)
        if (h, i) == (0, 0):
            result("w")
            gate, up = dot(full, pulled[0]), dot(full, pulled[1])
        else:
            gate, up = dot(full, gate_weight[:, part]), dot(full, up_weight[:, part])
        send = issued(name + ".dots", jnp.stack([gate[half:], up[half:]]).astype(jnp.bfloat16))
        got = issued(name + ".cores_swapped", flip(send, "col", 1))
        yield
        got = ordered(name + ".sum", got)
        gate, up = gate[:half] + got[0], up[:half] + got[1]
        send = issued(name + ".sum", jnp.stack([gate[piece:], up[piece:]]).astype(jnp.bfloat16))
        got = swap_x(send)
        yield
        got = ordered(name + ".hidden", got)
        gate, up = gate[:piece] + got[0], up[:piece] + got[1]
        hidden = issued(name + ".hidden", (jax.nn.silu(gate) * up).astype(jnp.bfloat16))
        whole = yield from spread_steps(name, hidden)
        yield
        whole = ordered(name + ".down", whole)
        return issued(name + ".down", dot(whole, down_weight[part]))

    def branch_steps(name, h):
        parts = [result("c" + str(h) + str(i)) for i in range(len(spans[h]))]
        branch = issued(name + ".branch", sum(parts[1:], parts[0]))
        got = flip(branch[half:].astype(jnp.bfloat16), "col", 1)
        yield
        total = issued(name + ".total", branch[:half] + ordered(name + ".total", got))
        got = swap_x(total.astype(jnp.bfloat16))
        yield
        got = ordered(name + ".all", got)
        return issued(name + ".all", total + jnp.concatenate([got[piece:], got[:piece]], axis=0))

    chains = {"w": pull_steps()}
    results = {}
    for h in range(HALVES):
        chains["t" + str(h)] = half_steps("t" + str(h), h)
        for i in range(len(spans[h])):
            chains["c" + str(h) + str(i)] = chunk_steps("c" + str(h) + str(i), h, i)
        chains["b" + str(h)] = branch_steps("b" + str(h), h)

    def advance(name):
        try:
            next(chains[name])
        except StopIteration as stop:
            results[name] = stop.value

    def result(name):
        while name not in results:
            advance(name)
        return results[name]

    for name in EDGES:
        while name not in seen:
            advance(name.split(".")[0])
    for h in range(HALVES):
        result("b" + str(h))

    totals = [results["b" + str(h)] for h in range(HALVES)]
    theirs = [flip(total.astype(jnp.bfloat16), "col", 1) for total in totals]
    put = places[0][:, None] == jnp.concatenate(mine)[None]
    moved = jnp.dot(
        put.astype(jnp.float32), jnp.concatenate(totals), precision=lax.Precision.HIGHEST
    )
    put = places[0][:, None] == jnp.concatenate(mine_of(c ^ 1))[None]
    moved = moved + dot(put.astype(jnp.bfloat16), jnp.concatenate(theirs))
    used = (places[0] >= 0)[:, None]
    return jnp.where(used, tokens.astype(jnp.float32) + moved, 0.0).astype(jnp.bfloat16)


def general(tokens, lengths, gate_weight, up_weight, down_weight):
    c = lax.axis_index("col")
    slots = tokens.shape[0]
    whole = lax.all_gather(tokens, "row", axis=1, tiled=True)
    whole = lax.all_gather(whole, "col", axis=0, tiled=True)
    depth = gate_weight.shape[0]
    block = lax.dynamic_slice_in_dim(whole, c * depth, depth, axis=1)

    def summed(a, b):
        return lax.psum_scatter(dot(a, b), "col", scatter_dimension=0, tiled=True)

    hidden = (jax.nn.silu(summed(block, gate_weight)) * summed(block, up_weight)).astype(jnp.bfloat16)
    hidden = lax.all_gather(hidden, "row", axis=1, tiled=True)
    hidden = lax.all_gather(hidden, "col", axis=0, tiled=True)
    depth = down_weight.shape[0]
    branch = summed(lax.dynamic_slice_in_dim(hidden, c * depth, depth, axis=1), down_weight)
    valid = jnp.arange(slots, dtype=jnp.int32) < jnp.take(lengths, c)
    total = tokens.astype(jnp.float32) + branch
    return jnp.where(valid[:, None], total, jnp.float32(0.0)).astype(jnp.bfloat16)


def solution(mesh):
    square = mesh.shape["row"] == 4 and mesh.shape["col"] == 4
    in_specs = (
        P(("groups", "col"), "row"),
        P("groups"),
        P("col", "row"),
        P("col", "row"),
        P("col", "row"),
    )
    out_specs = P(("groups", "col"), "row")
    return jax.shard_map(
        stationary if square else general,
        mesh=mesh, in_specs=in_specs, out_specs=out_specs, check_vma=False,
    )
```
